32 devices in a mesh: rows: 4 (over y, x), blk: 4 (over z), rep: 2 (over core).
Axes of the slice: x: 2, y: 2, z: 4, core: 2. Of those that a mesh axis runs over, the one named last changes fastest.
Arguments:
- pair_left: bfloat16 [512, 64, 128], P(('rep', 'rows'), 'blk'), parts along dimension 0, may hold values from -6 to 6
- pair_right: bfloat16 [256, 64, 128], P(('rep', 'blk'), 'rows'), parts along dimension 0, may hold values from -6 to 6
- pair_middle: bfloat16 [512, 128, 128], P(('rep', 'rows'), 'blk'), parts along dimension 0, may hold values from -6 to 6
- cotangent: bfloat16 [512, 128, 128], P(('rep', 'rows'), 'blk'), parts along dimension 0, may hold values from -6 to 6
- left_weight: bfloat16 [128, 256], replicated, may hold values from -0.5 to 0.5
- right_weight: bfloat16 [128, 256], replicated, may hold values from -0.5 to 0.5
- gate_weight: bfloat16 [128, 128], replicated, may hold values from -0.5 to 0.5
- output_weight: bfloat16 [128, 128], replicated, may hold values from -0.5 to 0.5
Outputs:
- update: bfloat16 [512, 128, 128], P(('rep', 'rows'), 'blk'), parts along dimension 0
- grad_left: bfloat16 [512, 64, 128], P(('rep', 'rows'), 'blk'), parts along dimension 0
- grad_right: bfloat16 [256, 64, 128], P(('rep', 'blk'), 'rows'), parts along dimension 0
- grad_middle: bfloat16 [512, 128, 128], P(('rep', 'rows'), 'blk'), parts along dimension 0
- left_delta: float32 [256, 256], P('rep'), parts along dimension 0
- right_delta: float32 [256, 256], P('rep'), parts along dimension 0
- gate_delta: float32 [256, 128], P('rep'), parts along dimension 0
- output_delta: float32 [256, 128], P('rep'), parts along dimension 0
The draws below stay inside these ranges and needn't reach their ends.
There are 2 independent parts, one for each index of `rep`. The reference program is written for one: setup_inputs(seed, part) draws one part's arguments, and reference() takes and returns one part's arrays. A program takes and returns all parts, laid end to end along the dimension named above; an argument that names none is the same for every part. Nothing has to cross between parts.
All inputs are finite; a program needn't handle non-finite values.
Results may differ from the reference program's by a relative error of at most 0.025.
Values may be sent and summed in bfloat16 or wider, within the bound.
No kernel may reach another device: no remote copies, remote signals or barrier semaphores. Data moves between devices by JAX's collectives and lax.ppermute only.
A program may use at most 64 MiB of HBM per device.

```python
import jax
import jax.numpy as jnp
from jax import lax

C = 128
CH = 128
ID = 64
JD = 32
I = 256
J = 128
K = 64
N_ROWS = 4
N_BLK = 4


def levels(rng, extent, cuts, low, top_value):
    def one(axis_at, blocks):
        draws = jax.random.uniform(jax.random.fold_in(jax.random.fold_in(rng, 6), axis_at), (blocks,), jnp.float32, low / len(cuts), top_value / len(cuts))
        return jnp.repeat(jnp.exp(draws), extent[axis_at] // blocks).reshape((-1,) + (1,) * (len(extent) - axis_at - 1))

    level = one(*cuts[0])
    for cut in cuts[1:]:
        level = level * one(*cut)
    return level


def normal_values(key, extent, spread, limit, pieces=(), kind=jnp.bfloat16):
    values = spread * jax.random.normal(key, extent, jnp.float32)
    if pieces:
        values = values * levels(key, extent, pieces, -0.22, 0.18)
    return jnp.clip(values, -limit, limit).astype(kind)


def setup_inputs(seed: int = 0, part: int = 0) -> dict:
    keys = jax.random.split(jax.random.key(seed), 9)
    part_keys = jax.random.split(jax.random.fold_in(keys[8], part), 9)
    pair_left = normal_values(part_keys[0], (I, K, C), 1.0, 6.0, ((0, 4), (1, 4)))
    pair_right = normal_values(part_keys[1], (J, K, C), 1.0, 6.0, ((0, 4), (1, 4)))
    pair_middle = normal_values(part_keys[2], (I, J, C), 1.0, 6.0, ((0, 4), (1, 4)))
    cotangent = normal_values(part_keys[3], (I, J, C), 1.0, 6.0, ((0, 4), (1, 4)))
    left_weight = normal_values(keys[4], (C, 2 * CH), C ** -0.5, 0.5)
    right_weight = normal_values(keys[5], (C, 2 * CH), C ** -0.5, 0.5)
    gate_weight = normal_values(keys[6], (C, C), C ** -0.5, 0.5)
    output_weight = normal_values(keys[7], (CH, C), CH ** -0.5, 0.5)
    return {"pair_left": pair_left, "pair_right": pair_right, "pair_middle": pair_middle, "cotangent": cotangent, "left_weight": left_weight, "right_weight": right_weight, "gate_weight": gate_weight, "output_weight": output_weight}


epsilon = 1e-05

def normalize(field):
    values = field.astype(jnp.float32)
    centred = values - lax.optimization_barrier(jnp.mean(values, axis=-1, keepdims=True))
    inverse = lax.rsqrt(lax.optimization_barrier(jnp.mean(centred * centred, axis=-1, keepdims=True)) + epsilon)
    return (centred * inverse, inverse)

def normalize_back(normed, inverse, upstream):
    first = lax.optimization_barrier(jnp.mean(upstream, axis=-1, keepdims=True))
    second = lax.optimization_barrier(jnp.mean(upstream * normed, axis=-1, keepdims=True))
    return inverse * (upstream - first - normed * second)

def flat_dot(inputs, weight):
    flat = inputs.reshape(-1, inputs.shape[-1])
    result = jnp.dot(flat, weight, preferred_element_type=jnp.float32)
    return result.reshape(inputs.shape[:-1] + (weight.shape[1],))

def outer_sum(inputs, grads):
    flat_in = inputs.reshape(-1, inputs.shape[-1])
    flat_back = grads.reshape(-1, grads.shape[-1])
    return jnp.dot(flat_in.T, flat_back, preferred_element_type=jnp.float32)

def gated_project(inputs, weight):
    width = weight.shape[1] // 2
    mixed_cols = flat_dot(inputs, weight)
    linear = mixed_cols[..., :width]
    switch = jax.nn.sigmoid(mixed_cols[..., width:])
    return (switch * linear, switch, linear)

def gated_back(inputs, switch, linear, upstream, weight):
    back_linear = upstream * switch
    back_gate = upstream * linear * switch * (1.0 - switch)
    joined = jnp.concatenate([back_linear, back_gate], axis=-1).astype(jnp.bfloat16)
    return (outer_sum(inputs, joined), flat_dot(joined, weight.T))

def reference(pair_left, pair_right, pair_middle, cotangent, left_weight, right_weight, gate_weight, output_weight):
    left_norm, left_inverse = normalize(pair_left)
    left_input = left_norm.astype(jnp.bfloat16)
    left_act, left_switch, left_linear = gated_project(left_input, left_weight)
    left_slab = left_act.astype(jnp.bfloat16)
    right_norm, right_inverse = normalize(pair_right)
    right_input = right_norm.astype(jnp.bfloat16)
    right_act, right_switch, right_linear = gated_project(right_input, right_weight)
    right_slab = right_act.astype(jnp.bfloat16)
    triangle = jnp.einsum('ikc,jkc->ijc', left_slab.astype(jnp.float32), right_slab.astype(jnp.float32))
    tri_norm, tri_inverse = normalize(triangle)
    tri_input = tri_norm.astype(jnp.bfloat16)
    middle_norm, middle_inverse = normalize(pair_middle)
    middle_input = middle_norm.astype(jnp.bfloat16)
    gate = jax.nn.sigmoid(flat_dot(middle_input, gate_weight))
    head = flat_dot(tri_input, output_weight)
    update = (gate * head).astype(jnp.bfloat16)
    upstream = cotangent.astype(jnp.float32)
    head_back = (upstream * gate).astype(jnp.bfloat16)
    pre_back = (upstream * head * gate * (1.0 - gate)).astype(jnp.bfloat16)
    output_delta = outer_sum(tri_input, head_back)
    gate_delta = outer_sum(middle_input, pre_back)
    grad_middle = normalize_back(middle_norm, middle_inverse, flat_dot(pre_back, gate_weight.T)).astype(jnp.bfloat16)
    tri_back = normalize_back(tri_norm, tri_inverse, flat_dot(head_back, output_weight.T)).astype(jnp.bfloat16)

    def left_group(group, total):
        start = jnp.asarray(group, jnp.int32) * JD
        rows_back = lax.dynamic_slice_in_dim(tri_back, start, JD, 1).astype(jnp.float32)
        partner = lax.dynamic_slice_in_dim(right_slab, start, JD, 0).astype(jnp.float32)
        term = jnp.einsum('ijc,jkc->ikc', rows_back, partner)
        rounded = lax.optimization_barrier(term.astype(jnp.bfloat16))
        return total + rounded.astype(jnp.float32)
    left_back = lax.fori_loop(0, N_BLK, left_group, jnp.zeros((I, K, CH), jnp.float32))

    def right_group(group, total):
        start = jnp.asarray(group, jnp.int32) * ID
        rows_back = lax.dynamic_slice_in_dim(tri_back, start, ID, 0).astype(jnp.float32)
        partner = lax.dynamic_slice_in_dim(left_slab, start, ID, 0).astype(jnp.float32)
        term = jnp.einsum('ijc,ikc->jkc', rows_back, partner)
        rounded = lax.optimization_barrier(term.astype(jnp.bfloat16))
        return total + rounded.astype(jnp.float32)
    right_back = lax.fori_loop(0, N_ROWS, right_group, jnp.zeros((J, K, CH), jnp.float32))
    left_delta, left_up = gated_back(left_input, left_switch, left_linear, left_back, left_weight)
    right_delta, right_up = gated_back(right_input, right_switch, right_linear, right_back, right_weight)
    grad_left = normalize_back(left_norm, left_inverse, left_up).astype(jnp.bfloat16)
    grad_right = normalize_back(right_norm, right_inverse, right_up).astype(jnp.bfloat16)
    return (update, grad_left, grad_right, grad_middle, left_delta, right_delta, gate_delta, output_delta)
```

```python
import functools
import math

import jax
import jax.numpy as jnp
from jax import lax
from jax.experimental import pallas as pl
from jax.experimental.pallas import tpu as pltpu
from jax.sharding import PartitionSpec as P

epsilon = 1e-05
f32 = jnp.float32
bf16 = jnp.bfloat16
SCOPED = 6 * 1024 * 1024


def normalize(values):
    centred = values - jnp.mean(values, axis=-1, keepdims=True)
    inverse = lax.rsqrt(jnp.mean(centred * centred, axis=-1, keepdims=True) + epsilon)
    return (centred * inverse, inverse)


def normalize_back(normed, inverse, upstream):
    first = jnp.mean(upstream, axis=-1, keepdims=True)
    second = jnp.mean(upstream * normed, axis=-1, keepdims=True)
    return inverse * (upstream - first - normed * second)


def sigmoid(x):
    return 0.5 * jnp.tanh(0.5 * x) + 0.5


def dot(a, b):
    return lax.dot_general(a, b, (((1,), (0,)), ((), ())), preferred_element_type=f32)


def dot_nt(a, b):
    return lax.dot_general(a, b, (((1,), (1,)), ((), ())), preferred_element_type=f32)


def dot_tn(a, b):
    return lax.dot_general(a, b, (((0,), (0,)), ((), ())), preferred_element_type=f32)


def gated(inputs, weight):
    pre = dot(inputs, weight)
    width = weight.shape[1] // 2
    return pre[:, :width], sigmoid(pre[:, width:])


def joined_grad(back, lin, sw):
    return jnp.concatenate([back * sw, back * lin * sw * (1.0 - sw)], axis=-1).astype(bf16)


def middle_kernel(middle, cotangent, gate_weight, output_weight, gate, middle_in, head_back, tri_up):
    n_i, n_j, width = middle.shape
    step = 8

    def body(at, _):
        rows = pl.ds(at * step, step)
        normed, _ = normalize(middle[rows].astype(f32).reshape(step * n_j, width))
        inputs = normed.astype(bf16)
        opened = sigmoid(dot(inputs, gate_weight[...]))
        back = (cotangent[rows].astype(f32).reshape(step * n_j, width) * opened).astype(bf16)
        gate[rows] = opened.reshape(step, n_j, width)
        middle_in[rows] = inputs.reshape(step, n_j, width)
        head_back[rows] = back.reshape(step, n_j, width)
        tri_up[rows] = dot_nt(back, output_weight[...]).reshape(step, n_j, width)
        return 0

    lax.fori_loop(0, n_i // step, body, 0, unroll=2)


def right_kernel(n_rows, n_blk, k_left, ids, *refs):
    raw, (weight, act_out, in_out, *flip_out) = refs[:n_rows], refs[n_rows:]
    n_j, k_right, width = raw[0].shape
    n_k = k_left * n_blk
    unit = math.gcd(k_left, k_right)
    step = 16
    for s in range(n_rows):

        def body(at, _, s=s):
            rows = pl.ds(at * step, step)
            normed, _ = normalize(raw[s][rows].astype(f32).reshape(step * k_right, width))
            inputs = normed.astype(bf16)
            in_out[s, rows] = inputs.reshape(step, k_right, width)
            lin, sw = gated(inputs, weight[...])
            act = (sw * lin).astype(bf16).astype(f32).reshape(step, k_right, width)
            for part in range(k_right // unit):
                at_k = place(ids, n_rows, n_blk, k_left, k_right, s, part)
                for j in range(step):
                    start = pl.multiple_of((at * step + j) * n_k + at_k, unit)
                    act_out[pl.ds(start, unit), :] = act[j, part * unit : (part + 1) * unit]
            return 0

        lax.fori_loop(0, n_j // step, body, 0)

    for s in range(n_blk):

        def flip(k, _, s=s):
            flip_out[s][k] = act_out[pl.ds(s * k_left + k, n_j, stride=n_k), :]
            return 0

        lax.fori_loop(0, k_left, flip, 0, unroll=True)


def place(ids, n_rows, n_blk, k_left, k_right, piece, part):
    unit = math.gcd(k_left, k_right)
    vertex = lax.rem(ids[0] - piece + n_rows, n_rows) * k_right + part * unit
    block = vertex // k_left
    at = lax.rem(ids[1] - block + n_blk, n_blk) * k_left + vertex - block * k_left
    return pl.multiple_of(at, unit)


def project_left(raw, weight, act_out, in_out):
    n_i, k_left, width = raw.shape
    step = 8

    def body(at, _):
        rows = pl.ds(at * step, step)
        normed, _ = normalize(raw[rows].astype(f32).reshape(step * k_left, width))
        inputs = normed.astype(bf16)
        in_out[rows] = inputs.reshape(step, k_left, width)
        lin, sw = gated(inputs, weight[...])
        act_out[rows] = (sw * lin).astype(bf16).astype(f32).reshape(step, k_left, width)
        return 0

    lax.fori_loop(0, n_i // step, body, 0, unroll=2)


def add_vertices(total, rows, act, flip):
    for k in range(act.shape[1]):
        total = total + act[rows, k : k + 1, :] * flip[k][None]
    return total


def left_kernel(first, raw, weight, flip, *refs):
    total_in, (act_out, in_out, total_out) = refs[: 0 if first else 1], refs[0 if first else 1 :]
    n_i, n_j, width = total_out.shape
    step = 8
    project_left(raw, weight, act_out, in_out)

    def body(at, _):
        rows = pl.ds(at * step, step)
        total = jnp.zeros((step, n_j, width), f32) if first else total_in[0][rows]
        total_out[rows] = add_vertices(total, rows, act_out, flip)
        return 0

    lax.fori_loop(0, n_i // step, body, 0)


def triangle_kernel(
    has_total, raw, left_w, flip, out_w, gate, middle_in, head_back, tri_up, cotangent, *refs
):
    total_in, refs = refs[: 1 if has_total else 0], refs[1 if has_total else 0 :]
    act_out, in_out, update, pre_back, tri_back, gate_part, output_part = refs
    n_i, n_j, width = update.shape
    step = 8
    project_left(raw, left_w, act_out, in_out)
    gate_part[...] = jnp.zeros_like(gate_part)
    output_part[...] = jnp.zeros_like(output_part)

    def triangle_rows(at, _):
        rows = pl.ds(at * step, step)
        total = total_in[0][rows] if has_total else jnp.zeros((step, n_j, width), f32)
        total = add_vertices(total, rows, act_out, flip)
        flat = step * n_j
        normed, inverse = normalize(total.reshape(flat, width))
        tri_in = normed.astype(bf16)
        head = dot(tri_in, out_w[...])
        opened = gate[rows].reshape(flat, width)
        update[rows] = (opened * head).astype(bf16).reshape(step, n_j, width)
        upstream = cotangent[rows].astype(f32).reshape(flat, width)
        pre = (upstream * head * opened * (1.0 - opened)).astype(bf16)
        pre_back[rows] = pre.reshape(step, n_j, width)
        gate_part[...] += dot_tn(middle_in[rows].reshape(flat, width), pre)
        output_part[...] += dot_tn(tri_in, head_back[rows].reshape(flat, width))
        back = normalize_back(normed, inverse, tri_up[rows].reshape(flat, width))
        tri_back[rows] = back.astype(bf16).astype(f32).reshape(step, n_j, width)
        return 0

    lax.fori_loop(0, n_i // step, triangle_rows, 0, unroll=2)


def vertex_step(n_k, unit):
    size = unit
    while size * 2 <= 64 and n_k % (size * 2) == 0:
        size *= 2
    return size


def left_back_kernel(tri_back, right_act, *left_out):
    n_i, n_j, width = tri_back.shape
    k_left = left_out[0].shape[1]
    n_k = k_left * len(left_out)
    few = 4
    k_step = vertex_step(n_k, k_left)
    for k0 in range(0, n_k, k_step):

        def rows_sum(at, _, k0=k0):
            rows = pl.ds(at * few, few)
            total = jnp.zeros((few, k_step, width), f32)
            for j in range(n_j):
                start = j * n_k + k0
                total = total + tri_back[rows, j : j + 1, :] * right_act[start : start + k_step, :][None]
            total = total.astype(bf16)
            for s in range(k0 // k_left, (k0 + k_step) // k_left):
                left_out[s][rows] = total[:, s * k_left - k0 : (s + 1) * k_left - k0]
            return 0

        lax.fori_loop(0, n_i // few, rows_sum, 0)


def right_back_kernel(n_rows, n_blk, ids, tri_back, *refs):
    left_act, refs = refs[:n_blk], refs[n_blk + 1 :]
    right_out, (right_sum,) = refs[:n_rows], refs[n_rows:]
    n_i, n_j, width = tri_back.shape
    k_left = left_act[0].shape[1]
    n_k = k_left * n_blk
    k_right = right_out[0].shape[1]
    unit = math.gcd(k_left, k_right)
    few = 4
    k_step = vertex_step(n_k, k_left)
    for k0 in range(0, n_k, k_step):
        blocks = range(k0 // k_left, (k0 + k_step) // k_left)

        def rows_sum(at, _, k0=k0, blocks=blocks):
            eight = pl.ds(pl.multiple_of(at * 8, 8), 8)
            for half in range(0, 8, few):

                def add(i, totals):
                    some = tri_back[i, eight, :][half : half + few][:, None]
                    return tuple(
                        total + some * left_act[s][i][None] for s, total in zip(blocks, totals)
                    )

                zeros = tuple(jnp.zeros((few, k_left, width), f32) for _ in blocks)
                totals = lax.fori_loop(0, n_i, add, zeros, unroll=16)
                for s, total in zip(blocks, totals):
                    right_sum[pl.ds(at * 8 + half, few), s * k_left : (s + 1) * k_left, :] = total.astype(bf16)
            return 0

        lax.fori_loop(0, n_j // 8, rows_sum, 0)
    for s in range(n_rows):
        for part in range(k_right // unit):
            right_out[s][:, part * unit : (part + 1) * unit, :] = right_sum[
                :, pl.ds(place(ids, n_rows, n_blk, k_left, k_right, s, part), unit), :
            ]


def weights_kernel(n_rows, n_blk, right_in, left_w, right_w, *refs):
    left_in, refs = refs[:n_blk], refs[n_blk:]
    left_out, refs = refs[:n_blk], refs[n_blk:]
    right_out, (left_part, right_part) = refs[:n_rows], refs[n_rows:]
    for inputs_ref, weight, backs, part in (
        (left_in, left_w, left_out, left_part),
        (right_in, right_w, right_out, right_part),
    ):
        part[...] = jnp.zeros_like(part)
        n, k, width = backs[0].shape
        step = 16
        flat = step * k
        for s, back_ref in enumerate(backs):

            def body(at, _, s=s, back_ref=back_ref, inputs_ref=inputs_ref, weight=weight, part=part, flat=flat, width=width):
                rows = pl.ds(at * step, step)
                inputs = (inputs_ref[s] if isinstance(inputs_ref, tuple) else inputs_ref.at[s])[rows].reshape(flat, width)
                lin, sw = gated(inputs, weight[...])
                back = back_ref[rows].reshape(flat, width).astype(f32)
                part[...] += dot_tn(inputs, joined_grad(back, lin, sw))
                return 0

            lax.fori_loop(0, n // step, body, 0, unroll=2)


def grad_middle_kernel(middle, pre_back, gate_weight, grad_middle):
    n_i, n_j, width = middle.shape
    step = 8

    def body(at, _):
        rows = pl.ds(at * step, step)
        flat = step * n_j
        normed, inverse = normalize(middle[rows].astype(f32).reshape(flat, width))
        up = dot_nt(pre_back[rows].reshape(flat, width), gate_weight[...])
        grad_middle[rows] = normalize_back(normed, inverse, up).astype(bf16).reshape(step, n_j, width)
        return 0

    lax.fori_loop(0, n_i // step, body, 0, unroll=2)


def side_kernel(n_left, n_right, *refs):
    left, right, left_w, right_w = refs[:4]
    left_back, refs = refs[4 : 4 + n_left], refs[4 + n_left :]
    right_back, refs = refs[:n_right], refs[n_right:]
    for raw, weight, backs, grad in (
        (left, left_w, left_back, refs[0]),
        (right, right_w, right_back, refs[1]),
    ):
        n, k, width = raw.shape
        step = 16
        flat = step * k

        def body(at, _, raw=raw, weight=weight, backs=backs, grad=grad, step=step, flat=flat, k=k, width=width):
            rows = pl.ds(at * step, step)
            normed, inverse = normalize(raw[rows].astype(f32).reshape(flat, width))
            lin, sw = gated(normed.astype(bf16), weight[...])
            back = backs[0][rows].astype(f32)
            for other in backs[1:]:
                back = back + other[rows].astype(f32)
            up = dot_nt(joined_grad(back.reshape(flat, width), lin, sw), weight[...])
            grad[rows] = normalize_back(normed, inverse, up).astype(bf16).reshape(step, k, width)
            return 0

        lax.fori_loop(0, n // step, body, 0, unroll=2)


def shift(x, axis, n, step):
    return lax.ppermute(x, axis, [(a, (a + step) % n) for a in range(n)])


def combine_kernel(blocks, *refs):
    refs[-1][...] = jnp.sum(blocks[...].astype(f32), axis=0).astype(bf16)


def sum_all(x, n, after):
    axes = ("rows", "blk")
    blocks = lax.all_to_all(x.reshape(n, -1, 128), axes, 0, 0)
    (total,) = call(combine_kernel, "combine", [shape(blocks.shape[1:], bf16)], after=len(after))(
        blocks, *after
    )
    whole = lax.all_to_all(jnp.broadcast_to(total[None], blocks.shape), axes, 0, 0)
    return whole.reshape(x.shape).astype(f32)


def shape(dims, kind):
    return jax.ShapeDtypeStruct(tuple(dims), kind)


def call(kernel, name, outs, scalars=0, scratch=(), after=0):
    def run(*operands):
        spaces = [pltpu.SMEM] * scalars + [pltpu.VMEM] * (len(operands) - scalars - after) + [pl.ANY] * after
        held = sum(math.prod(x.shape) * x.dtype.itemsize for x in scratch)
        return pl.pallas_call(
            kernel,
            in_specs=[pl.BlockSpec(memory_space=space) for space in spaces],
            out_specs=[pl.BlockSpec(memory_space=pltpu.VMEM)] * len(outs),
            out_shape=outs,
            scratch_shapes=list(scratch),
            compiler_params=pltpu.CompilerParams(vmem_limit_bytes=held + SCOPED),
            cost_estimate=pl.CostEstimate(flops=1000, bytes_accessed=1000, transcendentals=0),
            name=name,
        )(*operands)

    return run


def per_device(
    n_rows,
    n_blk,
    pair_left,
    pair_right,
    pair_middle,
    cotangent,
    left_weight,
    right_weight,
    gate_weight,
    output_weight,
):
    n_i, k_left, width = pair_left.shape
    n_j, k_right, _ = pair_right.shape
    n_k = k_left * n_blk
    left_raw = [pair_left] + [shift(pair_left, "blk", n_blk, s) for s in range(1, n_blk)]
    right_raw = [pair_right] + [shift(pair_right, "rows", n_rows, s) for s in range(1, n_rows)]
    middle_shape = (n_i, n_j, width)
    gate, middle_in, head_back, tri_up = call(
        middle_kernel,
        "middle",
        [shape(middle_shape, f32), shape(middle_shape, bf16), shape(middle_shape, bf16), shape(middle_shape, f32)],
    )(pair_middle, cotangent, gate_weight, output_weight)
    ids = jnp.stack([lax.axis_index("rows"), lax.axis_index("blk")]).astype(jnp.int32)
    right_act, right_in, *right_flip = call(
        functools.partial(right_kernel, n_rows, n_blk, k_left),
        "right",
        [shape((n_j * n_k, width), f32), shape((n_rows, n_j, k_right, width), bf16)]
        + [shape((k_left, n_j, width), f32)] * n_blk,
        scalars=1,
    )(ids, *right_raw, right_weight)
    left_act, left_in, total = [], [], []
    act_shape = shape(pair_left.shape, f32)
    in_shape = shape(pair_left.shape, bf16)
    for s in range(n_blk - 1):
        act, inputs, total = call(
            functools.partial(left_kernel, s == 0),
            "left",
            [act_shape, in_shape, shape(middle_shape, f32)],
        )(left_raw[s], left_weight, right_flip[s], *total)
        left_act.append(act)
        left_in.append(inputs)
        total = [total]
    act, inputs, update, pre_back, tri_back, gate_part, output_part = call(
        functools.partial(triangle_kernel, n_blk > 1),
        "triangle",
        [
            act_shape,
            in_shape,
            shape(middle_shape, bf16),
            shape(middle_shape, bf16),
            shape(middle_shape, f32),
            shape(gate_weight.shape, f32),
            shape(output_weight.shape, f32),
        ],
    )(
        left_raw[-1],
        left_weight,
        right_flip[-1],
        output_weight,
        gate,
        middle_in,
        head_back,
        tri_up,
        cotangent,
        *total,
    )
    left_act.append(act)
    left_in.append(inputs)
    left_out = call(left_back_kernel, "left_back", [shape(pair_left.shape, bf16)] * n_blk)(
        tri_back, right_act
    )
    left_back = [left_out[0]] + [shift(left_out[s], "blk", n_blk, n_blk - s) for s in range(1, n_blk)]
    right_out = call(
        functools.partial(right_back_kernel, n_rows, n_blk),
        "right_back",
        [shape(pair_right.shape, bf16)] * n_rows,
        scalars=1,
        scratch=[pltpu.VMEM((n_j, n_k, width), bf16)],
        after=1,
    )(ids, tri_back, *left_act, left_out[0])
    right_back = [right_out[0]] + [
        shift(right_out[s], "rows", n_rows, n_rows - s) for s in range(1, n_rows)
    ]
    left_part, right_part = call(
        functools.partial(weights_kernel, n_rows, n_blk),
        "weights",
        [shape(left_weight.shape, f32), shape(right_weight.shape, f32)],
    )(right_in, left_weight, right_weight, *left_in, *left_out, *right_out)
    parts = jnp.concatenate([left_part, right_part, gate_part, output_part], axis=1).astype(bf16)
    summed = sum_all(parts, n_rows * n_blk, (*left_back[1:], *right_back[1:]))
    (grad_middle,) = call(grad_middle_kernel, "grad_middle", [shape(middle_shape, bf16)])(
        pair_middle, pre_back, gate_weight
    )
    grad_left, grad_right = call(
        functools.partial(side_kernel, n_blk, n_rows),
        "sides",
        [shape(pair_left.shape, bf16), shape(pair_right.shape, bf16)],
    )(pair_left, pair_right, left_weight, right_weight, *left_back, *right_back)
    cuts = (2 * width, 4 * width, 5 * width)
    left_delta, right_delta, gate_delta, output_delta = jnp.split(summed, cuts, axis=1)
    return (
        update,
        grad_left,
        grad_right,
        grad_middle,
        left_delta,
        right_delta,
        gate_delta,
        output_delta,
    )


def solution(mesh):
    sides = P(("rep", "rows"), "blk", None)
    right = P(("rep", "blk"), "rows", None)
    return jax.shard_map(
        functools.partial(per_device, mesh.shape["rows"], mesh.shape["blk"]),
        mesh=mesh,
        in_specs=(sides, right, sides, sides, P(), P(), P(), P()),
        out_specs=(sides, sides, right, sides) + (P("rep", None),) * 4,
        check_vma=False,
    )
```

```python
import functools
import math

import jax
import jax.numpy as jnp
from jax import lax
from jax.experimental import pallas as pl
from jax.experimental.pallas import tpu as pltpu
from jax.sharding import PartitionSpec as P

epsilon = 1e-05
f32 = jnp.float32
bf16 = jnp.bfloat16
SCOPED = 6 * 1024 * 1024


def normalize(values):
    centred = values - jnp.mean(values, axis=-1, keepdims=True)
    inverse = lax.rsqrt(jnp.mean(centred * centred, axis=-1, keepdims=True) + epsilon)
    return (centred * inverse, inverse)


def normalize_back(normed, inverse, upstream):
    first = jnp.mean(upstream, axis=-1, keepdims=True)
    second = jnp.mean(upstream * normed, axis=-1, keepdims=True)
    return inverse * (upstream - first - normed * second)


def sigmoid(x):
    return 0.5 * jnp.tanh(0.5 * x) + 0.5


def dot(a, b):
    return lax.dot_general(a, b, (((1,), (0,)), ((), ())), preferred_element_type=f32)


def dot_nt(a, b):
    return lax.dot_general(a, b, (((1,), (1,)), ((), ())), preferred_element_type=f32)


def dot_tn(a, b):
    return lax.dot_general(a, b, (((0,), (0,)), ((), ())), preferred_element_type=f32)


def gated(inputs, weight):
    pre = dot(inputs, weight)
    width = weight.shape[1] // 2
    return pre[:, :width], sigmoid(pre[:, width:])


def joined_grad(back, lin, sw):
    return jnp.concatenate([back * sw, back * lin * sw * (1.0 - sw)], axis=-1).astype(bf16)


def middle_kernel(middle, cotangent, gate_weight, output_weight, gate, middle_in, head_back, tri_up):
    n_i, n_j, width = middle.shape
    step = 8

    def body(at, _):
        rows = pl.ds(at * step, step)
        normed, _ = normalize(middle[rows].astype(f32).reshape(step * n_j, width))
        inputs = normed.astype(bf16)
        opened = sigmoid(dot(inputs, gate_weight[...]))
        back = (cotangent[rows].astype(f32).reshape(step * n_j, width) * opened).astype(bf16)
        gate[rows] = opened.reshape(step, n_j, width)
        middle_in[rows] = inputs.reshape(step, n_j, width)
        head_back[rows] = back.reshape(step, n_j, width)
        tri_up[rows] = dot_nt(back, output_weight[...]).reshape(step, n_j, width)
        return 0

    lax.fori_loop(0, n_i // step, body, 0, unroll=2)


def right_kernel(n_rows, n_blk, k_left, ids, *refs):
    raw, (weight, act_out, in_out, *flip_out) = refs[:n_rows], refs[n_rows:]
    n_j, k_right, width = raw[0].shape
    n_k = k_left * n_blk
    unit = math.gcd(k_left, k_right)
    step = 16
    for s in range(n_rows):

        def body(at, _, s=s):
            rows = pl.ds(at * step, step)
            normed, _ = normalize(raw[s][rows].astype(f32).reshape(step * k_right, width))
            inputs = normed.astype(bf16)
            in_out[s, rows] = inputs.reshape(step, k_right, width)
            lin, sw = gated(inputs, weight[...])
            act = (sw * lin).astype(bf16).astype(f32).reshape(step, k_right, width)
            for part in range(k_right // unit):
                at_k = place(ids, n_rows, n_blk, k_left, k_right, s, part)
                for j in range(step):
                    start = pl.multiple_of((at * step + j) * n_k + at_k, unit)
                    act_out[pl.ds(start, unit), :] = act[j, part * unit : (part + 1) * unit]
            return 0

        lax.fori_loop(0, n_j // step, body, 0)

    for s in range(n_blk):

        def flip(k, _, s=s):
            flip_out[s][k] = act_out[pl.ds(s * k_left + k, n_j, stride=n_k), :]
            return 0

        lax.fori_loop(0, k_left, flip, 0, unroll=True)


def place(ids, n_rows, n_blk, k_left, k_right, piece, part):
    unit = math.gcd(k_left, k_right)
    vertex = lax.rem(ids[0] - piece + n_rows, n_rows) * k_right + part * unit
    block = vertex // k_left
    at = lax.rem(ids[1] - block + n_blk, n_blk) * k_left + vertex - block * k_left
    return pl.multiple_of(at, unit)


def project_left(raw, weight, act_out, in_out):
    n_i, k_left, width = raw.shape
    step = 8

    def body(at, _):
        rows = pl.ds(at * step, step)
        normed, _ = normalize(raw[rows].astype(f32).reshape(step * k_left, width))
        inputs = normed.astype(bf16)
        in_out[rows] = inputs.reshape(step, k_left, width)
        lin, sw = gated(inputs, weight[...])
        act_out[rows] = (sw * lin).astype(bf16).astype(f32).reshape(step, k_left, width)
        return 0

    lax.fori_loop(0, n_i // step, body, 0, unroll=2)


def add_vertices(total, rows, act, flip):
    for k in range(act.shape[1]):
        total = total + act[rows, k : k + 1, :] * flip[k][None]
    return total


def left_kernel(first, raw, weight, flip, *refs):
    total_in, (act_out, in_out, total_out) = refs[: 0 if first else 1], refs[0 if first else 1 :]
    n_i, n_j, width = total_out.shape
    step = 8
    project_left(raw, weight, act_out, in_out)

    def body(at, _):
        rows = pl.ds(at * step, step)
        total = jnp.zeros((step, n_j, width), f32) if first else total_in[0][rows]
        total_out[rows] = add_vertices(total, rows, act_out, flip)
        return 0

    lax.fori_loop(0, n_i // step, body, 0)


def triangle_kernel(
    has_total, raw, left_w, flip, out_w, gate, middle_in, head_back, tri_up, cotangent, *refs
):
    total_in, refs = refs[: 1 if has_total else 0], refs[1 if has_total else 0 :]
    act_out, in_out, update, pre_back, tri_back, gate_part, output_part = refs
    n_i, n_j, width = update.shape
    step = 8
    project_left(raw, left_w, act_out, in_out)
    gate_part[...] = jnp.zeros_like(gate_part)
    output_part[...] = jnp.zeros_like(output_part)

    def triangle_rows(at, _):
        rows = pl.ds(at * step, step)
        total = total_in[0][rows] if has_total else jnp.zeros((step, n_j, width), f32)
        total = add_vertices(total, rows, act_out, flip)
        flat = step * n_j
        normed, inverse = normalize(total.reshape(flat, width))
        tri_in = normed.astype(bf16)
        head = dot(tri_in, out_w[...])
        opened = gate[rows].reshape(flat, width)
        update[rows] = (opened * head).astype(bf16).reshape(step, n_j, width)
        upstream = cotangent[rows].astype(f32).reshape(flat, width)
        pre = (upstream * head * opened * (1.0 - opened)).astype(bf16)
        pre_back[rows] = pre.reshape(step, n_j, width)
        gate_part[...] += dot_tn(middle_in[rows].reshape(flat, width), pre)
        output_part[...] += dot_tn(tri_in, head_back[rows].reshape(flat, width))
        back = normalize_back(normed, inverse, tri_up[rows].reshape(flat, width))
        tri_back[rows] = back.astype(bf16).astype(f32).reshape(step, n_j, width)
        return 0

    lax.fori_loop(0, n_i // step, triangle_rows, 0, unroll=2)


def vertex_step(n_k, unit):
    size = unit
    while size * 2 <= 64 and n_k % (size * 2) == 0:
        size *= 2
    return size


def left_back_kernel(ids, tri_back, right_act, left_out):
    n_i, n_j, width = tri_back.shape
    n_blk, _, k_left, _ = left_out.shape
    n_k = k_left * n_blk
    few = 4
    k_step = vertex_step(n_k, k_left)
    for k0 in range(0, n_k, k_step):

        def rows_sum(at, _, k0=k0):
            rows = pl.ds(at * few, few)
            total = jnp.zeros((few, k_step, width), f32)
            for j in range(n_j):
                start = j * n_k + k0
                total = total + tri_back[rows, j : j + 1, :] * right_act[start : start + k_step, :][None]
            total = total.astype(bf16)
            for s in range(k0 // k_left, (k0 + k_step) // k_left):
                left_out[owner(ids, n_blk, s), rows] = total[:, s * k_left - k0 : (s + 1) * k_left - k0]
            return 0

        lax.fori_loop(0, n_i // few, rows_sum, 0)


def owner(ids, n_blk, piece):
    return lax.rem(ids[1] - piece + n_blk, n_blk)


def right_back_kernel(n_rows, n_blk, ids, tri_back, *refs):
    left_act, refs = refs[:n_blk], refs[n_blk + 1 :]
    right_out, (right_sum,) = refs[:n_rows], refs[n_rows:]
    n_i, n_j, width = tri_back.shape
    k_left = left_act[0].shape[1]
    n_k = k_left * n_blk
    k_right = right_out[0].shape[1]
    unit = math.gcd(k_left, k_right)
    few = 4
    k_step = vertex_step(n_k, k_left)
    for k0 in range(0, n_k, k_step):
        blocks = range(k0 // k_left, (k0 + k_step) // k_left)

        def rows_sum(at, _, k0=k0, blocks=blocks):
            eight = pl.ds(pl.multiple_of(at * 8, 8), 8)
            for half in range(0, 8, few):

                def add(i, totals):
                    some = tri_back[i, eight, :][half : half + few][:, None]
                    return tuple(
                        total + some * left_act[s][i][None] for s, total in zip(blocks, totals)
                    )

                zeros = tuple(jnp.zeros((few, k_left, width), f32) for _ in blocks)
                totals = lax.fori_loop(0, n_i, add, zeros, unroll=16)
                for s, total in zip(blocks, totals):
                    right_sum[pl.ds(at * 8 + half, few), s * k_left : (s + 1) * k_left, :] = total.astype(bf16)
            return 0

        lax.fori_loop(0, n_j // 8, rows_sum, 0)
    for s in range(n_rows):
        for part in range(k_right // unit):
            right_out[s][:, part * unit : (part + 1) * unit, :] = right_sum[
                :, pl.ds(place(ids, n_rows, n_blk, k_left, k_right, s, part), unit), :
            ]


def weights_kernel(n_rows, n_blk, ids, right_in, left_w, right_w, *refs):
    left_in, refs = refs[:n_blk], refs[n_blk:]
    left_out, right_out, (left_part, right_part) = refs[0], refs[1 : 1 + n_rows], refs[1 + n_rows :]
    left_backs = [left_out.at[owner(ids, n_blk, s)] for s in range(n_blk)]
    right_ins = [right_in.at[s] for s in range(n_rows)]
    for inputs_refs, weight, backs, part in (
        (left_in, left_w, left_backs, left_part),
        (right_ins, right_w, right_out, right_part),
    ):
        part[...] = jnp.zeros_like(part)
        n, k, width = inputs_refs[0].shape
        step = 16
        flat = step * k
        for inputs_ref, back_ref in zip(inputs_refs, backs):

            def body(at, _, inputs_ref=inputs_ref, back_ref=back_ref, weight=weight, part=part, flat=flat, width=width):
                rows = pl.ds(at * step, step)
                inputs = inputs_ref[rows].reshape(flat, width)
                lin, sw = gated(inputs, weight[...])
                back = back_ref[rows].reshape(flat, width).astype(f32)
                part[...] += dot_tn(inputs, joined_grad(back, lin, sw))
                return 0

            lax.fori_loop(0, n // step, body, 0, unroll=2)


def grad_middle_kernel(middle, pre_back, gate_weight, grad_middle):
    n_i, n_j, width = middle.shape
    step = 8

    def body(at, _):
        rows = pl.ds(at * step, step)
        flat = step * n_j
        normed, inverse = normalize(middle[rows].astype(f32).reshape(flat, width))
        up = dot_nt(pre_back[rows].reshape(flat, width), gate_weight[...])
        grad_middle[rows] = normalize_back(normed, inverse, up).astype(bf16).reshape(step, n_j, width)
        return 0

    lax.fori_loop(0, n_i // step, body, 0, unroll=2)


def side_kernel(n_right, *refs):
    left, right, left_w, right_w, left_backs = refs[:5]
    refs = refs[5:]
    left_back = [left_backs.at[s] for s in range(left_backs.shape[0])]
    right_back, refs = refs[:n_right], refs[n_right:]
    for raw, weight, backs, grad in (
        (left, left_w, left_back, refs[0]),
        (right, right_w, right_back, refs[1]),
    ):
        n, k, width = raw.shape
        step = 16
        flat = step * k

        def body(at, _, raw=raw, weight=weight, backs=backs, grad=grad, step=step, flat=flat, k=k, width=width):
            rows = pl.ds(at * step, step)
            normed, inverse = normalize(raw[rows].astype(f32).reshape(flat, width))
            lin, sw = gated(normed.astype(bf16), weight[...])
            back = backs[0][rows].astype(f32)
            for other in backs[1:]:
                back = back + other[rows].astype(f32)
            up = dot_nt(joined_grad(back.reshape(flat, width), lin, sw), weight[...])
            grad[rows] = normalize_back(normed, inverse, up).astype(bf16).reshape(step, k, width)
            return 0

        lax.fori_loop(0, n // step, body, 0, unroll=2)


def shift(x, axis, n, step):
    return lax.ppermute(x, axis, [(a, (a + step) % n) for a in range(n)])


def combine_kernel(blocks, *refs):
    refs[-1][...] = jnp.sum(blocks[...].astype(f32), axis=0).astype(bf16)


def sum_all(x, n, after):
    axes = ("rows", "blk")
    blocks = lax.all_to_all(x.reshape(n, -1, 128), axes, 0, 0)
    (total,) = call(combine_kernel, "combine", [shape(blocks.shape[1:], bf16)], after=len(after))(
        blocks, *after
    )
    whole = lax.all_to_all(jnp.broadcast_to(total[None], blocks.shape), axes, 0, 0)
    return whole.reshape(x.shape).astype(f32)


def shape(dims, kind):
    return jax.ShapeDtypeStruct(tuple(dims), kind)


def call(kernel, name, outs, scalars=0, scratch=(), after=0):
    def run(*operands):
        spaces = [pltpu.SMEM] * scalars + [pltpu.VMEM] * (len(operands) - scalars - after) + [pl.ANY] * after
        held = sum(math.prod(x.shape) * x.dtype.itemsize for x in scratch)
        return pl.pallas_call(
            kernel,
            in_specs=[pl.BlockSpec(memory_space=space) for space in spaces],
            out_specs=[pl.BlockSpec(memory_space=pltpu.VMEM)] * len(outs),
            out_shape=outs,
            scratch_shapes=list(scratch),
            compiler_params=pltpu.CompilerParams(vmem_limit_bytes=held + SCOPED),
            cost_estimate=pl.CostEstimate(flops=1000, bytes_accessed=1000, transcendentals=0),
            name=name,
        )(*operands)

    return run


def per_device(
    n_rows,
    n_blk,
    pair_left,
    pair_right,
    pair_middle,
    cotangent,
    left_weight,
    right_weight,
    gate_weight,
    output_weight,
):
    n_i, k_left, width = pair_left.shape
    n_j, k_right, _ = pair_right.shape
    n_k = k_left * n_blk
    left_raw = [pair_left] + [shift(pair_left, "blk", n_blk, s) for s in range(1, n_blk)]
    right_raw = [pair_right] + [shift(pair_right, "rows", n_rows, s) for s in range(1, n_rows)]
    middle_shape = (n_i, n_j, width)
    gate, middle_in, head_back, tri_up = call(
        middle_kernel,
        "middle",
        [shape(middle_shape, f32), shape(middle_shape, bf16), shape(middle_shape, bf16), shape(middle_shape, f32)],
    )(pair_middle, cotangent, gate_weight, output_weight)
    ids = jnp.stack([lax.axis_index("rows"), lax.axis_index("blk")]).astype(jnp.int32)
    right_act, right_in, *right_flip = call(
        functools.partial(right_kernel, n_rows, n_blk, k_left),
        "right",
        [shape((n_j * n_k, width), f32), shape((n_rows, n_j, k_right, width), bf16)]
        + [shape((k_left, n_j, width), f32)] * n_blk,
        scalars=1,
    )(ids, *right_raw, right_weight)
    left_act, left_in, total = [], [], []
    act_shape = shape(pair_left.shape, f32)
    in_shape = shape(pair_left.shape, bf16)
    for s in range(n_blk - 1):
        act, inputs, total = call(
            functools.partial(left_kernel, s == 0),
            "left",
            [act_shape, in_shape, shape(middle_shape, f32)],
        )(left_raw[s], left_weight, right_flip[s], *total)
        left_act.append(act)
        left_in.append(inputs)
        total = [total]
    act, inputs, update, pre_back, tri_back, gate_part, output_part = call(
        functools.partial(triangle_kernel, n_blk > 1),
        "triangle",
        [
            act_shape,
            in_shape,
            shape(middle_shape, bf16),
            shape(middle_shape, bf16),
            shape(middle_shape, f32),
            shape(gate_weight.shape, f32),
            shape(output_weight.shape, f32),
        ],
    )(
        left_raw[-1],
        left_weight,
        right_flip[-1],
        output_weight,
        gate,
        middle_in,
        head_back,
        tri_up,
        cotangent,
        *total,
    )
    left_act.append(act)
    left_in.append(inputs)
    (left_out,) = call(
        left_back_kernel, "left_back", [shape((n_blk,) + pair_left.shape, bf16)], scalars=1
    )(ids, tri_back, right_act)
    left_back = lax.all_to_all(left_out, "blk", 0, 0)
    right_out = call(
        functools.partial(right_back_kernel, n_rows, n_blk),
        "right_back",
        [shape(pair_right.shape, bf16)] * n_rows,
        scalars=1,
        scratch=[pltpu.VMEM((n_j, n_k, width), bf16)],
        after=1,
    )(ids, tri_back, *left_act, left_out)
    right_back = [right_out[0]] + [
        shift(right_out[s], "rows", n_rows, n_rows - s) for s in range(1, n_rows)
    ]
    left_part, right_part = call(
        functools.partial(weights_kernel, n_rows, n_blk),
        "weights",
        [shape(left_weight.shape, f32), shape(right_weight.shape, f32)],
        scalars=1,
    )(ids, right_in, left_weight, right_weight, *left_in, left_out, *right_out)
    parts = jnp.concatenate([left_part, right_part, gate_part, output_part], axis=1).astype(bf16)
    summed = sum_all(parts, n_rows * n_blk, tuple(right_back[1:]))
    (grad_middle,) = call(grad_middle_kernel, "grad_middle", [shape(middle_shape, bf16)])(
        pair_middle, pre_back, gate_weight
    )
    grad_left, grad_right = call(
        functools.partial(side_kernel, n_rows),
        "sides",
        [shape(pair_left.shape, bf16), shape(pair_right.shape, bf16)],
    )(pair_left, pair_right, left_weight, right_weight, left_back, *right_back)
    cuts = (2 * width, 4 * width, 5 * width)
    left_delta, right_delta, gate_delta, output_delta = jnp.split(summed, cuts, axis=1)
    return (
        update,
        grad_left,
        grad_right,
        grad_middle,
        left_delta,
        right_delta,
        gate_delta,
        output_delta,
    )


def solution(mesh):
    sides = P(("rep", "rows"), "blk", None)
    right = P(("rep", "blk"), "rows", None)
    return jax.shard_map(
        functools.partial(per_device, mesh.shape["rows"], mesh.shape["blk"]),
        mesh=mesh,
        in_specs=(sides, right, sides, sides, P(), P(), P(), P()),
        out_specs=(sides, sides, right, sides) + (P("rep", None),) * 4,
        check_vma=False,
    )
```

```python
import functools
import math

import jax
import jax.numpy as jnp
from jax import lax
from jax.experimental import pallas as pl
from jax.experimental.pallas import tpu as pltpu
from jax.sharding import PartitionSpec as P

epsilon = 1e-05
f32 = jnp.float32
bf16 = jnp.bfloat16
SCOPED = 6 * 1024 * 1024


def normalize(values):
    centred = values - jnp.mean(values, axis=-1, keepdims=True)
    inverse = lax.rsqrt(jnp.mean(centred * centred, axis=-1, keepdims=True) + epsilon)
    return (centred * inverse, inverse)


def normalize_back(normed, inverse, upstream):
    first = jnp.mean(upstream, axis=-1, keepdims=True)
    second = jnp.mean(upstream * normed, axis=-1, keepdims=True)
    return inverse * (upstream - first - normed * second)


def sigmoid(x):
    return 0.5 * jnp.tanh(0.5 * x) + 0.5


def dot(a, b):
    return lax.dot_general(a, b, (((1,), (0,)), ((), ())), preferred_element_type=f32)


def dot_nt(a, b):
    return lax.dot_general(a, b, (((1,), (1,)), ((), ())), preferred_element_type=f32)


def dot_tn(a, b):
    return lax.dot_general(a, b, (((0,), (0,)), ((), ())), preferred_element_type=f32)


def gated(inputs, weight):
    pre = dot(inputs, weight)
    width = weight.shape[1] // 2
    return pre[:, :width], sigmoid(pre[:, width:])


def joined_grad(back, lin, sw):
    return jnp.concatenate([back * sw, back * lin * sw * (1.0 - sw)], axis=-1).astype(bf16)


def middle_kernel(middle, cotangent, gate_weight, output_weight, gate, middle_in, head_back, tri_up):
    n_i, n_j, width = middle.shape
    step = 8

    def body(at, _):
        rows = pl.ds(at * step, step)
        normed, _ = normalize(middle[rows].astype(f32).reshape(step * n_j, width))
        inputs = normed.astype(bf16)
        opened = sigmoid(dot(inputs, gate_weight[...]))
        back = (cotangent[rows].astype(f32).reshape(step * n_j, width) * opened).astype(bf16)
        gate[rows] = opened.reshape(step, n_j, width)
        middle_in[rows] = inputs.reshape(step, n_j, width)
        head_back[rows] = back.reshape(step, n_j, width)
        tri_up[rows] = dot_nt(back, output_weight[...]).reshape(step, n_j, width)
        return 0

    lax.fori_loop(0, n_i // step, body, 0, unroll=2)


def right_kernel(n_rows, n_blk, k_left, ids, *refs):
    raw, (weight, act_out, in_out, *flip_out) = refs[:n_rows], refs[n_rows:]
    n_j, k_right, width = raw[0].shape
    n_k = k_left * n_blk
    unit = math.gcd(k_left, k_right)
    step = 16
    for s in range(n_rows):

        def body(at, _, s=s):
            rows = pl.ds(at * step, step)
            normed, _ = normalize(raw[s][rows].astype(f32).reshape(step * k_right, width))
            inputs = normed.astype(bf16)
            in_out[s, rows] = inputs.reshape(step, k_right, width)
            lin, sw = gated(inputs, weight[...])
            act = (sw * lin).astype(bf16).astype(f32).reshape(step, k_right, width)
            for part in range(k_right // unit):
                at_k = place(ids, n_rows, n_blk, k_left, k_right, s, part)
                for j in range(step):
                    start = pl.multiple_of((at * step + j) * n_k + at_k, unit)
                    act_out[pl.ds(start, unit), :] = act[j, part * unit : (part + 1) * unit]
            return 0

        lax.fori_loop(0, n_j // step, body, 0)

    for s in range(n_blk):

        def flip(k, _, s=s):
            flip_out[s][k] = act_out[pl.ds(s * k_left + k, n_j, stride=n_k), :]
            return 0

        lax.fori_loop(0, k_left, flip, 0, unroll=True)


def place(ids, n_rows, n_blk, k_left, k_right, piece, part):
    unit = math.gcd(k_left, k_right)
    vertex = lax.rem(ids[0] - piece + n_rows, n_rows) * k_right + part * unit
    block = vertex // k_left
    at = lax.rem(ids[1] - block + n_blk, n_blk) * k_left + vertex - block * k_left
    return pl.multiple_of(at, unit)


def project_left(raw, weight, act_out, in_out):
    n_i, k_left, width = raw.shape
    step = 8

    def body(at, _):
        rows = pl.ds(at * step, step)
        normed, _ = normalize(raw[rows].astype(f32).reshape(step * k_left, width))
        inputs = normed.astype(bf16)
        in_out[rows] = inputs.reshape(step, k_left, width)
        lin, sw = gated(inputs, weight[...])
        act_out[rows] = (sw * lin).astype(bf16).astype(f32).reshape(step, k_left, width)
        return 0

    lax.fori_loop(0, n_i // step, body, 0, unroll=2)


def add_vertices(total, rows, act, flip):
    for k in range(act.shape[1]):
        total = total + act[rows, k : k + 1, :] * flip[k][None]
    return total


def left_kernel(first, raw, weight, flip, *refs):
    total_in, (act_out, in_out, total_out) = refs[: 0 if first else 1], refs[0 if first else 1 :]
    n_i, n_j, width = total_out.shape
    step = 8
    project_left(raw, weight, act_out, in_out)

    def body(at, _):
        rows = pl.ds(at * step, step)
        total = jnp.zeros((step, n_j, width), f32) if first else total_in[0][rows]
        total_out[rows] = add_vertices(total, rows, act_out, flip)
        return 0

    lax.fori_loop(0, n_i // step, body, 0)


def triangle_kernel(
    has_total, raw, left_w, flip, out_w, gate, middle_in, head_back, tri_up, cotangent, *refs
):
    total_in, refs = refs[: 1 if has_total else 0], refs[1 if has_total else 0 :]
    act_out, in_out, update, pre_back, tri_back, gate_part, output_part = refs
    n_i, n_j, width = update.shape
    step = 8
    project_left(raw, left_w, act_out, in_out)
    gate_part[...] = jnp.zeros_like(gate_part)
    output_part[...] = jnp.zeros_like(output_part)

    def triangle_rows(at, _):
        rows = pl.ds(at * step, step)
        total = total_in[0][rows] if has_total else jnp.zeros((step, n_j, width), f32)
        total = add_vertices(total, rows, act_out, flip)
        flat = step * n_j
        normed, inverse = normalize(total.reshape(flat, width))
        tri_in = normed.astype(bf16)
        head = dot(tri_in, out_w[...])
        opened = gate[rows].reshape(flat, width)
        update[rows] = (opened * head).astype(bf16).reshape(step, n_j, width)
        upstream = cotangent[rows].astype(f32).reshape(flat, width)
        pre = (upstream * head * opened * (1.0 - opened)).astype(bf16)
        pre_back[rows] = pre.reshape(step, n_j, width)
        gate_part[...] += dot_tn(middle_in[rows].reshape(flat, width), pre)
        output_part[...] += dot_tn(tri_in, head_back[rows].reshape(flat, width))
        back = normalize_back(normed, inverse, tri_up[rows].reshape(flat, width))
        tri_back[rows] = back.astype(bf16).astype(f32).reshape(step, n_j, width)
        return 0

    lax.fori_loop(0, n_i // step, triangle_rows, 0, unroll=2)


def vertex_step(n_k, unit):
    size = unit
    while size * 2 <= 64 and n_k % (size * 2) == 0:
        size *= 2
    return size


def left_back_kernel(ids, tri_back, right_act, left_out):
    n_i, n_j, width = tri_back.shape
    n_blk, _, k_left, _ = left_out.shape
    n_k = k_left * n_blk
    few = 4
    k_step = vertex_step(n_k, k_left)
    for k0 in range(0, n_k, k_step):

        def rows_sum(at, _, k0=k0):
            rows = pl.ds(at * few, few)
            total = jnp.zeros((few, k_step, width), f32)
            for j in range(n_j):
                start = j * n_k + k0
                total = total + tri_back[rows, j : j + 1, :] * right_act[start : start + k_step, :][None]
            total = total.astype(bf16)
            for s in range(k0 // k_left, (k0 + k_step) // k_left):
                left_out[owner(ids, n_blk, s), rows] = total[:, s * k_left - k0 : (s + 1) * k_left - k0]
            return 0

        lax.fori_loop(0, n_i // few, rows_sum, 0)


def owner(ids, n_blk, piece):
    return lax.rem(ids[1] - piece + n_blk, n_blk)


def right_back_kernel(n_rows, n_blk, ids, tri_back, *refs):
    left_act, refs = refs[:n_blk], refs[n_blk + 1 :]
    right_out, (right_sum,) = refs[:n_rows], refs[n_rows:]
    n_i, n_j, width = tri_back.shape
    k_left = left_act[0].shape[1]
    n_k = k_left * n_blk
    k_right = right_out[0].shape[1]
    unit = math.gcd(k_left, k_right)
    few = 4
    k_step = vertex_step(n_k, k_left)
    for k0 in range(0, n_k, k_step):
        blocks = range(k0 // k_left, (k0 + k_step) // k_left)

        def rows_sum(at, _, k0=k0, blocks=blocks):
            eight = pl.ds(pl.multiple_of(at * 8, 8), 8)
            for half in range(0, 8, few):

                def add(i, totals):
                    some = tri_back[i, eight, :][half : half + few][:, None]
                    return tuple(
                        total + some * left_act[s][i][None] for s, total in zip(blocks, totals)
                    )

                zeros = tuple(jnp.zeros((few, k_left, width), f32) for _ in blocks)
                totals = lax.fori_loop(0, n_i, add, zeros, unroll=16)
                for s, total in zip(blocks, totals):
                    right_sum[pl.ds(at * 8 + half, few), s * k_left : (s + 1) * k_left, :] = total.astype(bf16)
            return 0

        lax.fori_loop(0, n_j // 8, rows_sum, 0)
    for s in range(n_rows):
        for part in range(k_right // unit):
            right_out[s][:, part * unit : (part + 1) * unit, :] = right_sum[
                :, pl.ds(place(ids, n_rows, n_blk, k_left, k_right, s, part), unit), :
            ]


def weights_kernel(n_rows, n_blk, ids, right_in, left_w, right_w, gate_part, output_part, *refs):
    left_in, refs = refs[:n_blk], refs[n_blk:]
    left_out, right_out, refs = refs[0], refs[1 : 1 + n_rows], refs[1 + n_rows :]
    pieces, (total,) = refs[:n_rows], refs[n_rows:]
    left_backs = [left_out.at[owner(ids, n_blk, s)] for s in range(n_blk)]
    right_ins = [right_in.at[s] for s in range(n_rows)]
    width = gate_part.shape[0]
    total[:, 4 * width : 5 * width] = gate_part[...]
    total[:, 5 * width :] = output_part[...]
    for inputs_refs, weight, backs, first in (
        (left_in, left_w, left_backs, 0),
        (right_ins, right_w, right_out, 2 * width),
    ):
        columns = slice(first, first + 2 * width)
        total[:, columns] = jnp.zeros((width, 2 * width), f32)
        n, k, _ = inputs_refs[0].shape
        step = 16
        flat = step * k
        for inputs_ref, back_ref in zip(inputs_refs, backs):

            def body(at, _, inputs_ref=inputs_ref, back_ref=back_ref, weight=weight, columns=columns, flat=flat):
                rows = pl.ds(at * step, step)
                inputs = inputs_ref[rows].reshape(flat, width)
                lin, sw = gated(inputs, weight[...])
                back = back_ref[rows].reshape(flat, width).astype(f32)
                total[:, columns] += dot_tn(inputs, joined_grad(back, lin, sw))
                return 0

            lax.fori_loop(0, n // step, body, 0, unroll=2)
    size = width // n_rows
    for s, piece in enumerate(pieces):
        start = pl.multiple_of(lax.rem(ids[0] + s, n_rows) * size, size)
        piece[...] = total[pl.ds(start, size), :].astype(bf16)


def grad_middle_kernel(middle, pre_back, gate_weight, grad_middle):
    n_i, n_j, width = middle.shape
    step = 8

    def body(at, _):
        rows = pl.ds(at * step, step)
        flat = step * n_j
        normed, inverse = normalize(middle[rows].astype(f32).reshape(flat, width))
        up = dot_nt(pre_back[rows].reshape(flat, width), gate_weight[...])
        grad_middle[rows] = normalize_back(normed, inverse, up).astype(bf16).reshape(step, n_j, width)
        return 0

    lax.fori_loop(0, n_i // step, body, 0, unroll=2)


def side_kernel(n_right, *refs):
    left, right, left_w, right_w, left_backs = refs[:5]
    refs = refs[5:]
    left_back = [left_backs.at[s] for s in range(left_backs.shape[0])]
    right_back, refs = refs[:n_right], refs[n_right:]
    for raw, weight, backs, grad in (
        (left, left_w, left_back, refs[0]),
        (right, right_w, right_back, refs[1]),
    ):
        n, k, width = raw.shape
        step = 16
        flat = step * k

        def body(at, _, raw=raw, weight=weight, backs=backs, grad=grad, step=step, flat=flat, k=k, width=width):
            rows = pl.ds(at * step, step)
            normed, inverse = normalize(raw[rows].astype(f32).reshape(flat, width))
            lin, sw = gated(normed.astype(bf16), weight[...])
            back = backs[0][rows].astype(f32)
            for other in backs[1:]:
                back = back + other[rows].astype(f32)
            up = dot_nt(joined_grad(back.reshape(flat, width), lin, sw), weight[...])
            grad[rows] = normalize_back(normed, inverse, up).astype(bf16).reshape(step, k, width)
            return 0

        lax.fori_loop(0, n // step, body, 0, unroll=2)


def shift(x, axis, n, step):
    return lax.ppermute(x, axis, [(a, (a + step) % n) for a in range(n)])


def combine_kernel(n, *refs):
    total = refs[0][...].astype(f32)
    for other in refs[1:n]:
        total = total + other[...].astype(f32)
    refs[-1][...] = total.astype(bf16)


def combine(pieces, after=()):
    (total,) = call(
        functools.partial(combine_kernel, len(pieces)),
        "combine",
        [shape(pieces[0].shape, bf16)],
        after=len(after),
    )(*pieces, *after)
    return total


def deltas_kernel(n_rows, ids, *refs):
    pieces, outs = refs[:n_rows], refs[n_rows:]
    size = pieces[0].shape[0]
    for s, piece in enumerate(pieces):
        start = pl.multiple_of(lax.rem(ids[0] - s + n_rows, n_rows) * size, size)
        first = 0
        for out in outs:
            last = first + out.shape[1]
            out[pl.ds(start, size), :] = piece[:, first:last].astype(f32)
            first = last


def shape(dims, kind):
    return jax.ShapeDtypeStruct(tuple(dims), kind)


def call(kernel, name, outs, scalars=0, scratch=(), after=0):
    def run(*operands):
        spaces = [pltpu.SMEM] * scalars + [pltpu.VMEM] * (len(operands) - scalars - after) + [pl.ANY] * after
        held = sum(math.prod(x.shape) * x.dtype.itemsize for x in scratch)
        return pl.pallas_call(
            kernel,
            in_specs=[pl.BlockSpec(memory_space=space) for space in spaces],
            out_specs=[pl.BlockSpec(memory_space=pltpu.VMEM)] * len(outs),
            out_shape=outs,
            scratch_shapes=list(scratch),
            compiler_params=pltpu.CompilerParams(vmem_limit_bytes=held + SCOPED),
            cost_estimate=pl.CostEstimate(flops=1000, bytes_accessed=1000, transcendentals=0),
            name=name,
        )(*operands)

    return run


def per_device(
    n_rows,
    n_blk,
    pair_left,
    pair_right,
    pair_middle,
    cotangent,
    left_weight,
    right_weight,
    gate_weight,
    output_weight,
):
    n_i, k_left, width = pair_left.shape
    n_j, k_right, _ = pair_right.shape
    n_k = k_left * n_blk
    left_raw = [pair_left] + [shift(pair_left, "blk", n_blk, s) for s in range(1, n_blk)]
    right_raw = [pair_right] + [shift(pair_right, "rows", n_rows, s) for s in range(1, n_rows)]
    middle_shape = (n_i, n_j, width)
    gate, middle_in, head_back, tri_up = call(
        middle_kernel,
        "middle",
        [shape(middle_shape, f32), shape(middle_shape, bf16), shape(middle_shape, bf16), shape(middle_shape, f32)],
    )(pair_middle, cotangent, gate_weight, output_weight)
    ids = jnp.stack([lax.axis_index("rows"), lax.axis_index("blk")]).astype(jnp.int32)
    right_act, right_in, *right_flip = call(
        functools.partial(right_kernel, n_rows, n_blk, k_left),
        "right",
        [shape((n_j * n_k, width), f32), shape((n_rows, n_j, k_right, width), bf16)]
        + [shape((k_left, n_j, width), f32)] * n_blk,
        scalars=1,
    )(ids, *right_raw, right_weight)
    left_act, left_in, total = [], [], []
    act_shape = shape(pair_left.shape, f32)
    in_shape = shape(pair_left.shape, bf16)
    for s in range(n_blk - 1):
        act, inputs, total = call(
            functools.partial(left_kernel, s == 0),
            "left",
            [act_shape, in_shape, shape(middle_shape, f32)],
        )(left_raw[s], left_weight, right_flip[s], *total)
        left_act.append(act)
        left_in.append(inputs)
        total = [total]
    act, inputs, update, pre_back, tri_back, gate_part, output_part = call(
        functools.partial(triangle_kernel, n_blk > 1),
        "triangle",
        [
            act_shape,
            in_shape,
            shape(middle_shape, bf16),
            shape(middle_shape, bf16),
            shape(middle_shape, f32),
            shape(gate_weight.shape, f32),
            shape(output_weight.shape, f32),
        ],
    )(
        left_raw[-1],
        left_weight,
        right_flip[-1],
        output_weight,
        gate,
        middle_in,
        head_back,
        tri_up,
        cotangent,
        *total,
    )
    left_act.append(act)
    left_in.append(inputs)
    (left_out,) = call(
        left_back_kernel, "left_back", [shape((n_blk,) + pair_left.shape, bf16)], scalars=1
    )(ids, tri_back, right_act)
    left_back = lax.all_to_all(left_out, "blk", 0, 0)
    right_out = call(
        functools.partial(right_back_kernel, n_rows, n_blk),
        "right_back",
        [shape(pair_right.shape, bf16)] * n_rows,
        scalars=1,
        scratch=[pltpu.VMEM((n_j, n_k, width), bf16)],
        after=1,
    )(ids, tri_back, *left_act, left_out)
    right_back = [right_out[0]] + [
        shift(right_out[s], "rows", n_rows, n_rows - s) for s in range(1, n_rows)
    ]
    pieces = call(
        functools.partial(weights_kernel, n_rows, n_blk),
        "weights",
        [shape((width // n_rows, 6 * width), bf16)] * n_rows,
        scalars=1,
        scratch=[pltpu.VMEM((width, 6 * width), f32)],
    )(ids, right_in, left_weight, right_weight, gate_part, output_part, *left_in, left_out, *right_out)
    pieces = [pieces[0]] + [shift(pieces[s], "rows", n_rows, s) for s in range(1, n_rows)]
    part = combine(pieces, (left_back, *right_back[1:]))
    part = combine([part] + [shift(part, "blk", n_blk, s) for s in range(1, n_blk)])
    pieces = [part] + [shift(part, "rows", n_rows, s) for s in range(1, n_rows)]
    deltas = call(
        functools.partial(deltas_kernel, n_rows),
        "deltas",
        [shape(x.shape, f32) for x in (left_weight, right_weight, gate_weight, output_weight)],
        scalars=1,
    )(ids, *pieces)
    (grad_middle,) = call(grad_middle_kernel, "grad_middle", [shape(middle_shape, bf16)])(
        pair_middle, pre_back, gate_weight
    )
    grad_left, grad_right = call(
        functools.partial(side_kernel, n_rows),
        "sides",
        [shape(pair_left.shape, bf16), shape(pair_right.shape, bf16)],
    )(pair_left, pair_right, left_weight, right_weight, left_back, *right_back)
    return (
        update,
        grad_left,
        grad_right,
        grad_middle,
        *deltas,
    )


def solution(mesh):
    sides = P(("rep", "rows"), "blk", None)
    right = P(("rep", "blk"), "rows", None)
    return jax.shard_map(
        functools.partial(per_device, mesh.shape["rows"], mesh.shape["blk"]),
        mesh=mesh,
        in_specs=(sides, right, sides, sides, P(), P(), P(), P()),
        out_specs=(sides, sides, right, sides) + (P("rep", None),) * 4,
        check_vma=False,
    )
```

```python
import functools
import math

import jax
import jax.numpy as jnp
from jax import lax
from jax.experimental import pallas as pl
from jax.experimental.pallas import tpu as pltpu
from jax.sharding import PartitionSpec as P

epsilon = 1e-05
f32 = jnp.float32
bf16 = jnp.bfloat16
SCOPED = 6 * 1024 * 1024


def normalize(values):
    centred = values - jnp.mean(values, axis=-1, keepdims=True)
    inverse = lax.rsqrt(jnp.mean(centred * centred, axis=-1, keepdims=True) + epsilon)
    return (centred * inverse, inverse)


def normalize_back(normed, inverse, upstream):
    first = jnp.mean(upstream, axis=-1, keepdims=True)
    second = jnp.mean(upstream * normed, axis=-1, keepdims=True)
    return inverse * (upstream - first - normed * second)


def sigmoid(x):
    return 0.5 * jnp.tanh(0.5 * x) + 0.5


def dot(a, b):
    return lax.dot_general(a, b, (((1,), (0,)), ((), ())), preferred_element_type=f32)


def dot_nt(a, b):
    return lax.dot_general(a, b, (((1,), (1,)), ((), ())), preferred_element_type=f32)


def dot_tn(a, b):
    return lax.dot_general(a, b, (((0,), (0,)), ((), ())), preferred_element_type=f32)


def gated(inputs, weight):
    pre = dot(inputs, weight)
    width = weight.shape[1] // 2
    return pre[:, :width], sigmoid(pre[:, width:])


def joined_grad(back, lin, sw):
    return jnp.concatenate([back * sw, back * lin * sw * (1.0 - sw)], axis=-1).astype(bf16)


def middle_kernel(*refs):
    sources, refs = refs[:4], refs[4:]
    gate, middle_in, head_back, tri_up, middle, cotangent, gate_weight, output_weight, arrived = refs
    n_i, n_j, width = middle.shape
    step = 8
    copies = [
        pltpu.make_async_copy(source, target, arrived.at[at])
        for at, (source, target) in enumerate(zip(sources, (middle, cotangent, gate_weight, output_weight)))
    ]
    for copy in copies:
        copy.start()
    for copy in copies:
        copy.wait()

    def body(at, _):
        rows = pl.ds(at * step, step)
        normed, _ = normalize(middle[rows].astype(f32).reshape(step * n_j, width))
        inputs = normed.astype(bf16)
        opened = sigmoid(dot(inputs, gate_weight[...]))
        back = (cotangent[rows].astype(f32).reshape(step * n_j, width) * opened).astype(bf16)
        gate[rows] = opened.reshape(step, n_j, width)
        middle_in[rows] = inputs.reshape(step, n_j, width)
        head_back[rows] = back.reshape(step, n_j, width)
        tri_up[rows] = dot_nt(back, output_weight[...]).reshape(step, n_j, width)
        return 0

    lax.fori_loop(0, n_i // step, body, 0, unroll=2)


def right_kernel(n_rows, n_blk, k_left, *refs):
    raw, (weight, act_out, in_out, *flip_out) = refs[:n_rows], refs[n_rows:]
    n_j, k_right, width = raw[0].shape
    n_k = k_left * n_blk
    unit = math.gcd(k_left, k_right)
    step = 16
    for s in range(n_rows):

        def body(at, _, s=s):
            rows = pl.ds(at * step, step)
            normed, _ = normalize(raw[s][rows].astype(f32).reshape(step * k_right, width))
            inputs = normed.astype(bf16)
            in_out[s, rows] = inputs.reshape(step, k_right, width)
            lin, sw = gated(inputs, weight[...])
            act = (sw * lin).astype(bf16).astype(f32).reshape(step, k_right, width)
            for part in range(k_right // unit):
                at_k = place(n_rows, n_blk, k_left, k_right, s, part)
                for j in range(step):
                    start = pl.multiple_of((at * step + j) * n_k + at_k, unit)
                    act_out[pl.ds(start, unit), :] = act[j, part * unit : (part + 1) * unit]
            return 0

        lax.fori_loop(0, n_j // step, body, 0)

    for s in range(n_blk):

        def flip(k, _, s=s):
            flip_out[s][k] = act_out[pl.ds(s * k_left + k, n_j, stride=n_k), :]
            return 0

        lax.fori_loop(0, k_left, flip, 0, unroll=True)


def place(n_rows, n_blk, k_left, k_right, piece, part):
    unit = math.gcd(k_left, k_right)
    vertex = lax.rem(lax.axis_index("rows") - piece + n_rows, n_rows) * k_right + part * unit
    block = vertex // k_left
    at = lax.rem(lax.axis_index("blk") - block + n_blk, n_blk) * k_left + vertex - block * k_left
    return pl.multiple_of(at, unit)


def project_left(raw, weight, act_out, in_out):
    n_i, k_left, width = raw.shape
    step = 8

    def body(at, _):
        rows = pl.ds(at * step, step)
        normed, _ = normalize(raw[rows].astype(f32).reshape(step * k_left, width))
        inputs = normed.astype(bf16)
        in_out[rows] = inputs.reshape(step, k_left, width)
        lin, sw = gated(inputs, weight[...])
        act_out[rows] = (sw * lin).astype(bf16).astype(f32).reshape(step, k_left, width)
        return 0

    lax.fori_loop(0, n_i // step, body, 0, unroll=2)


def add_vertices(rows, act, flip):
    total = act[rows, 0:1, :] * flip[0][None]
    for k in range(1, act.shape[1]):
        total = total + act[rows, k : k + 1, :] * flip[k][None]
    return total


def left_kernel(first, raw, weight, flip, *refs):
    total_in, (act_out, in_out, total_out) = refs[: 0 if first else 1], refs[0 if first else 1 :]
    n_i, n_j, width = total_out.shape
    step = 8
    project_left(raw, weight, act_out, in_out)

    def body(at, _):
        rows = pl.ds(at * step, step)
        total = add_vertices(rows, act_out, flip)
        total_out[rows] = total if first else total_in[0][rows] + total
        return 0

    lax.fori_loop(0, n_i // step, body, 0)


def triangle_kernel(
    has_total, raw, left_w, flip, out_w, gate, middle_in, head_back, tri_up, cotangent, *refs
):
    total_in, refs = refs[: 1 if has_total else 0], refs[1 if has_total else 0 :]
    act_out, in_out, update, pre_back, tri_back, gate_part, output_part = refs
    n_i, n_j, width = update.shape
    step = 8
    project_left(raw, left_w, act_out, in_out)
    gate_part[...] = jnp.zeros_like(gate_part)
    output_part[...] = jnp.zeros_like(output_part)

    def triangle_rows(at, _):
        rows = pl.ds(at * step, step)
        total = add_vertices(rows, act_out, flip)
        if has_total:
            total = total + total_in[0][rows]
        flat = step * n_j
        normed, inverse = normalize(total.reshape(flat, width))
        tri_in = normed.astype(bf16)
        head = dot(tri_in, out_w[...])
        opened = gate[rows].reshape(flat, width)
        update[rows] = (opened * head).astype(bf16).reshape(step, n_j, width)
        upstream = cotangent[rows].astype(f32).reshape(flat, width)
        pre = (upstream * head * opened * (1.0 - opened)).astype(bf16)
        pre_back[rows] = pre.reshape(step, n_j, width)
        gate_part[...] += dot_tn(middle_in[rows].reshape(flat, width), pre)
        output_part[...] += dot_tn(tri_in, head_back[rows].reshape(flat, width))
        back = normalize_back(normed, inverse, tri_up[rows].reshape(flat, width))
        tri_back[rows] = back.astype(bf16).astype(f32).reshape(step, n_j, width)
        return 0

    lax.fori_loop(0, n_i // step, triangle_rows, 0, unroll=2)


def vertex_step(n_k, unit):
    size = unit
    while size * 2 <= 64 and n_k % (size * 2) == 0:
        size *= 2
    return size


def left_back_kernel(tri_back, right_act, *left_out):
    n_i, n_j, width = tri_back.shape
    k_left = left_out[0].shape[1]
    n_k = k_left * len(left_out)
    few = 4
    k_step = vertex_step(n_k, k_left)
    for k0 in range(0, n_k, k_step):

        def rows_sum(at, _, k0=k0):
            rows = pl.ds(at * few, few)
            total = jnp.zeros((few, k_step, width), f32)
            for j in range(n_j):
                start = j * n_k + k0
                total = total + tri_back[rows, j : j + 1, :] * right_act[start : start + k_step, :][None]
            total = total.astype(bf16)
            for s in range(k0 // k_left, (k0 + k_step) // k_left):
                left_out[s][rows] = total[:, s * k_left - k0 : (s + 1) * k_left - k0]
            return 0

        lax.fori_loop(0, n_i // few, rows_sum, 0)


def right_back_kernel(n_rows, n_blk, tri_back, *refs):
    left_act, refs = refs[:n_blk], refs[n_blk + 1 :]
    right_out, (right_sum,) = refs[:n_rows], refs[n_rows:]
    n_i, n_j, width = tri_back.shape
    k_left = left_act[0].shape[1]
    n_k = k_left * n_blk
    k_right = right_out[0].shape[1]
    unit = math.gcd(k_left, k_right)
    few = 4
    k_step = vertex_step(n_k, k_left)
    for k0 in range(0, n_k, k_step):
        blocks = range(k0 // k_left, (k0 + k_step) // k_left)

        def rows_sum(at, _, k0=k0, blocks=blocks):
            eight = pl.ds(pl.multiple_of(at * 8, 8), 8)
            for half in range(0, 8, few):

                def add(i, totals):
                    some = tri_back[i, eight, :][half : half + few][:, None]
                    return tuple(
                        total + some * left_act[s][i][None] for s, total in zip(blocks, totals)
                    )

                zeros = tuple(jnp.zeros((few, k_left, width), f32) for _ in blocks)
                totals = lax.fori_loop(0, n_i, add, zeros, unroll=16)
                for s, total in zip(blocks, totals):
                    right_sum[pl.ds(at * 8 + half, few), s * k_left : (s + 1) * k_left, :] = total.astype(bf16)
            return 0

        lax.fori_loop(0, n_j // 8, rows_sum, 0)
    for s in range(n_rows):
        for part in range(k_right // unit):
            right_out[s][:, part * unit : (part + 1) * unit, :] = right_sum[
                :, pl.ds(place(n_rows, n_blk, k_left, k_right, s, part), unit), :
            ]


def weights_kernel(n_rows, n_blk, right_in, left_w, right_w, gate_part, output_part, *refs):
    left_in, refs = refs[:n_blk], refs[n_blk:]
    left_out, refs = refs[:n_blk], refs[n_blk:]
    right_out, refs = refs[:n_rows], refs[n_rows:]
    pieces, (total,) = refs[:n_rows], refs[n_rows:]
    right_ins = [right_in.at[s] for s in range(n_rows)]
    width = gate_part.shape[0]
    total[:, 4 * width : 5 * width] = gate_part[...]
    total[:, 5 * width :] = output_part[...]
    for inputs_refs, weight, backs, first in (
        (left_in, left_w, left_out, 0),
        (right_ins, right_w, right_out, 2 * width),
    ):
        columns = slice(first, first + 2 * width)
        total[:, columns] = jnp.zeros((width, 2 * width), f32)
        n, k, _ = inputs_refs[0].shape
        step = 16
        flat = step * k
        for inputs_ref, back_ref in zip(inputs_refs, backs):

            def body(at, _, inputs_ref=inputs_ref, back_ref=back_ref, weight=weight, columns=columns, flat=flat):
                rows = pl.ds(at * step, step)
                inputs = inputs_ref[rows].reshape(flat, width)
                lin, sw = gated(inputs, weight[...])
                back = back_ref[rows].reshape(flat, width).astype(f32)
                total[:, columns] += dot_tn(inputs, joined_grad(back, lin, sw))
                return 0

            lax.fori_loop(0, n // step, body, 0, unroll=2)
    size = width // n_rows
    for s, piece in enumerate(pieces):
        start = pl.multiple_of(lax.rem(lax.axis_index("rows") + s, n_rows) * size, size)
        piece[...] = total[pl.ds(start, size), :].astype(bf16)


def grad_middle_kernel(middle, pre_back, gate_weight, grad_middle):
    n_i, n_j, width = middle.shape
    step = 8

    def body(at, _):
        rows = pl.ds(at * step, step)
        flat = step * n_j
        normed, inverse = normalize(middle[rows].astype(f32).reshape(flat, width))
        up = dot_nt(pre_back[rows].reshape(flat, width), gate_weight[...])
        grad_middle[rows] = normalize_back(normed, inverse, up).astype(bf16).reshape(step, n_j, width)
        return 0

    lax.fori_loop(0, n_i // step, body, 0, unroll=2)


def side_kernel(n_left, n_right, *refs):
    left, right, left_w, right_w = refs[:4]
    left_back, refs = refs[4 : 4 + n_left], refs[4 + n_left :]
    right_back, refs = refs[:n_right], refs[n_right:]
    for raw, weight, backs, grad in (
        (left, left_w, left_back, refs[0]),
        (right, right_w, right_back, refs[1]),
    ):
        n, k, width = raw.shape
        step = 16
        flat = step * k

        def body(at, _, raw=raw, weight=weight, backs=backs, grad=grad, step=step, flat=flat, k=k, width=width):
            rows = pl.ds(at * step, step)
            normed, inverse = normalize(raw[rows].astype(f32).reshape(flat, width))
            lin, sw = gated(normed.astype(bf16), weight[...])
            back = backs[0][rows].astype(f32)
            for other in backs[1:]:
                back = back + other[rows].astype(f32)
            up = dot_nt(joined_grad(back.reshape(flat, width), lin, sw), weight[...])
            grad[rows] = normalize_back(normed, inverse, up).astype(bf16).reshape(step, k, width)
            return 0

        lax.fori_loop(0, n // step, body, 0, unroll=2)


def shift(x, axis, n, step):
    return lax.ppermute(x, axis, [(a, (a + step) % n) for a in range(n)])


def combine_kernel(n, *refs):
    total = refs[0][...].astype(f32)
    for other in refs[1:n]:
        total = total + other[...].astype(f32)
    refs[-1][...] = total.astype(bf16)


def combine(pieces, after=()):
    (total,) = call(
        functools.partial(combine_kernel, len(pieces)),
        "combine",
        [shape(pieces[0].shape, bf16)],
        after=len(after),
    )(*pieces, *after)
    return total


def deltas_kernel(n_rows, *refs):
    pieces, outs = refs[:n_rows], refs[n_rows:]
    size = pieces[0].shape[0]
    for s, piece in enumerate(pieces):
        start = pl.multiple_of(lax.rem(lax.axis_index("rows") - s + n_rows, n_rows) * size, size)
        first = 0
        for out in outs:
            last = first + out.shape[1]
            out[pl.ds(start, size), :] = piece[:, first:last].astype(f32)
            first = last


def shape(dims, kind):
    return jax.ShapeDtypeStruct(tuple(dims), kind)


def call(kernel, name, outs, scratch=(), after=0):
    def run(*operands):
        spaces = [pltpu.VMEM] * (len(operands) - after) + [pl.ANY] * after
        held = sum(math.prod(x.shape) * 4 for x in scratch)
        return pl.pallas_call(
            kernel,
            in_specs=[pl.BlockSpec(memory_space=space) for space in spaces],
            out_specs=[pl.BlockSpec(memory_space=pltpu.VMEM)] * len(outs),
            out_shape=outs,
            scratch_shapes=list(scratch),
            compiler_params=pltpu.CompilerParams(vmem_limit_bytes=held + SCOPED),
            cost_estimate=pl.CostEstimate(flops=1000, bytes_accessed=1000, transcendentals=0),
            name=name,
        )(*operands)

    return run


def per_device(
    n_rows,
    n_blk,
    pair_left,
    pair_right,
    pair_middle,
    cotangent,
    left_weight,
    right_weight,
    gate_weight,
    output_weight,
):
    n_i, k_left, width = pair_left.shape
    n_j, k_right, _ = pair_right.shape
    n_k = k_left * n_blk
    left_raw = [pair_left] + [shift(pair_left, "blk", n_blk, s) for s in range(1, n_blk)]
    right_raw = [pair_right] + [shift(pair_right, "rows", n_rows, s) for s in range(1, n_rows)]
    middle_shape = (n_i, n_j, width)
    gate, middle_in, head_back, tri_up = call(
        middle_kernel,
        "middle",
        [shape(middle_shape, f32), shape(middle_shape, bf16), shape(middle_shape, bf16), shape(middle_shape, f32)],
        scratch=[
            *(pltpu.VMEM(x.shape, bf16) for x in (pair_middle, cotangent, gate_weight, output_weight)),
            pltpu.SemaphoreType.DMA((4,)),
        ],
        after=4,
    )(pair_middle, cotangent, gate_weight, output_weight)
    right_act, right_in, *right_flip = call(
        functools.partial(right_kernel, n_rows, n_blk, k_left),
        "right",
        [shape((n_j * n_k, width), f32), shape((n_rows, n_j, k_right, width), bf16)]
        + [shape((k_left, n_j, width), f32)] * n_blk,
    )(*right_raw, right_weight)
    left_act, left_in, total = [], [], []
    act_shape = shape(pair_left.shape, f32)
    in_shape = shape(pair_left.shape, bf16)
    for s in range(n_blk - 1):
        act, inputs, total = call(
            functools.partial(left_kernel, s == 0),
            "left",
            [act_shape, in_shape, shape(middle_shape, f32)],
        )(left_raw[s], left_weight, right_flip[s], *total)
        left_act.append(act)
        left_in.append(inputs)
        total = [total]
    act, inputs, update, pre_back, tri_back, gate_part, output_part = call(
        functools.partial(triangle_kernel, n_blk > 1),
        "triangle",
        [
            act_shape,
            in_shape,
            shape(middle_shape, bf16),
            shape(middle_shape, bf16),
            shape(middle_shape, f32),
            shape(gate_weight.shape, f32),
            shape(output_weight.shape, f32),
        ],
    )(
        left_raw[-1],
        left_weight,
        right_flip[-1],
        output_weight,
        gate,
        middle_in,
        head_back,
        tri_up,
        cotangent,
        *total,
    )
    left_act.append(act)
    left_in.append(inputs)
    left_out = call(left_back_kernel, "left_back", [shape(pair_left.shape, bf16)] * n_blk)(
        tri_back, right_act
    )
    left_back = [left_out[0]] + [shift(left_out[s], "blk", n_blk, n_blk - s) for s in range(1, n_blk)]
    right_out = call(
        functools.partial(right_back_kernel, n_rows, n_blk),
        "right_back",
        [shape(pair_right.shape, bf16)] * n_rows,
        scratch=[pltpu.VMEM((n_j, n_k, width), bf16)],
        after=1,
    )(tri_back, *left_act, left_out[0])
    right_back = [right_out[0]] + [
        shift(right_out[s], "rows", n_rows, n_rows - s) for s in range(1, n_rows)
    ]
    pieces = call(
        functools.partial(weights_kernel, n_rows, n_blk),
        "weights",
        [shape((width // n_rows, 6 * width), bf16)] * n_rows,
        scratch=[pltpu.VMEM((width, 6 * width), f32)],
    )(right_in, left_weight, right_weight, gate_part, output_part, *left_in, *left_out, *right_out)
    pieces = [pieces[0]] + [shift(pieces[s], "rows", n_rows, s) for s in range(1, n_rows)]
    part = combine(pieces, (*left_back[1:], *right_back[1:]))
    part = combine([part] + [shift(part, "blk", n_blk, s) for s in range(1, n_blk)])
    pieces = [part] + [shift(part, "rows", n_rows, s) for s in range(1, n_rows)]
    deltas = call(
        functools.partial(deltas_kernel, n_rows),
        "deltas",
        [shape(x.shape, f32) for x in (left_weight, right_weight, gate_weight, output_weight)],
    )(*pieces)
    (grad_middle,) = call(grad_middle_kernel, "grad_middle", [shape(middle_shape, bf16)])(
        pair_middle, pre_back, gate_weight
    )
    grad_left, grad_right = call(
        functools.partial(side_kernel, n_blk, n_rows),
        "sides",
        [shape(pair_left.shape, bf16), shape(pair_right.shape, bf16)],
    )(pair_left, pair_right, left_weight, right_weight, *left_back, *right_back)
    return (
        update,
        grad_left,
        grad_right,
        grad_middle,
        *deltas,
    )


def solution(mesh):
    sides = P(("rep", "rows"), "blk", None)
    right = P(("rep", "blk"), "rows", None)
    return jax.shard_map(
        functools.partial(per_device, mesh.shape["rows"], mesh.shape["blk"]),
        mesh=mesh,
        in_specs=(sides, right, sides, sides, P(), P(), P(), P()),
        out_specs=(sides, sides, right, sides) + (P("rep", None),) * 4,
        check_vma=False,
    )
```

```python
import functools
import math

import jax
import jax.numpy as jnp
from jax import lax
from jax.experimental import pallas as pl
from jax.experimental.pallas import tpu as pltpu
from jax.sharding import PartitionSpec as P

epsilon = 1e-05
f32 = jnp.float32
bf16 = jnp.bfloat16
SCOPED = 6 * 1024 * 1024


def normalize(values):
    centred = values - jnp.mean(values, axis=-1, keepdims=True)
    inverse = lax.rsqrt(jnp.mean(centred * centred, axis=-1, keepdims=True) + epsilon)
    return (centred * inverse, inverse)


def normalize_back(normed, inverse, upstream):
    first = jnp.mean(upstream, axis=-1, keepdims=True)
    second = jnp.mean(upstream * normed, axis=-1, keepdims=True)
    return inverse * (upstream - first - normed * second)


def sigmoid(x):
    return 0.5 * jnp.tanh(0.5 * x) + 0.5


def dot(a, b):
    return lax.dot_general(a, b, (((1,), (0,)), ((), ())), preferred_element_type=f32)


def dot_nt(a, b):
    return lax.dot_general(a, b, (((1,), (1,)), ((), ())), preferred_element_type=f32)


def dot_tn(a, b):
    return lax.dot_general(a, b, (((0,), (0,)), ((), ())), preferred_element_type=f32)


def gated(inputs, weight):
    pre = dot(inputs, weight)
    width = weight.shape[1] // 2
    return pre[:, :width], sigmoid(pre[:, width:])


def joined_grad(back, lin, sw):
    return jnp.concatenate([back * sw, back * lin * sw * (1.0 - sw)], axis=-1).astype(bf16)


def middle_kernel(*refs):
    sources, refs = refs[:4], refs[4:]
    gate, middle_in, head_back, tri_up, middle, cotangent, gate_weight, output_weight, arrived = refs
    n_i, n_j, width = middle.shape
    step = 8
    copies = [
        pltpu.make_async_copy(source, target, arrived.at[at])
        for at, (source, target) in enumerate(zip(sources, (middle, cotangent, gate_weight, output_weight)))
    ]
    for copy in copies:
        copy.start()
    for copy in copies:
        copy.wait()

    def body(at, _):
        rows = pl.ds(at * step, step)
        normed, _ = normalize(middle[rows].astype(f32).reshape(step * n_j, width))
        inputs = normed.astype(bf16)
        opened = sigmoid(dot(inputs, gate_weight[...]))
        back = (cotangent[rows].astype(f32).reshape(step * n_j, width) * opened).astype(bf16)
        gate[rows] = opened.reshape(step, n_j, width)
        middle_in[rows] = inputs.reshape(step, n_j, width)
        head_back[rows] = back.reshape(step, n_j, width)
        tri_up[rows] = dot_nt(back, output_weight[...]).reshape(step, n_j, width)
        return 0

    lax.fori_loop(0, n_i // step, body, 0, unroll=2)


def right_kernel(n_rows, n_blk, k_left, *refs):
    raw, (weight, act_out, in_out, *flip_out) = refs[:n_rows], refs[n_rows:]
    n_j, k_right, width = raw[0].shape
    n_k = k_left * n_blk
    unit = math.gcd(k_left, k_right)
    step = 16
    for s in range(n_rows):

        def body(at, _, s=s):
            rows = pl.ds(at * step, step)
            normed, _ = normalize(raw[s][rows].astype(f32).reshape(step * k_right, width))
            inputs = normed.astype(bf16)
            in_out[s, rows] = inputs.reshape(step, k_right, width)
            lin, sw = gated(inputs, weight[...])
            act = (sw * lin).astype(bf16).astype(f32).reshape(step, k_right, width)
            for part in range(k_right // unit):
                at_k = place(n_blk, k_left, k_right, s, part)
                for j in range(step):
                    start = pl.multiple_of((at * step + j) * n_k + at_k, unit)
                    act_out[pl.ds(start, unit), :] = act[j, part * unit : (part + 1) * unit]
            return 0

        lax.fori_loop(0, n_j // step, body, 0)

    for s in range(n_blk):

        def flip(k, _, s=s):
            flip_out[s][k] = act_out[pl.ds(s * k_left + k, n_j, stride=n_k), :]
            return 0

        lax.fori_loop(0, k_left, flip, 0, unroll=True)


def place(n_blk, k_left, k_right, piece, part):
    unit = math.gcd(k_left, k_right)
    vertex = lax.bitwise_xor(lax.axis_index("rows"), piece) * k_right + part * unit
    block = vertex // k_left
    at = lax.rem(lax.axis_index("blk") - block + n_blk, n_blk) * k_left + vertex - block * k_left
    return pl.multiple_of(at, unit)


def project_left(raw, weight, act_out, in_out):
    n_i, k_left, width = raw.shape
    step = 8

    def body(at, _):
        rows = pl.ds(at * step, step)
        normed, _ = normalize(raw[rows].astype(f32).reshape(step * k_left, width))
        inputs = normed.astype(bf16)
        in_out[rows] = inputs.reshape(step, k_left, width)
        lin, sw = gated(inputs, weight[...])
        act_out[rows] = (sw * lin).astype(bf16).astype(f32).reshape(step, k_left, width)
        return 0

    lax.fori_loop(0, n_i // step, body, 0, unroll=2)


def add_vertices(rows, act, flip):
    total = act[rows, 0:1, :] * flip[0][None]
    for k in range(1, act.shape[1]):
        total = total + act[rows, k : k + 1, :] * flip[k][None]
    return total


def left_kernel(first, raw, weight, flip, *refs):
    total_in, (act_out, in_out, total_out) = refs[: 0 if first else 1], refs[0 if first else 1 :]
    n_i, n_j, width = total_out.shape
    step = 8
    project_left(raw, weight, act_out, in_out)

    def body(at, _):
        rows = pl.ds(at * step, step)
        total = add_vertices(rows, act_out, flip)
        total_out[rows] = total if first else total_in[0][rows] + total
        return 0

    lax.fori_loop(0, n_i // step, body, 0)


def triangle_kernel(
    has_total, raw, left_w, flip, out_w, gate, middle_in, head_back, tri_up, cotangent, *refs
):
    total_in, refs = refs[: 1 if has_total else 0], refs[1 if has_total else 0 :]
    act_out, in_out, update, pre_back, tri_back, gate_part, output_part = refs
    n_i, n_j, width = update.shape
    step = 8
    project_left(raw, left_w, act_out, in_out)
    gate_part[...] = jnp.zeros_like(gate_part)
    output_part[...] = jnp.zeros_like(output_part)

    def triangle_rows(at, _):
        rows = pl.ds(at * step, step)
        total = add_vertices(rows, act_out, flip)
        if has_total:
            total = total + total_in[0][rows]
        flat = step * n_j
        normed, inverse = normalize(total.reshape(flat, width))
        tri_in = normed.astype(bf16)
        head = dot(tri_in, out_w[...])
        opened = gate[rows].reshape(flat, width)
        update[rows] = (opened * head).astype(bf16).reshape(step, n_j, width)
        upstream = cotangent[rows].astype(f32).reshape(flat, width)
        pre = (upstream * head * opened * (1.0 - opened)).astype(bf16)
        pre_back[rows] = pre.reshape(step, n_j, width)
        gate_part[...] += dot_tn(middle_in[rows].reshape(flat, width), pre)
        output_part[...] += dot_tn(tri_in, head_back[rows].reshape(flat, width))
        back = normalize_back(normed, inverse, tri_up[rows].reshape(flat, width))
        tri_back[rows] = back.astype(bf16).astype(f32).reshape(step, n_j, width)
        return 0

    lax.fori_loop(0, n_i // step, triangle_rows, 0, unroll=2)


def vertex_step(n_k, unit):
    size = unit
    while size * 2 <= 64 and n_k % (size * 2) == 0:
        size *= 2
    return size


def left_back_kernel(tri_back, right_act, *left_out):
    n_i, n_j, width = tri_back.shape
    k_left = left_out[0].shape[1]
    n_k = k_left * len(left_out)
    few = 4
    k_step = vertex_step(n_k, k_left)
    for k0 in range(0, n_k, k_step):

        def rows_sum(at, _, k0=k0):
            rows = pl.ds(at * few, few)
            total = jnp.zeros((few, k_step, width), f32)
            for j in range(n_j):
                start = j * n_k + k0
                total = total + tri_back[rows, j : j + 1, :] * right_act[start : start + k_step, :][None]
            total = total.astype(bf16)
            for s in range(k0 // k_left, (k0 + k_step) // k_left):
                left_out[s][rows] = total[:, s * k_left - k0 : (s + 1) * k_left - k0]
            return 0

        lax.fori_loop(0, n_i // few, rows_sum, 0)


def right_back_kernel(n_rows, n_blk, tri_back, *refs):
    left_act, refs = refs[:n_blk], refs[n_blk + 1 :]
    keep, send, right_sum = refs
    n_i, n_j, width = tri_back.shape
    k_left = left_act[0].shape[1]
    n_k = k_left * n_blk
    k_right = keep.shape[2]
    unit = math.gcd(k_left, k_right)
    few = 4
    k_step = vertex_step(n_k, k_left)
    for k0 in range(0, n_k, k_step):
        blocks = range(k0 // k_left, (k0 + k_step) // k_left)

        def rows_sum(at, _, k0=k0, blocks=blocks):
            eight = pl.ds(pl.multiple_of(at * 8, 8), 8)
            for half in range(0, 8, few):

                def add(i, totals):
                    some = tri_back[i, eight, :][half : half + few][:, None]
                    return tuple(
                        total + some * left_act[s][i][None] for s, total in zip(blocks, totals)
                    )

                zeros = tuple(jnp.zeros((few, k_left, width), f32) for _ in blocks)
                totals = lax.fori_loop(0, n_i, add, zeros, unroll=16)
                for s, total in zip(blocks, totals):
                    right_sum[pl.ds(at * 8 + half, few), s * k_left : (s + 1) * k_left, :] = total.astype(bf16)
            return 0

        lax.fori_loop(0, n_j // 8, rows_sum, 0)
    for s in range(n_rows):
        for part in range(k_right // unit):
            out = send if s % 2 else keep
            out[s // 2, :, part * unit : (part + 1) * unit, :] = right_sum[
                :, pl.ds(place(n_blk, k_left, k_right, s, part), unit), :
            ]


def weights_kernel(n_rows, n_blk, right_in, left_w, right_w, gate_part, output_part, *refs):
    left_in, refs = refs[:n_blk], refs[n_blk:]
    left_out, refs = refs[:n_blk], refs[n_blk:]
    keep, send, parts, total = refs
    right_out = [(send if s % 2 else keep).at[s // 2] for s in range(n_rows)]
    right_ins = [right_in.at[s] for s in range(n_rows)]
    width = gate_part.shape[0]
    total[:, 4 * width : 5 * width] = gate_part[...]
    total[:, 5 * width :] = output_part[...]
    for inputs_refs, weight, backs, first in (
        (left_in, left_w, left_out, 0),
        (right_ins, right_w, right_out, 2 * width),
    ):
        columns = slice(first, first + 2 * width)
        total[:, columns] = jnp.zeros((width, 2 * width), f32)
        n, k, _ = inputs_refs[0].shape
        step = 16
        flat = step * k
        for inputs_ref, back_ref in zip(inputs_refs, backs):

            def body(at, _, inputs_ref=inputs_ref, back_ref=back_ref, weight=weight, columns=columns, flat=flat):
                rows = pl.ds(at * step, step)
                inputs = inputs_ref[rows].reshape(flat, width)
                lin, sw = gated(inputs, weight[...])
                back = back_ref[rows].reshape(flat, width).astype(f32)
                total[:, columns] += dot_tn(inputs, joined_grad(back, lin, sw))
                return 0

            lax.fori_loop(0, n // step, body, 0, unroll=2)
    parts[...] = total[...].astype(bf16)


def grad_middle_kernel(middle, pre_back, gate_weight, grad_middle):
    n_i, n_j, width = middle.shape
    step = 8

    def body(at, _):
        rows = pl.ds(at * step, step)
        flat = step * n_j
        normed, inverse = normalize(middle[rows].astype(f32).reshape(flat, width))
        up = dot_nt(pre_back[rows].reshape(flat, width), gate_weight[...])
        grad_middle[rows] = normalize_back(normed, inverse, up).astype(bf16).reshape(step, n_j, width)
        return 0

    lax.fori_loop(0, n_i // step, body, 0, unroll=2)


def side_kernel(n_left, *refs):
    left, right, left_w, right_w = refs[:4]
    left_back, refs = refs[4 : 4 + n_left], refs[4 + n_left :]
    right_back, refs = [ref.at[0] for ref in refs[:2]], refs[2:]
    for raw, weight, backs, grad in (
        (left, left_w, left_back, refs[0]),
        (right, right_w, right_back, refs[1]),
    ):
        n, k, width = raw.shape
        step = 16
        flat = step * k

        def body(at, _, raw=raw, weight=weight, backs=backs, grad=grad, step=step, flat=flat, k=k, width=width):
            rows = pl.ds(at * step, step)
            normed, inverse = normalize(raw[rows].astype(f32).reshape(flat, width))
            lin, sw = gated(normed.astype(bf16), weight[...])
            back = backs[0][rows].astype(f32)
            for other in backs[1:]:
                back = back + other[rows].astype(f32)
            up = dot_nt(joined_grad(back.reshape(flat, width), lin, sw), weight[...])
            grad[rows] = normalize_back(normed, inverse, up).astype(bf16).reshape(step, k, width)
            return 0

        lax.fori_loop(0, n // step, body, 0, unroll=2)


def shift(x, axis, n, step):
    return lax.ppermute(x, axis, [(a, (a + step) % n) for a in range(n)])


def exchange(x, axis, n, bit):
    return lax.ppermute(x, axis, [(a, a ^ bit) for a in range(n)])


def halve_kernel(keep, came, *refs):
    kept, send = refs[-2:]
    for at in range(keep.shape[0]):
        total = keep[at].astype(f32) + came[at].astype(f32)
        if at % 2:
            send[at // 2] = total.astype(bf16)
        else:
            kept[at // 2] = total


def halving_sum(keep, send, axis, n, after):
    came = exchange(send, axis, n, 1)
    bit = 2
    while bit < n:
        half = (keep.shape[0] // 2,) + keep.shape[1:]
        keep, send = call(halve_kernel, "halve", [shape(half, f32), shape(half, bf16)], after=len(after))(
            keep, came, *after
        )
        came = exchange(send, axis, n, bit)
        bit *= 2
    return keep, came, send


def order_kernel(*refs):
    refs[-1][...] = jnp.zeros_like(refs[-1])


def behind(*arrays):
    (mark,) = call(order_kernel, "order", [shape((8, 128), f32)], after=len(arrays), cost=2 * 10**10)(*arrays)
    return mark


def combine_kernel(n, *refs):
    total = refs[0][0].astype(f32)
    for at in range(1, refs[0].shape[0]):
        total = total + refs[0][at].astype(f32)
    for other in refs[1:n]:
        total = total + other[0].astype(f32)
    refs[-1][0] = total.astype(bf16)


def combine(pieces, after=()):
    (total,) = call(
        functools.partial(combine_kernel, len(pieces)),
        "combine",
        [shape((1,) + pieces[0].shape[1:], bf16)],
        after=len(after),
    )(*pieces, *after)
    return total


def deltas_kernel(n_rows, *refs):
    pieces, outs = [ref.at[0] for ref in refs[:n_rows]], refs[n_rows:]
    size = pieces[0].shape[0]
    for s, piece in enumerate(pieces):
        start = pl.multiple_of(lax.bitwise_xor(lax.axis_index("rows"), s) * size, size)
        first = 0
        for out in outs:
            last = first + out.shape[1]
            out[pl.ds(start, size), :] = piece[:, first:last].astype(f32)
            first = last


def shape(dims, kind):
    return jax.ShapeDtypeStruct(tuple(dims), kind)


def call(kernel, name, outs, scratch=(), after=0, cost=1000):
    def run(*operands):
        spaces = [pltpu.VMEM] * (len(operands) - after) + [pl.ANY] * after
        held = sum(math.prod(x.shape) * 4 for x in scratch)
        return pl.pallas_call(
            kernel,
            in_specs=[pl.BlockSpec(memory_space=space) for space in spaces],
            out_specs=[pl.BlockSpec(memory_space=pltpu.VMEM)] * len(outs),
            out_shape=outs,
            scratch_shapes=list(scratch),
            compiler_params=pltpu.CompilerParams(vmem_limit_bytes=held + SCOPED),
            cost_estimate=pl.CostEstimate(flops=cost, bytes_accessed=1000, transcendentals=0),
            name=name,
        )(*operands)

    return run


def per_device(
    n_rows,
    n_blk,
    pair_left,
    pair_right,
    pair_middle,
    cotangent,
    left_weight,
    right_weight,
    gate_weight,
    output_weight,
):
    n_i, k_left, width = pair_left.shape
    n_j, k_right, _ = pair_right.shape
    n_k = k_left * n_blk
    left_raw = [pair_left] + [shift(pair_left, "blk", n_blk, s) for s in range(1, n_blk)]
    right_raw = [pair_right] + [exchange(pair_right, "rows", n_rows, s) for s in range(1, n_rows)]
    middle_shape = (n_i, n_j, width)
    gate, middle_in, head_back, tri_up = call(
        middle_kernel,
        "middle",
        [shape(middle_shape, f32), shape(middle_shape, bf16), shape(middle_shape, bf16), shape(middle_shape, f32)],
        scratch=[
            *(pltpu.VMEM(x.shape, bf16) for x in (pair_middle, cotangent, gate_weight, output_weight)),
            pltpu.SemaphoreType.DMA((4,)),
        ],
        after=4,
    )(pair_middle, cotangent, gate_weight, output_weight)
    right_act, right_in, *right_flip = call(
        functools.partial(right_kernel, n_rows, n_blk, k_left),
        "right",
        [shape((n_j * n_k, width), f32), shape((n_rows, n_j, k_right, width), bf16)]
        + [shape((k_left, n_j, width), f32)] * n_blk,
    )(*right_raw, right_weight)
    left_act, left_in, total = [], [], []
    act_shape = shape(pair_left.shape, f32)
    in_shape = shape(pair_left.shape, bf16)
    for s in range(n_blk - 1):
        act, inputs, total = call(
            functools.partial(left_kernel, s == 0),
            "left",
            [act_shape, in_shape, shape(middle_shape, f32)],
        )(left_raw[s], left_weight, right_flip[s], *total)
        left_act.append(act)
        left_in.append(inputs)
        total = [total]
    act, inputs, update, pre_back, tri_back, gate_part, output_part = call(
        functools.partial(triangle_kernel, n_blk > 1),
        "triangle",
        [
            act_shape,
            in_shape,
            shape(middle_shape, bf16),
            shape(middle_shape, bf16),
            shape(middle_shape, f32),
            shape(gate_weight.shape, f32),
            shape(output_weight.shape, f32),
        ],
    )(
        left_raw[-1],
        left_weight,
        right_flip[-1],
        output_weight,
        gate,
        middle_in,
        head_back,
        tri_up,
        cotangent,
        *total,
    )
    left_act.append(act)
    left_in.append(inputs)
    left_out = call(left_back_kernel, "left_back", [shape(pair_left.shape, bf16)] * n_blk)(
        tri_back, right_act
    )
    left_back = [left_out[0]] + [shift(left_out[s], "blk", n_blk, n_blk - s) for s in range(1, n_blk)]
    right_stack = shape((n_rows // 2,) + pair_right.shape, bf16)
    keep, send = call(
        functools.partial(right_back_kernel, n_rows, n_blk),
        "right_back",
        [right_stack, right_stack],
        scratch=[pltpu.VMEM((n_j, n_k, width), bf16)],
        after=1,
    )(tri_back, *left_act, left_out[0])
    kept, came, sent = halving_sum(keep, send, "rows", n_rows, (behind(*left_back[1:]),))
    (parts,) = call(
        functools.partial(weights_kernel, n_rows, n_blk),
        "weights",
        [shape((width, 6 * width), bf16)],
        scratch=[pltpu.VMEM((width, 6 * width), f32)],
    )(right_in, left_weight, right_weight, gate_part, output_part, *left_in, *left_out, keep, send)
    parts = lax.all_to_all(parts.reshape(n_rows, width // n_rows, 6 * width), "rows", 0, 0)
    part = combine([parts], (behind(sent),))
    part = combine([part] + [shift(part, "blk", n_blk, s) for s in range(1, n_blk)])
    pieces = [part] + [exchange(part, "rows", n_rows, s) for s in range(1, n_rows)]
    deltas = call(
        functools.partial(deltas_kernel, n_rows),
        "deltas",
        [shape(x.shape, f32) for x in (left_weight, right_weight, gate_weight, output_weight)],
    )(*pieces)
    (grad_middle,) = call(grad_middle_kernel, "grad_middle", [shape(middle_shape, bf16)])(
        pair_middle, pre_back, gate_weight
    )
    grad_left, grad_right = call(
        functools.partial(side_kernel, n_blk),
        "sides",
        [shape(pair_left.shape, bf16), shape(pair_right.shape, bf16)],
    )(pair_left, pair_right, left_weight, right_weight, *left_back, kept, came)
    return (
        update,
        grad_left,
        grad_right,
        grad_middle,
        *deltas,
    )


def solution(mesh):
    sides = P(("rep", "rows"), "blk", None)
    right = P(("rep", "blk"), "rows", None)
    return jax.shard_map(
        functools.partial(per_device, mesh.shape["rows"], mesh.shape["blk"]),
        mesh=mesh,
        in_specs=(sides, right, sides, sides, P(), P(), P(), P()),
        out_specs=(sides, sides, right, sides) + (P("rep", None),) * 4,
        check_vma=False,
    )
```

```python
import functools
import math

import jax
import jax.numpy as jnp
from jax import lax
from jax.experimental import pallas as pl
from jax.experimental.pallas import tpu as pltpu
from jax.sharding import PartitionSpec as P

epsilon = 1e-05
f32 = jnp.float32
bf16 = jnp.bfloat16
SCOPED = 6 * 1024 * 1024


def normalize(values):
    centred = values - jnp.mean(values, axis=-1, keepdims=True)
    inverse = lax.rsqrt(jnp.mean(centred * centred, axis=-1, keepdims=True) + epsilon)
    return (centred * inverse, inverse)


def normalize_back(normed, inverse, upstream):
    first = jnp.mean(upstream, axis=-1, keepdims=True)
    second = jnp.mean(upstream * normed, axis=-1, keepdims=True)
    return inverse * (upstream - first - normed * second)


def sigmoid(x):
    return 0.5 * jnp.tanh(0.5 * x) + 0.5


def dot(a, b):
    return lax.dot_general(a, b, (((1,), (0,)), ((), ())), preferred_element_type=f32)


def dot_nt(a, b):
    return lax.dot_general(a, b, (((1,), (1,)), ((), ())), preferred_element_type=f32)


def dot_tn(a, b):
    return lax.dot_general(a, b, (((0,), (0,)), ((), ())), preferred_element_type=f32)


def gated(inputs, weight):
    pre = dot(inputs, weight)
    width = weight.shape[1] // 2
    return pre[:, :width], sigmoid(pre[:, width:])


def joined_grad(back, lin, sw):
    return jnp.concatenate([back * sw, back * lin * sw * (1.0 - sw)], axis=-1).astype(bf16)


def middle_kernel(*refs):
    sources, refs = refs[:4], refs[4:]
    gate, middle_in, head_back, tri_up, middle, cotangent, gate_weight, output_weight, arrived = refs
    n_i, n_j, width = middle.shape
    step = 8
    copies = [
        pltpu.make_async_copy(source, target, arrived.at[at])
        for at, (source, target) in enumerate(zip(sources, (middle, cotangent, gate_weight, output_weight)))
    ]
    for copy in copies:
        copy.start()
    for copy in copies:
        copy.wait()

    def body(at, _):
        rows = pl.ds(at * step, step)
        normed, _ = normalize(middle[rows].astype(f32).reshape(step * n_j, width))
        inputs = normed.astype(bf16)
        opened = sigmoid(dot(inputs, gate_weight[...]))
        back = (cotangent[rows].astype(f32).reshape(step * n_j, width) * opened).astype(bf16)
        gate[rows] = opened.reshape(step, n_j, width)
        middle_in[rows] = inputs.reshape(step, n_j, width)
        head_back[rows] = back.reshape(step, n_j, width)
        up = dot_nt(back, output_weight[...])
        tri_up[rows] = (up - jnp.mean(up, axis=-1, keepdims=True)).reshape(step, n_j, width)
        return 0

    lax.fori_loop(0, n_i // step, body, 0, unroll=2)


def right_kernel(n_rows, n_blk, k_left, *refs):
    raw, (weight, act_out, in_out, *flip_out) = refs[:n_rows], refs[n_rows:]
    n_j, k_right, width = raw[0].shape
    n_k = k_left * n_blk
    unit = math.gcd(k_left, k_right)
    step = 16
    for s in range(n_rows):

        def body(at, _, s=s):
            rows = pl.ds(at * step, step)
            normed, _ = normalize(raw[s][rows].astype(f32).reshape(step * k_right, width))
            inputs = normed.astype(bf16)
            in_out[s, rows] = inputs.reshape(step, k_right, width)
            lin, sw = gated(inputs, weight[...])
            act = (sw * lin).astype(bf16).astype(f32).reshape(step, k_right, width)
            for part in range(k_right // unit):
                at_k = place(n_blk, k_left, k_right, s, part)
                for j in range(step):
                    start = pl.multiple_of((at * step + j) * n_k + at_k, unit)
                    act_out[pl.ds(start, unit), :] = act[j, part * unit : (part + 1) * unit]
            return 0

        lax.fori_loop(0, n_j // step, body, 0)

    for s in range(n_blk):

        def flip(k, _, s=s):
            flip_out[s][k] = act_out[pl.ds(s * k_left + k, n_j, stride=n_k), :]
            return 0

        lax.fori_loop(0, k_left, flip, 0, unroll=True)


def place(n_blk, k_left, k_right, piece, part):
    unit = math.gcd(k_left, k_right)
    vertex = lax.bitwise_xor(lax.axis_index("rows"), piece) * k_right + part * unit
    block = vertex // k_left
    at = lax.rem(lax.axis_index("blk") - block + n_blk, n_blk) * k_left + vertex - block * k_left
    return pl.multiple_of(at, unit)


def project_left(raw, weight, act_out, in_out):
    n_i, k_left, width = raw.shape
    step = 8

    def body(at, _):
        rows = pl.ds(at * step, step)
        normed, _ = normalize(raw[rows].astype(f32).reshape(step * k_left, width))
        inputs = normed.astype(bf16)
        in_out[rows] = inputs.reshape(step, k_left, width)
        lin, sw = gated(inputs, weight[...])
        act_out[rows] = (sw * lin).astype(bf16).astype(f32).reshape(step, k_left, width)
        return 0

    lax.fori_loop(0, n_i // step, body, 0, unroll=2)


def add_vertices(rows, act, flip):
    total = act[rows, 0:1, :] * flip[0][None]
    for k in range(1, act.shape[1]):
        total = total + act[rows, k : k + 1, :] * flip[k][None]
    return total


def left_kernel(first, raw, weight, flip, *refs):
    total_in, (act_out, in_out, total_out) = refs[: 0 if first else 1], refs[0 if first else 1 :]
    n_i, n_j, width = total_out.shape
    step = 8
    project_left(raw, weight, act_out, in_out)

    def body(at, _):
        rows = pl.ds(at * step, step)
        total = add_vertices(rows, act_out, flip)
        total_out[rows] = total if first else total_in[0][rows] + total
        return 0

    lax.fori_loop(0, n_i // step, body, 0)


def triangle_kernel(has_total, raw, left_w, flip, tri_up, *refs):
    total_in, refs = refs[: 1 if has_total else 0], refs[1 if has_total else 0 :]
    act_out, in_out, tri_in, tri_back = refs
    n_i, n_j, width = tri_in.shape
    step = 8
    project_left(raw, left_w, act_out, in_out)

    def triangle_rows(at, _):
        rows = pl.ds(at * step, step)
        total = add_vertices(rows, act_out, flip)
        if has_total:
            total = total + total_in[0][rows]
        flat = step * n_j
        normed, inverse = normalize(total.reshape(flat, width))
        tri_in[rows] = normed.astype(bf16).reshape(step, n_j, width)
        up = tri_up[rows].reshape(flat, width)
        second = jnp.mean(up * normed, axis=-1, keepdims=True)
        back = inverse * (up - normed * second)
        tri_back[rows] = back.astype(bf16).astype(f32).reshape(step, n_j, width)
        return 0

    lax.fori_loop(0, n_i // step, triangle_rows, 0, unroll=2)


def heads_kernel(tri_in, out_w, gate, middle_in, head_back, cotangent, _, *refs):
    update, pre_back, gate_part, output_part = refs
    n_i, n_j, width = update.shape
    step = 8
    gate_part[...] = jnp.zeros_like(gate_part)
    output_part[...] = jnp.zeros_like(output_part)

    def body(at, _):
        rows = pl.ds(at * step, step)
        flat = step * n_j
        inputs = tri_in[rows].reshape(flat, width)
        head = dot(inputs, out_w[...])
        opened = gate[rows].reshape(flat, width)
        update[rows] = (opened * head).astype(bf16).reshape(step, n_j, width)
        upstream = cotangent[rows].astype(f32).reshape(flat, width)
        pre = (upstream * head * opened * (1.0 - opened)).astype(bf16)
        pre_back[rows] = pre.reshape(step, n_j, width)
        gate_part[...] += dot_tn(middle_in[rows].reshape(flat, width), pre)
        output_part[...] += dot_tn(inputs, head_back[rows].reshape(flat, width))
        return 0

    lax.fori_loop(0, n_i // step, body, 0, unroll=2)


def vertex_step(n_k, unit):
    size = unit
    while size * 2 <= 64 and n_k % (size * 2) == 0:
        size *= 2
    return size


def left_back_kernel(tri_back, right_act, *left_out):
    n_i, n_j, width = tri_back.shape
    k_left = left_out[0].shape[1]
    n_k = k_left * len(left_out)
    few = 4
    k_step = vertex_step(n_k, k_left)
    for k0 in range(0, n_k, k_step):

        def rows_sum(at, _, k0=k0):
            rows = pl.ds(at * few, few)
            total = jnp.zeros((few, k_step, width), f32)
            for j in range(n_j):
                start = j * n_k + k0
                total = total + tri_back[rows, j : j + 1, :] * right_act[start : start + k_step, :][None]
            total = total.astype(bf16)
            for s in range(k0 // k_left, (k0 + k_step) // k_left):
                left_out[s][rows] = total[:, s * k_left - k0 : (s + 1) * k_left - k0]
            return 0

        lax.fori_loop(0, n_i // few, rows_sum, 0)


def right_back_kernel(n_rows, n_blk, tri_back, *refs):
    left_act, refs = refs[:n_blk], refs[n_blk + 1 :]
    keep, send, right_sum = refs
    n_i, n_j, width = tri_back.shape
    k_left = left_act[0].shape[1]
    n_k = k_left * n_blk
    k_right = keep.shape[2]
    unit = math.gcd(k_left, k_right)
    few = 4
    k_step = vertex_step(n_k, k_left)
    for k0 in range(0, n_k, k_step):
        blocks = range(k0 // k_left, (k0 + k_step) // k_left)

        def rows_sum(at, _, k0=k0, blocks=blocks):
            eight = pl.ds(pl.multiple_of(at * 8, 8), 8)
            for half in range(0, 8, few):

                def add(i, totals):
                    some = tri_back[i, eight, :][half : half + few][:, None]
                    return tuple(
                        total + some * left_act[s][i][None] for s, total in zip(blocks, totals)
                    )

                zeros = tuple(jnp.zeros((few, k_left, width), f32) for _ in blocks)
                totals = lax.fori_loop(0, n_i, add, zeros, unroll=16)
                for s, total in zip(blocks, totals):
                    right_sum[pl.ds(at * 8 + half, few), s * k_left : (s + 1) * k_left, :] = total.astype(bf16)
            return 0

        lax.fori_loop(0, n_j // 8, rows_sum, 0)
    for s in range(n_rows):
        for part in range(k_right // unit):
            out = send if s % 2 else keep
            out[s // 2, :, part * unit : (part + 1) * unit, :] = right_sum[
                :, pl.ds(place(n_blk, k_left, k_right, s, part), unit), :
            ]


def weights_kernel(n_rows, n_blk, right_in, left_w, right_w, gate_part, output_part, *refs):
    left_in, refs = refs[:n_blk], refs[n_blk:]
    left_out, refs = refs[:n_blk], refs[n_blk:]
    keep, send, keep_out, send_out, total = refs
    right_out = [(send if s % 2 else keep).at[s // 2] for s in range(n_rows)]
    right_ins = [right_in.at[s] for s in range(n_rows)]
    width = gate_part.shape[0]
    total[:, 4 * width : 5 * width] = gate_part[...]
    total[:, 5 * width :] = output_part[...]
    for inputs_refs, weight, backs, first in (
        (left_in, left_w, left_out, 0),
        (right_ins, right_w, right_out, 2 * width),
    ):
        columns = slice(first, first + 2 * width)
        total[:, columns] = jnp.zeros((width, 2 * width), f32)
        n, k, _ = inputs_refs[0].shape
        step = 16
        flat = step * k
        for inputs_ref, back_ref in zip(inputs_refs, backs):

            def body(at, _, inputs_ref=inputs_ref, back_ref=back_ref, weight=weight, columns=columns, flat=flat):
                rows = pl.ds(at * step, step)
                inputs = inputs_ref[rows].reshape(flat, width)
                lin, sw = gated(inputs, weight[...])
                back = back_ref[rows].reshape(flat, width).astype(f32)
                total[:, columns] += dot_tn(inputs, joined_grad(back, lin, sw))
                return 0

            lax.fori_loop(0, n // step, body, 0, unroll=2)
    size = width // n_rows
    for s in range(n_rows):
        start = pl.multiple_of(lax.bitwise_xor(lax.axis_index("rows"), s) * size, size)
        piece = total[pl.ds(start, size), :]
        if s % 2:
            send_out[s // 2] = piece.astype(bf16)
        else:
            keep_out[s // 2] = piece


def grad_middle_kernel(middle, pre_back, gate_weight, grad_middle):
    n_i, n_j, width = middle.shape
    step = 8

    def body(at, _):
        rows = pl.ds(at * step, step)
        flat = step * n_j
        normed, inverse = normalize(middle[rows].astype(f32).reshape(flat, width))
        up = dot_nt(pre_back[rows].reshape(flat, width), gate_weight[...])
        grad_middle[rows] = normalize_back(normed, inverse, up).astype(bf16).reshape(step, n_j, width)
        return 0

    lax.fori_loop(0, n_i // step, body, 0, unroll=2)


def side_kernel(n_left, *refs):
    left, right, left_w, right_w = refs[:4]
    left_back, refs = refs[4 : 4 + n_left], refs[4 + n_left :]
    right_back, refs = [ref.at[0] for ref in refs[:2]], refs[2:]
    for raw, weight, backs, grad in (
        (left, left_w, left_back, refs[0]),
        (right, right_w, right_back, refs[1]),
    ):
        n, k, width = raw.shape
        step = 16
        flat = step * k

        def body(at, _, raw=raw, weight=weight, backs=backs, grad=grad, step=step, flat=flat, k=k, width=width):
            rows = pl.ds(at * step, step)
            normed, inverse = normalize(raw[rows].astype(f32).reshape(flat, width))
            lin, sw = gated(normed.astype(bf16), weight[...])
            back = backs[0][rows].astype(f32)
            for other in backs[1:]:
                back = back + other[rows].astype(f32)
            up = dot_nt(joined_grad(back.reshape(flat, width), lin, sw), weight[...])
            grad[rows] = normalize_back(normed, inverse, up).astype(bf16).reshape(step, k, width)
            return 0

        lax.fori_loop(0, n // step, body, 0, unroll=2)


def shift(x, axis, n, step):
    return lax.ppermute(x, axis, [(a, (a + step) % n) for a in range(n)])


def exchange(x, axis, n, bit):
    return lax.ppermute(x, axis, [(a, a ^ bit) for a in range(n)])


def halve_kernel(keep, came, *refs):
    kept, send = refs[-2:]
    for at in range(keep.shape[0]):
        total = keep[at].astype(f32) + came[at].astype(f32)
        if at % 2:
            send[at // 2] = total.astype(bf16)
        else:
            kept[at // 2] = total


def halving_sum(keep, send, axis, n, after):
    came = exchange(send, axis, n, 1)
    bit = 2
    while bit < n:
        half = (keep.shape[0] // 2,) + keep.shape[1:]
        keep, send = call(halve_kernel, "halve", [shape(half, f32), shape(half, bf16)], after=len(after))(
            keep, came, *after
        )
        came = exchange(send, axis, n, bit)
        bit *= 2
    return keep, came, send


def order_kernel(*refs):
    refs[-1][...] = jnp.zeros_like(refs[-1])


def behind(*arrays):
    (mark,) = call(order_kernel, "order", [shape((8, 128), f32)], after=len(arrays), cost=2 * 10**10)(*arrays)
    return mark


def combine_kernel(n, *refs):
    total = refs[0][0].astype(f32)
    for at in range(1, refs[0].shape[0]):
        total = total + refs[0][at].astype(f32)
    for other in refs[1:n]:
        total = total + other[0].astype(f32)
    refs[-1][0] = total.astype(bf16)


def combine(pieces, after=()):
    (total,) = call(
        functools.partial(combine_kernel, len(pieces)),
        "combine",
        [shape((1,) + pieces[0].shape[1:], bf16)],
        after=len(after),
    )(*pieces, *after)
    return total


def deltas_kernel(n_rows, *refs):
    pieces, outs = [ref.at[0] for ref in refs[:n_rows]], refs[n_rows + 1 :]
    size = pieces[0].shape[0]
    for s, piece in enumerate(pieces):
        start = pl.multiple_of(lax.bitwise_xor(lax.axis_index("rows"), s) * size, size)
        first = 0
        for out in outs:
            last = first + out.shape[1]
            out[pl.ds(start, size), :] = piece[:, first:last].astype(f32)
            first = last


def shape(dims, kind):
    return jax.ShapeDtypeStruct(tuple(dims), kind)


def call(kernel, name, outs, scratch=(), after=0, space=pl.ANY, cost=1000):
    def run(*operands):
        spaces = [pltpu.VMEM] * (len(operands) - after) + [space] * after
        held = sum(math.prod(x.shape) * 4 for x in scratch)
        return pl.pallas_call(
            kernel,
            in_specs=[pl.BlockSpec(memory_space=space) for space in spaces],
            out_specs=[pl.BlockSpec(memory_space=pltpu.VMEM)] * len(outs),
            out_shape=outs,
            scratch_shapes=list(scratch),
            compiler_params=pltpu.CompilerParams(vmem_limit_bytes=held + SCOPED),
            cost_estimate=pl.CostEstimate(flops=cost, bytes_accessed=1000, transcendentals=0),
            name=name,
        )(*operands)

    return run


def per_device(
    n_rows,
    n_blk,
    pair_left,
    pair_right,
    pair_middle,
    cotangent,
    left_weight,
    right_weight,
    gate_weight,
    output_weight,
):
    n_i, k_left, width = pair_left.shape
    n_j, k_right, _ = pair_right.shape
    n_k = k_left * n_blk
    left_raw = [pair_left] + [shift(pair_left, "blk", n_blk, s) for s in range(1, n_blk)]
    right_raw = [pair_right] + [exchange(pair_right, "rows", n_rows, s) for s in range(1, n_rows)]
    middle_shape = (n_i, n_j, width)
    gate, middle_in, head_back, tri_up = call(
        middle_kernel,
        "middle",
        [shape(middle_shape, f32), shape(middle_shape, bf16), shape(middle_shape, bf16), shape(middle_shape, f32)],
        scratch=[
            *(pltpu.VMEM(x.shape, bf16) for x in (pair_middle, cotangent, gate_weight, output_weight)),
            pltpu.SemaphoreType.DMA((4,)),
        ],
        after=4,
        space=pltpu.HBM,
    )(pair_middle, cotangent, gate_weight, output_weight)
    right_act, right_in, *right_flip = call(
        functools.partial(right_kernel, n_rows, n_blk, k_left),
        "right",
        [shape((n_j * n_k, width), f32), shape((n_rows, n_j, k_right, width), bf16)]
        + [shape((k_left, n_j, width), f32)] * n_blk,
    )(*right_raw, right_weight)
    left_act, left_in, total = [], [], []
    act_shape = shape(pair_left.shape, f32)
    in_shape = shape(pair_left.shape, bf16)
    for s in range(n_blk - 1):
        act, inputs, total = call(
            functools.partial(left_kernel, s == 0),
            "left",
            [act_shape, in_shape, shape(middle_shape, f32)],
        )(left_raw[s], left_weight, right_flip[s], *total)
        left_act.append(act)
        left_in.append(inputs)
        total = [total]
    act, inputs, tri_in, tri_back = call(
        functools.partial(triangle_kernel, n_blk > 1),
        "triangle",
        [act_shape, in_shape, shape(middle_shape, bf16), shape(middle_shape, f32)],
    )(left_raw[-1], left_weight, right_flip[-1], tri_up, *total)
    left_act.append(act)
    left_in.append(inputs)
    left_out = call(left_back_kernel, "left_back", [shape(pair_left.shape, bf16)] * n_blk)(
        tri_back, right_act
    )
    left_back = [left_out[0]] + [shift(left_out[s], "blk", n_blk, n_blk - s) for s in range(1, n_blk)]
    right_stack = shape((n_rows // 2,) + pair_right.shape, bf16)
    keep, send = call(
        functools.partial(right_back_kernel, n_rows, n_blk),
        "right_back",
        [right_stack, right_stack],
        scratch=[pltpu.VMEM((n_j, n_k, width), bf16)],
        after=1,
    )(tri_back, *left_act, left_out[0])
    kept, came, sent = halving_sum(keep, send, "rows", n_rows, (behind(*left_back[1:]),))
    update, pre_back, gate_part, output_part = call(
        heads_kernel,
        "heads",
        [
            shape(middle_shape, bf16),
            shape(middle_shape, bf16),
            shape(gate_weight.shape, f32),
            shape(output_weight.shape, f32),
        ],
        after=1,
    )(tri_in, output_weight, gate, middle_in, head_back, cotangent, left_out[0])
    parts = (n_rows // 2, width // n_rows, 6 * width)
    keep, send = call(
        functools.partial(weights_kernel, n_rows, n_blk),
        "weights",
        [shape(parts, f32), shape(parts, bf16)],
        scratch=[pltpu.VMEM((width, 6 * width), f32)],
    )(right_in, left_weight, right_weight, gate_part, output_part, *left_in, *left_out, keep, send)
    keep, part, _ = halving_sum(keep, send, "rows", n_rows, (behind(sent),))
    part = combine([keep, part])
    (grad_middle,) = call(grad_middle_kernel, "grad_middle", [shape(middle_shape, bf16)])(
        pair_middle, pre_back, gate_weight
    )
    part = combine([part] + [shift(part, "blk", n_blk, s) for s in range(1, n_blk)], (grad_middle,))
    pieces = [part] + [exchange(part, "rows", n_rows, s) for s in range(1, n_rows)]
    grad_left, grad_right = call(
        functools.partial(side_kernel, n_blk),
        "sides",
        [shape(pair_left.shape, bf16), shape(pair_right.shape, bf16)],
    )(pair_left, pair_right, left_weight, right_weight, *left_back, kept, came)
    deltas = call(
        functools.partial(deltas_kernel, n_rows),
        "deltas",
        [shape(x.shape, f32) for x in (left_weight, right_weight, gate_weight, output_weight)],
        after=1,
    )(*pieces, grad_left)
    return (
        update,
        grad_left,
        grad_right,
        grad_middle,
        *deltas,
    )


def solution(mesh):
    sides = P(("rep", "rows"), "blk", None)
    right = P(("rep", "blk"), "rows", None)
    return jax.shard_map(
        functools.partial(per_device, mesh.shape["rows"], mesh.shape["blk"]),
        mesh=mesh,
        in_specs=(sides, right, sides, sides, P(), P(), P(), P()),
        out_specs=(sides, sides, right, sides) + (P("rep", None),) * 4,
        check_vma=False,
    )
```

```python
import functools
import math

import jax
import jax.numpy as jnp
from jax import lax
from jax.experimental import pallas as pl
from jax.experimental.pallas import tpu as pltpu
from jax.sharding import PartitionSpec as P

epsilon = 1e-05
f32 = jnp.float32
bf16 = jnp.bfloat16
SCOPED = 6 * 1024 * 1024
MARK = jax.ShapeDtypeStruct((8, 128), jnp.float32)


def normalize(values):
    centred = values - jnp.mean(values, axis=-1, keepdims=True)
    inverse = lax.rsqrt(jnp.mean(centred * centred, axis=-1, keepdims=True) + epsilon)
    return (centred * inverse, inverse)


def normalize_back(normed, inverse, upstream):
    first = jnp.mean(upstream, axis=-1, keepdims=True)
    second = jnp.mean(upstream * normed, axis=-1, keepdims=True)
    return inverse * (upstream - first - normed * second)


def sigmoid(x):
    return 0.5 * jnp.tanh(0.5 * x) + 0.5


def dot(a, b):
    return lax.dot_general(a, b, (((1,), (0,)), ((), ())), preferred_element_type=f32)


def dot_nt(a, b):
    return lax.dot_general(a, b, (((1,), (1,)), ((), ())), preferred_element_type=f32)


def dot_tn(a, b):
    return lax.dot_general(a, b, (((0,), (0,)), ((), ())), preferred_element_type=f32)


def gated(inputs, weight):
    pre = dot(inputs, weight)
    width = weight.shape[1] // 2
    return pre[:, :width], sigmoid(pre[:, width:])


def joined_grad(back, lin, sw):
    return jnp.concatenate([back * sw, back * lin * sw * (1.0 - sw)], axis=-1).astype(bf16)


def middle_kernel(middle, cotangent, gate_weight, output_weight, _, gate, middle_in, head_back, tri_up):
    n_i, n_j, width = middle.shape
    step = 8

    def body(at, _):
        rows = pl.ds(at * step, step)
        normed, _ = normalize(middle[rows].astype(f32).reshape(step * n_j, width))
        inputs = normed.astype(bf16)
        opened = sigmoid(dot(inputs, gate_weight[...]))
        back = (cotangent[rows].astype(f32).reshape(step * n_j, width) * opened).astype(bf16)
        gate[rows] = opened.reshape(step, n_j, width)
        middle_in[rows] = inputs.reshape(step, n_j, width)
        head_back[rows] = back.reshape(step, n_j, width)
        up = dot_nt(back, output_weight[...])
        tri_up[rows] = (up - jnp.mean(up, axis=-1, keepdims=True)).reshape(step, n_j, width)
        return 0

    lax.fori_loop(0, n_i // step, body, 0, unroll=2)


def right_kernel(n_rows, n_blk, k_left, *refs):
    raw, (weight, act_out, in_out, *flip_out) = refs[:n_rows], refs[n_rows:]
    n_j, k_right, width = raw[0].shape
    n_k = k_left * n_blk
    unit = math.gcd(k_left, k_right)
    step = 16
    for s in range(n_rows):

        def body(at, _, s=s):
            rows = pl.ds(at * step, step)
            normed, _ = normalize(raw[s][rows].astype(f32).reshape(step * k_right, width))
            inputs = normed.astype(bf16)
            in_out[s, rows] = inputs.reshape(step, k_right, width)
            lin, sw = gated(inputs, weight[...])
            act = (sw * lin).astype(bf16).astype(f32).reshape(step, k_right, width)
            for part in range(k_right // unit):
                at_k = place(n_blk, k_left, k_right, s, part)
                for j in range(step):
                    start = pl.multiple_of((at * step + j) * n_k + at_k, unit)
                    act_out[pl.ds(start, unit), :] = act[j, part * unit : (part + 1) * unit]
            return 0

        lax.fori_loop(0, n_j // step, body, 0)

    for s in range(n_blk):

        def flip(k, _, s=s):
            flip_out[s][k] = act_out[pl.ds(s * k_left + k, n_j, stride=n_k), :]
            return 0

        lax.fori_loop(0, k_left, flip, 0, unroll=True)


def place(n_blk, k_left, k_right, piece, part):
    unit = math.gcd(k_left, k_right)
    vertex = lax.bitwise_xor(lax.axis_index("rows"), piece) * k_right + part * unit
    block = vertex // k_left
    at = lax.rem(lax.axis_index("blk") - block + n_blk, n_blk) * k_left + vertex - block * k_left
    return pl.multiple_of(at, unit)


def project_left(raw, weight, act_out, in_out):
    n_i, k_left, width = raw.shape
    step = 8

    def body(at, _):
        rows = pl.ds(at * step, step)
        normed, _ = normalize(raw[rows].astype(f32).reshape(step * k_left, width))
        inputs = normed.astype(bf16)
        in_out[rows] = inputs.reshape(step, k_left, width)
        lin, sw = gated(inputs, weight[...])
        act_out[rows] = (sw * lin).astype(bf16).astype(f32).reshape(step, k_left, width)
        return 0

    lax.fori_loop(0, n_i // step, body, 0, unroll=2)


def add_vertices(rows, act, flip):
    total = act[rows, 0:1, :] * flip[0][None]
    for k in range(1, act.shape[1]):
        total = total + act[rows, k : k + 1, :] * flip[k][None]
    return total


def left_kernel(first, raw, weight, flip, *refs):
    total_in, (act_out, in_out, total_out) = refs[: 0 if first else 1], refs[0 if first else 1 :]
    n_i, n_j, width = total_out.shape
    step = 8
    project_left(raw, weight, act_out, in_out)

    def body(at, _):
        rows = pl.ds(at * step, step)
        total = add_vertices(rows, act_out, flip)
        total_out[rows] = total if first else total_in[0][rows] + total
        return 0

    lax.fori_loop(0, n_i // step, body, 0)


def triangle_kernel(has_total, raw, left_w, flip, tri_up, *refs):
    total_in, refs = refs[: 1 if has_total else 0], refs[1 if has_total else 0 :]
    act_out, in_out, tri_in, tri_back = refs
    n_i, n_j, width = tri_in.shape
    step = 8
    project_left(raw, left_w, act_out, in_out)

    def triangle_rows(at, _):
        rows = pl.ds(at * step, step)
        total = add_vertices(rows, act_out, flip)
        if has_total:
            total = total + total_in[0][rows]
        flat = step * n_j
        normed, inverse = normalize(total.reshape(flat, width))
        tri_in[rows] = normed.astype(bf16).reshape(step, n_j, width)
        up = tri_up[rows].reshape(flat, width)
        second = jnp.mean(up * normed, axis=-1, keepdims=True)
        back = inverse * (up - normed * second)
        tri_back[rows] = back.astype(bf16).astype(f32).reshape(step, n_j, width)
        return 0

    lax.fori_loop(0, n_i // step, triangle_rows, 0, unroll=2)


def heads_kernel(tri_in, out_w, gate, middle_in, head_back, cotangent, _, *refs):
    update, pre_back, gate_part, output_part = refs
    n_i, n_j, width = update.shape
    step = 8
    gate_part[...] = jnp.zeros_like(gate_part)
    output_part[...] = jnp.zeros_like(output_part)

    def body(at, _):
        rows = pl.ds(at * step, step)
        flat = step * n_j
        inputs = tri_in[rows].reshape(flat, width)
        head = dot(inputs, out_w[...])
        opened = gate[rows].reshape(flat, width)
        update[rows] = (opened * head).astype(bf16).reshape(step, n_j, width)
        upstream = cotangent[rows].astype(f32).reshape(flat, width)
        pre = (upstream * head * opened * (1.0 - opened)).astype(bf16)
        pre_back[rows] = pre.reshape(step, n_j, width)
        gate_part[...] += dot_tn(middle_in[rows].reshape(flat, width), pre)
        output_part[...] += dot_tn(inputs, head_back[rows].reshape(flat, width))
        return 0

    lax.fori_loop(0, n_i // step, body, 0, unroll=2)


def vertex_step(n_k, unit):
    size = unit
    while size * 2 <= 64 and n_k % (size * 2) == 0:
        size *= 2
    return size


def left_back_kernel(tri_back, right_act, *left_out):
    n_i, n_j, width = tri_back.shape
    k_left = left_out[0].shape[1]
    n_k = k_left * len(left_out)
    few = 4
    k_step = vertex_step(n_k, k_left)
    for k0 in range(0, n_k, k_step):

        def rows_sum(at, _, k0=k0):
            rows = pl.ds(at * few, few)
            total = jnp.zeros((few, k_step, width), f32)
            for j in range(n_j):
                start = j * n_k + k0
                total = total + tri_back[rows, j : j + 1, :] * right_act[start : start + k_step, :][None]
            total = total.astype(bf16)
            for s in range(k0 // k_left, (k0 + k_step) // k_left):
                left_out[s][rows] = total[:, s * k_left - k0 : (s + 1) * k_left - k0]
            return 0

        lax.fori_loop(0, n_i // few, rows_sum, 0)


def right_back_kernel(n_rows, n_blk, tri_back, *refs):
    left_act, refs = refs[:n_blk], refs[n_blk + 1 :]
    keep, send, right_sum = refs
    n_i, n_j, width = tri_back.shape
    k_left = left_act[0].shape[1]
    n_k = k_left * n_blk
    k_right = keep.shape[2]
    unit = math.gcd(k_left, k_right)
    few = 4
    k_step = vertex_step(n_k, k_left)
    for k0 in range(0, n_k, k_step):
        blocks = range(k0 // k_left, (k0 + k_step) // k_left)

        def rows_sum(at, _, k0=k0, blocks=blocks):
            eight = pl.ds(pl.multiple_of(at * 8, 8), 8)
            for half in range(0, 8, few):

                def add(i, totals):
                    some = tri_back[i, eight, :][half : half + few][:, None]
                    return tuple(
                        total + some * left_act[s][i][None] for s, total in zip(blocks, totals)
                    )

                zeros = tuple(jnp.zeros((few, k_left, width), f32) for _ in blocks)
                totals = lax.fori_loop(0, n_i, add, zeros, unroll=16)
                for s, total in zip(blocks, totals):
                    right_sum[pl.ds(at * 8 + half, few), s * k_left : (s + 1) * k_left, :] = total.astype(bf16)
            return 0

        lax.fori_loop(0, n_j // 8, rows_sum, 0)
    for s in range(n_rows):
        for part in range(k_right // unit):
            out = send if s % 2 else keep
            out[s // 2, :, part * unit : (part + 1) * unit, :] = right_sum[
                :, pl.ds(place(n_blk, k_left, k_right, s, part), unit), :
            ]


def weights_kernel(n_rows, n_blk, right_in, left_w, right_w, gate_part, output_part, *refs):
    left_in, refs = refs[:n_blk], refs[n_blk:]
    left_out, refs = refs[:n_blk], refs[n_blk:]
    keep, send, _, keep_out, send_out, total = refs
    right_out = [(send if s % 2 else keep).at[s // 2] for s in range(n_rows)]
    right_ins = [right_in.at[s] for s in range(n_rows)]
    width = gate_part.shape[0]
    total[:, 4 * width : 5 * width] = gate_part[...]
    total[:, 5 * width :] = output_part[...]
    for inputs_refs, weight, backs, first in (
        (left_in, left_w, left_out, 0),
        (right_ins, right_w, right_out, 2 * width),
    ):
        columns = slice(first, first + 2 * width)
        total[:, columns] = jnp.zeros((width, 2 * width), f32)
        n, k, _ = inputs_refs[0].shape
        step = 16
        flat = step * k
        for inputs_ref, back_ref in zip(inputs_refs, backs):

            def body(at, _, inputs_ref=inputs_ref, back_ref=back_ref, weight=weight, columns=columns, flat=flat):
                rows = pl.ds(at * step, step)
                inputs = inputs_ref[rows].reshape(flat, width)
                lin, sw = gated(inputs, weight[...])
                back = back_ref[rows].reshape(flat, width).astype(f32)
                total[:, columns] += dot_tn(inputs, joined_grad(back, lin, sw))
                return 0

            lax.fori_loop(0, n // step, body, 0, unroll=2)
    size = width // n_rows
    for s in range(n_rows):
        start = pl.multiple_of(lax.bitwise_xor(lax.axis_index("rows"), s) * size, size)
        piece = total[pl.ds(start, size), :]
        if s % 2:
            send_out[s // 2] = piece.astype(bf16)
        else:
            keep_out[s // 2] = piece


def grad_middle_kernel(middle, pre_back, gate_weight, grad_middle, mark):
    mark[...] = jnp.zeros_like(mark)
    n_i, n_j, width = middle.shape
    step = 8

    def body(at, _):
        rows = pl.ds(at * step, step)
        flat = step * n_j
        normed, inverse = normalize(middle[rows].astype(f32).reshape(flat, width))
        up = dot_nt(pre_back[rows].reshape(flat, width), gate_weight[...])
        grad_middle[rows] = normalize_back(normed, inverse, up).astype(bf16).reshape(step, n_j, width)
        return 0

    lax.fori_loop(0, n_i // step, body, 0, unroll=2)


def side_kernel(n_left, *refs):
    *refs, mark = refs
    mark[...] = jnp.zeros_like(mark)
    left, right, left_w, right_w = refs[:4]
    left_back, refs = refs[4 : 4 + n_left], refs[4 + n_left :]
    right_back, refs = [ref.at[0] for ref in refs[:2]], refs[2:]
    for raw, weight, backs, grad in (
        (left, left_w, left_back, refs[0]),
        (right, right_w, right_back, refs[1]),
    ):
        n, k, width = raw.shape
        step = 16
        flat = step * k

        def body(at, _, raw=raw, weight=weight, backs=backs, grad=grad, step=step, flat=flat, k=k, width=width):
            rows = pl.ds(at * step, step)
            normed, inverse = normalize(raw[rows].astype(f32).reshape(flat, width))
            lin, sw = gated(normed.astype(bf16), weight[...])
            back = backs[0][rows].astype(f32)
            for other in backs[1:]:
                back = back + other[rows].astype(f32)
            up = dot_nt(joined_grad(back.reshape(flat, width), lin, sw), weight[...])
            grad[rows] = normalize_back(normed, inverse, up).astype(bf16).reshape(step, k, width)
            return 0

        lax.fori_loop(0, n // step, body, 0, unroll=2)


def shift(x, axis, n, step):
    return lax.ppermute(x, axis, [(a, (a + step) % n) for a in range(n)])


def exchange(x, axis, n, bit):
    return lax.ppermute(x, axis, [(a, a ^ bit) for a in range(n)])


def halve_kernel(keep, came, *refs):
    kept, send = refs[-2:]
    for at in range(keep.shape[0]):
        total = keep[at].astype(f32) + came[at].astype(f32)
        if at % 2:
            send[at // 2] = total.astype(bf16)
        else:
            kept[at // 2] = total


def halving_sum(keep, send, axis, n, after):
    came = exchange(send, axis, n, 1)
    bit = 2
    while bit < n:
        half = (keep.shape[0] // 2,) + keep.shape[1:]
        keep, send = call(halve_kernel, "halve", [shape(half, f32), shape(half, bf16)], after=len(after))(
            keep, came, *after
        )
        came = exchange(send, axis, n, bit)
        bit *= 2
    return keep, came, send


def order_kernel(*refs):
    refs[-1][...] = jnp.zeros_like(refs[-1])


def behind(*arrays):
    (mark,) = call(order_kernel, "order", [MARK], after=len(arrays), cost=2 * 10**10)(*arrays)
    return mark


def combine_kernel(n, *refs):
    total = refs[0][0].astype(f32)
    for at in range(1, refs[0].shape[0]):
        total = total + refs[0][at].astype(f32)
    for other in refs[1:n]:
        total = total + other[0].astype(f32)
    refs[-1][0] = total.astype(bf16)


def combine(pieces, after=()):
    (total,) = call(
        functools.partial(combine_kernel, len(pieces)),
        "combine",
        [shape((1,) + pieces[0].shape[1:], bf16)],
        after=len(after),
    )(*pieces, *after)
    return total


def deltas_kernel(n_rows, *refs):
    pieces, outs = [ref.at[0] for ref in refs[:n_rows]], refs[n_rows:]
    size = pieces[0].shape[0]
    for s, piece in enumerate(pieces):
        start = pl.multiple_of(lax.bitwise_xor(lax.axis_index("rows"), s) * size, size)
        first = 0
        for out in outs:
            last = first + out.shape[1]
            out[pl.ds(start, size), :] = piece[:, first:last].astype(f32)
            first = last


def shape(dims, kind):
    return jax.ShapeDtypeStruct(tuple(dims), kind)


def call(kernel, name, outs, scratch=(), after=0, cost=1000):
    def run(*operands):
        spaces = [pltpu.VMEM] * (len(operands) - after) + [pl.ANY] * after
        held = sum(math.prod(x.shape) * 4 for x in scratch)
        return pl.pallas_call(
            kernel,
            in_specs=[pl.BlockSpec(memory_space=space) for space in spaces],
            out_specs=[pl.BlockSpec(memory_space=pltpu.VMEM)] * len(outs),
            out_shape=outs,
            scratch_shapes=list(scratch),
            compiler_params=pltpu.CompilerParams(vmem_limit_bytes=held + SCOPED),
            cost_estimate=pl.CostEstimate(flops=cost, bytes_accessed=1000, transcendentals=0),
            name=name,
        )(*operands)

    return run


def per_device(
    n_rows,
    n_blk,
    pair_left,
    pair_right,
    pair_middle,
    cotangent,
    left_weight,
    right_weight,
    gate_weight,
    output_weight,
):
    n_i, k_left, width = pair_left.shape
    n_j, k_right, _ = pair_right.shape
    n_k = k_left * n_blk
    left_raw = [pair_left] + [shift(pair_left, "blk", n_blk, s) for s in range(1, n_blk)]
    right_raw = [pair_right] + [exchange(pair_right, "rows", n_rows, s) for s in range(1, n_rows)]
    middle_shape = (n_i, n_j, width)
    gate, middle_in, head_back, tri_up = call(
        middle_kernel,
        "middle",
        [shape(middle_shape, f32), shape(middle_shape, bf16), shape(middle_shape, bf16), shape(middle_shape, f32)],
        after=1,
    )(pair_middle, cotangent, gate_weight, output_weight, behind())
    right_act, right_in, *right_flip = call(
        functools.partial(right_kernel, n_rows, n_blk, k_left),
        "right",
        [shape((n_j * n_k, width), f32), shape((n_rows, n_j, k_right, width), bf16)]
        + [shape((k_left, n_j, width), f32)] * n_blk,
    )(*right_raw, right_weight)
    left_act, left_in, total = [], [], []
    act_shape = shape(pair_left.shape, f32)
    in_shape = shape(pair_left.shape, bf16)
    for s in range(n_blk - 1):
        act, inputs, total = call(
            functools.partial(left_kernel, s == 0),
            "left",
            [act_shape, in_shape, shape(middle_shape, f32)],
        )(left_raw[s], left_weight, right_flip[s], *total)
        left_act.append(act)
        left_in.append(inputs)
        total = [total]
    act, inputs, tri_in, tri_back = call(
        functools.partial(triangle_kernel, n_blk > 1),
        "triangle",
        [act_shape, in_shape, shape(middle_shape, bf16), shape(middle_shape, f32)],
    )(left_raw[-1], left_weight, right_flip[-1], tri_up, *total)
    left_act.append(act)
    left_in.append(inputs)
    left_out = call(left_back_kernel, "left_back", [shape(pair_left.shape, bf16)] * n_blk)(
        tri_back, right_act
    )
    left_back = [left_out[0]] + [shift(left_out[s], "blk", n_blk, n_blk - s) for s in range(1, n_blk)]
    right_stack = shape((n_rows // 2,) + pair_right.shape, bf16)
    keep, send = call(
        functools.partial(right_back_kernel, n_rows, n_blk),
        "right_back",
        [right_stack, right_stack],
        scratch=[pltpu.VMEM((n_j, n_k, width), bf16)],
        after=1,
    )(tri_back, *left_act, left_out[0])
    kept, came, sent = halving_sum(keep, send, "rows", n_rows, (behind(*left_back[1:]),))
    update, pre_back, gate_part, output_part = call(
        heads_kernel,
        "heads",
        [
            shape(middle_shape, bf16),
            shape(middle_shape, bf16),
            shape(gate_weight.shape, f32),
            shape(output_weight.shape, f32),
        ],
        after=1,
    )(tri_in, output_weight, gate, middle_in, head_back, cotangent, left_out[0])
    grad_middle, done_middle = call(
        grad_middle_kernel, "grad_middle", [shape(middle_shape, bf16), MARK]
    )(pair_middle, pre_back, gate_weight)
    parts = (n_rows // 2, width // n_rows, 6 * width)
    keep, send = call(
        functools.partial(weights_kernel, n_rows, n_blk),
        "weights",
        [shape(parts, f32), shape(parts, bf16)],
        scratch=[pltpu.VMEM((width, 6 * width), f32)],
        after=1,
    )(right_in, left_weight, right_weight, gate_part, output_part, *left_in, *left_out, keep, send, done_middle)
    keep, part, _ = halving_sum(keep, send, "rows", n_rows, ())
    part = combine([keep, part], (behind(sent),))
    grad_left, grad_right, done_sides = call(
        functools.partial(side_kernel, n_blk),
        "sides",
        [shape(pair_left.shape, bf16), shape(pair_right.shape, bf16), MARK],
    )(pair_left, pair_right, left_weight, right_weight, *left_back, kept, came)
    part = combine([part] + [shift(part, "blk", n_blk, s) for s in range(1, n_blk)], (done_sides,))
    pieces = [part] + [exchange(part, "rows", n_rows, s) for s in range(1, n_rows)]
    deltas = call(
        functools.partial(deltas_kernel, n_rows),
        "deltas",
        [shape(x.shape, f32) for x in (left_weight, right_weight, gate_weight, output_weight)],
    )(*pieces)
    return (
        update,
        grad_left,
        grad_right,
        grad_middle,
        *deltas,
    )


def solution(mesh):
    sides = P(("rep", "rows"), "blk", None)
    right = P(("rep", "blk"), "rows", None)
    return jax.shard_map(
        functools.partial(per_device, mesh.shape["rows"], mesh.shape["blk"]),
        mesh=mesh,
        in_specs=(sides, right, sides, sides, P(), P(), P(), P()),
        out_specs=(sides, sides, right, sides) + (P("rep", None),) * 4,
        check_vma=False,
    )
```

```python
import functools
import math

import jax
import jax.numpy as jnp
from jax import lax
from jax.experimental import pallas as pl
from jax.experimental.pallas import tpu as pltpu
from jax.sharding import PartitionSpec as P

epsilon = 1e-05
f32 = jnp.float32
bf16 = jnp.bfloat16
SCOPED = 6 * 1024 * 1024
LEFT_COST = 2 * 10**8
MARK = jax.ShapeDtypeStruct((8, 128), jnp.float32)


def normalize(values):
    centred = values - jnp.mean(values, axis=-1, keepdims=True)
    inverse = lax.rsqrt(jnp.mean(centred * centred, axis=-1, keepdims=True) + epsilon)
    return (centred * inverse, inverse)


def normalize_back(normed, inverse, upstream):
    first = jnp.mean(upstream, axis=-1, keepdims=True)
    second = jnp.mean(upstream * normed, axis=-1, keepdims=True)
    return inverse * (upstream - first - normed * second)


def sigmoid(x):
    return 0.5 * jnp.tanh(0.5 * x) + 0.5


def dot(a, b):
    return lax.dot_general(a, b, (((1,), (0,)), ((), ())), preferred_element_type=f32)


def dot_nt(a, b):
    return lax.dot_general(a, b, (((1,), (1,)), ((), ())), preferred_element_type=f32)


def dot_tn(a, b):
    return lax.dot_general(a, b, (((0,), (0,)), ((), ())), preferred_element_type=f32)


def gated(inputs, weight):
    pre = dot(inputs, weight)
    width = weight.shape[1] // 2
    return pre[:, :width], sigmoid(pre[:, width:])


def joined_grad(back, lin, sw):
    return jnp.concatenate([back * sw, back * lin * sw * (1.0 - sw)], axis=-1).astype(bf16)


def middle_kernel(middle, cotangent, gate_weight, output_weight, _, gate, middle_in, head_back, tri_up):
    n_i, n_j, width = middle.shape
    step = 8

    def body(at, _):
        rows = pl.ds(at * step, step)
        normed, _ = normalize(middle[rows].astype(f32).reshape(step * n_j, width))
        inputs = normed.astype(bf16)
        opened = sigmoid(dot(inputs, gate_weight[...]))
        back = (cotangent[rows].astype(f32).reshape(step * n_j, width) * opened).astype(bf16)
        gate[rows] = opened.reshape(step, n_j, width)
        middle_in[rows] = inputs.reshape(step, n_j, width)
        head_back[rows] = back.reshape(step, n_j, width)
        up = dot_nt(back, output_weight[...])
        tri_up[rows] = (up - jnp.mean(up, axis=-1, keepdims=True)).reshape(step, n_j, width)
        return 0

    lax.fori_loop(0, n_i // step, body, 0, unroll=2)


def right_kernel(n_rows, n_blk, k_left, *refs):
    raw, (weight, act_out, in_out, *flip_out) = refs[:n_rows], refs[n_rows:]
    n_j, k_right, width = raw[0].shape
    n_k = k_left * n_blk
    unit = math.gcd(k_left, k_right)
    step = 16
    for s in range(n_rows):

        def body(at, _, s=s):
            rows = pl.ds(at * step, step)
            normed, _ = normalize(raw[s][rows].astype(f32).reshape(step * k_right, width))
            inputs = normed.astype(bf16)
            in_out[s, rows] = inputs.reshape(step, k_right, width)
            lin, sw = gated(inputs, weight[...])
            act = (sw * lin).astype(bf16).astype(f32).reshape(step, k_right, width)
            for part in range(k_right // unit):
                at_k = place(n_blk, k_left, k_right, s, part)
                for j in range(step):
                    start = pl.multiple_of((at * step + j) * n_k + at_k, unit)
                    act_out[pl.ds(start, unit), :] = act[j, part * unit : (part + 1) * unit]
            return 0

        lax.fori_loop(0, n_j // step, body, 0)

    for s in range(n_blk):

        def flip(k, _, s=s):
            flip_out[s][k] = act_out[pl.ds(s * k_left + k, n_j, stride=n_k), :]
            return 0

        lax.fori_loop(0, k_left, flip, 0, unroll=True)


def place(n_blk, k_left, k_right, piece, part):
    unit = math.gcd(k_left, k_right)
    vertex = lax.bitwise_xor(lax.axis_index("rows"), piece) * k_right + part * unit
    block = vertex // k_left
    at = lax.bitwise_xor(lax.axis_index("blk"), block) * k_left + vertex - block * k_left
    return pl.multiple_of(at, unit)


def project_left(raws, weight, act_out, in_out):
    n_i, k_left, width = raws[0].shape
    step = 8

    def body(at, _):
        rows = pl.ds(at * step, step)
        raw = raws[0][rows].astype(f32)
        for other in raws[1:]:
            raw = raw + other[rows].astype(f32)
        normed, _ = normalize(raw.reshape(step * k_left, width))
        inputs = normed.astype(bf16)
        in_out[rows] = inputs.reshape(step, k_left, width)
        lin, sw = gated(inputs, weight[...])
        act_out[rows] = (sw * lin).astype(bf16).astype(f32).reshape(step, k_left, width)
        return 0

    lax.fori_loop(0, n_i // step, body, 0, unroll=2)


def add_vertices(rows, act, flip):
    total = act[rows, 0:1, :] * flip[0][None]
    for k in range(1, act.shape[1]):
        total = total + act[rows, k : k + 1, :] * flip[k][None]
    return total


def left_kernel(n_raw, first, *refs):
    raw, (weight, flip, *refs) = refs[:n_raw], refs[n_raw:]
    total_in, (act_out, in_out, total_out) = refs[: 0 if first else 1], refs[0 if first else 1 :]
    n_i, n_j, width = total_out.shape
    step = 8
    project_left(raw, weight, act_out, in_out)

    def body(at, _):
        rows = pl.ds(at * step, step)
        total = add_vertices(rows, act_out, flip)
        total_out[rows] = total if first else total_in[0][rows] + total
        return 0

    lax.fori_loop(0, n_i // step, body, 0)


def triangle_kernel(n_raw, has_total, *refs):
    raw, (left_w, flip, tri_up, *refs) = refs[:n_raw], refs[n_raw:]
    total_in, refs = refs[: 1 if has_total else 0], refs[1 if has_total else 0 :]
    act_out, in_out, tri_in, tri_back = refs
    n_i, n_j, width = tri_in.shape
    step = 8
    project_left(raw, left_w, act_out, in_out)

    def triangle_rows(at, _):
        rows = pl.ds(at * step, step)
        total = add_vertices(rows, act_out, flip)
        if has_total:
            total = total + total_in[0][rows]
        flat = step * n_j
        normed, inverse = normalize(total.reshape(flat, width))
        tri_in[rows] = normed.astype(bf16).reshape(step, n_j, width)
        up = tri_up[rows].reshape(flat, width)
        second = jnp.mean(up * normed, axis=-1, keepdims=True)
        back = inverse * (up - normed * second)
        tri_back[rows] = back.astype(bf16).astype(f32).reshape(step, n_j, width)
        return 0

    lax.fori_loop(0, n_i // step, triangle_rows, 0, unroll=2)


def heads_kernel(tri_in, out_w, gate, middle_in, head_back, cotangent, _, *refs):
    update, pre_back, gate_part, output_part = refs
    n_i, n_j, width = update.shape
    step = 8
    gate_part[...] = jnp.zeros_like(gate_part)
    output_part[...] = jnp.zeros_like(output_part)

    def body(at, _):
        rows = pl.ds(at * step, step)
        flat = step * n_j
        inputs = tri_in[rows].reshape(flat, width)
        head = dot(inputs, out_w[...])
        opened = gate[rows].reshape(flat, width)
        update[rows] = (opened * head).astype(bf16).reshape(step, n_j, width)
        upstream = cotangent[rows].astype(f32).reshape(flat, width)
        pre = (upstream * head * opened * (1.0 - opened)).astype(bf16)
        pre_back[rows] = pre.reshape(step, n_j, width)
        gate_part[...] += dot_tn(middle_in[rows].reshape(flat, width), pre)
        output_part[...] += dot_tn(inputs, head_back[rows].reshape(flat, width))
        return 0

    lax.fori_loop(0, n_i // step, body, 0, unroll=2)


def vertex_step(n_k, unit):
    size = unit
    while size * 2 <= 64 and n_k % (size * 2) == 0:
        size *= 2
    return size


def left_back_kernel(first, n_blk, tri_back, right_act, *left_out):
    n_i, n_j, width = tri_back.shape
    k_left = left_out[0].shape[1]
    n_k = k_left * n_blk
    last = (first + len(left_out)) * k_left
    k_step = k_left * math.gcd(len(left_out), max(1, 64 // k_left))
    few = max(1, 256 // k_step)
    for k0 in range(first * k_left, last, k_step):

        def rows_sum(at, _, k0=k0):
            rows = pl.ds(at * few, few)
            total = jnp.zeros((few, k_step, width), f32)
            for j in range(n_j):
                start = j * n_k + k0
                total = total + tri_back[rows, j : j + 1, :] * right_act[start : start + k_step, :][None]
            total = total.astype(bf16)
            for s in range(k_step // k_left):
                left_out[k0 // k_left - first + s][rows] = total[:, s * k_left : (s + 1) * k_left]
            return 0

        lax.fori_loop(0, n_i // few, rows_sum, 0)


def right_back_kernel(n_rows, n_blk, tri_back, *refs):
    left_act, refs = refs[:n_blk], refs[n_blk + 1 :]
    keep, send, right_sum = refs
    n_i, n_j, width = tri_back.shape
    k_left = left_act[0].shape[1]
    n_k = k_left * n_blk
    k_right = keep.shape[2]
    unit = math.gcd(k_left, k_right)
    few = 4
    k_step = vertex_step(n_k, k_left)
    for k0 in range(0, n_k, k_step):
        blocks = range(k0 // k_left, (k0 + k_step) // k_left)

        def rows_sum(at, _, k0=k0, blocks=blocks):
            eight = pl.ds(pl.multiple_of(at * 8, 8), 8)
            for half in range(0, 8, few):

                def add(i, totals):
                    some = tri_back[i, eight, :][half : half + few][:, None]
                    return tuple(
                        total + some * left_act[s][i][None] for s, total in zip(blocks, totals)
                    )

                zeros = tuple(jnp.zeros((few, k_left, width), f32) for _ in blocks)
                totals = lax.fori_loop(0, n_i, add, zeros, unroll=16)
                for s, total in zip(blocks, totals):
                    right_sum[pl.ds(at * 8 + half, few), s * k_left : (s + 1) * k_left, :] = total.astype(bf16)
            return 0

        lax.fori_loop(0, n_j // 8, rows_sum, 0)
    for s in range(n_rows):
        for part in range(k_right // unit):
            out = send if s % 2 else keep
            out[s // 2, :, part * unit : (part + 1) * unit, :] = right_sum[
                :, pl.ds(place(n_blk, k_left, k_right, s, part), unit), :
            ]


def weights_kernel(n_rows, n_blk, right_in, left_w, right_w, gate_part, output_part, *refs):
    left_in, refs = refs[:n_blk], refs[n_blk:]
    left_out, refs = refs[:n_blk], refs[n_blk:]
    keep, send, keep_out, send_out, total = refs
    right_out = [(send if s % 2 else keep).at[s // 2] for s in range(n_rows)]
    right_ins = [right_in.at[s] for s in range(n_rows)]
    width = gate_part.shape[0]
    total[:, 4 * width : 5 * width] = gate_part[...]
    total[:, 5 * width :] = output_part[...]
    for inputs_refs, weight, backs, first in (
        (left_in, left_w, left_out, 0),
        (right_ins, right_w, right_out, 2 * width),
    ):
        columns = slice(first, first + 2 * width)
        total[:, columns] = jnp.zeros((width, 2 * width), f32)
        n, k, _ = inputs_refs[0].shape
        step = 16
        flat = step * k
        for inputs_ref, back_ref in zip(inputs_refs, backs):

            def body(at, _, inputs_ref=inputs_ref, back_ref=back_ref, weight=weight, columns=columns, flat=flat):
                rows = pl.ds(at * step, step)
                inputs = inputs_ref[rows].reshape(flat, width)
                lin, sw = gated(inputs, weight[...])
                back = back_ref[rows].reshape(flat, width).astype(f32)
                total[:, columns] += dot_tn(inputs, joined_grad(back, lin, sw))
                return 0

            lax.fori_loop(0, n // step, body, 0, unroll=2)
    size = width // n_rows
    for s in range(n_rows):
        start = pl.multiple_of(lax.bitwise_xor(lax.axis_index("rows"), s) * size, size)
        piece = total[pl.ds(start, size), :]
        if s % 2:
            send_out[s // 2] = piece.astype(bf16)
        else:
            keep_out[s // 2] = piece


def grad_middle_kernel(middle, pre_back, gate_weight, _, grad_middle, mark):
    mark[...] = jnp.zeros_like(mark)
    n_i, n_j, width = middle.shape
    step = 8

    def body(at, _):
        rows = pl.ds(at * step, step)
        flat = step * n_j
        normed, inverse = normalize(middle[rows].astype(f32).reshape(flat, width))
        up = dot_nt(pre_back[rows].reshape(flat, width), gate_weight[...])
        grad_middle[rows] = normalize_back(normed, inverse, up).astype(bf16).reshape(step, n_j, width)
        return 0

    lax.fori_loop(0, n_i // step, body, 0, unroll=2)


def side_kernel(n_left, *refs):
    *refs, mark = refs
    mark[...] = jnp.zeros_like(mark)
    left, right, left_w, right_w = refs[:4]
    left_back, refs = refs[4 : 4 + n_left], refs[4 + n_left :]
    right_back, refs = [ref.at[0] for ref in refs[:2]], refs[2:]
    for raw, weight, backs, grad in (
        (left, left_w, left_back, refs[0]),
        (right, right_w, right_back, refs[1]),
    ):
        n, k, width = raw.shape
        step = 16
        flat = step * k

        def body(at, _, raw=raw, weight=weight, backs=backs, grad=grad, step=step, flat=flat, k=k, width=width):
            rows = pl.ds(at * step, step)
            normed, inverse = normalize(raw[rows].astype(f32).reshape(flat, width))
            lin, sw = gated(normed.astype(bf16), weight[...])
            back = backs[0][rows].astype(f32)
            for other in backs[1:]:
                back = back + other[rows].astype(f32)
            up = dot_nt(joined_grad(back.reshape(flat, width), lin, sw), weight[...])
            grad[rows] = normalize_back(normed, inverse, up).astype(bf16).reshape(step, k, width)
            return 0

        lax.fori_loop(0, n // step, body, 0, unroll=2)


def exchange(x, axis, n, bit):
    return lax.ppermute(x, axis, [(a, a ^ bit) for a in range(n)])


def halve_kernel(keep, came, *refs):
    kept, send = refs[-2:]
    for at in range(keep.shape[0]):
        total = keep[at].astype(f32) + came[at].astype(f32)
        if at % 2:
            send[at // 2] = total.astype(bf16)
        else:
            kept[at // 2] = total


def halving_sum(keep, send, axis, n, after):
    came = exchange(send, axis, n, 1)
    bit = 2
    while bit < n:
        half = (keep.shape[0] // 2,) + keep.shape[1:]
        keep, send = call(halve_kernel, "halve", [shape(half, f32), shape(half, bf16)], after=len(after))(
            keep, came, *after
        )
        came = exchange(send, axis, n, bit)
        bit *= 2
    return keep, came, send


def forward_kernel(*refs):
    for source, target in zip(refs[:2], refs[-2:]):
        target[...] = source[...]


def gather_left(block, n, after):
    if n != 4:
        return [(block,)] + [(exchange(block, "blk", n, s),) for s in range(1, n)]
    across = exchange(block, "blk", n, 2)
    beside = exchange(block, "blk", n, 1)
    passed, own = call(forward_kernel, "forward", [shape(block.shape, block.dtype)] * 2, after=len(after))(across, block, *after)
    outer = lax.ppermute(passed, "blk", [(1, 0), (2, 3)])
    inner = lax.ppermute(own, "blk", [(1, 2), (2, 1)])
    return [(block,), (beside,), (across,), (outer, inner)]


def order_kernel(*refs):
    refs[-1][...] = jnp.zeros_like(refs[-1])


def behind(*arrays, cost=2 * 10**10):
    (mark,) = call(order_kernel, "order", [MARK], after=len(arrays), cost=cost)(*arrays)
    return mark


def combine_kernel(n, *refs):
    total = refs[0][0].astype(f32)
    for at in range(1, refs[0].shape[0]):
        total = total + refs[0][at].astype(f32)
    for other in refs[1:n]:
        total = total + other[0].astype(f32)
    refs[-1][0] = total.astype(bf16)


def combine(pieces, after=()):
    (total,) = call(
        functools.partial(combine_kernel, len(pieces)),
        "combine",
        [shape((1,) + pieces[0].shape[1:], bf16)],
        after=len(after),
    )(*pieces, *after)
    return total


def deltas_kernel(n_rows, *refs):
    pieces, outs = [ref.at[0] for ref in refs[:n_rows]], refs[n_rows:]
    size = pieces[0].shape[0]
    for s, piece in enumerate(pieces):
        start = pl.multiple_of(lax.bitwise_xor(lax.axis_index("rows"), s) * size, size)
        first = 0
        for out in outs:
            last = first + out.shape[1]
            out[pl.ds(start, size), :] = piece[:, first:last].astype(f32)
            first = last


def shape(dims, kind):
    return jax.ShapeDtypeStruct(tuple(dims), kind)


def call(kernel, name, outs, scratch=(), after=0, cost=1000):
    def run(*operands):
        spaces = [pltpu.VMEM] * (len(operands) - after) + [pl.ANY] * after
        held = sum(math.prod(x.shape) * 4 for x in scratch)
        return pl.pallas_call(
            kernel,
            in_specs=[pl.BlockSpec(memory_space=space) for space in spaces],
            out_specs=[pl.BlockSpec(memory_space=pltpu.VMEM)] * len(outs),
            out_shape=outs,
            scratch_shapes=list(scratch),
            compiler_params=pltpu.CompilerParams(vmem_limit_bytes=held + SCOPED),
            cost_estimate=pl.CostEstimate(flops=cost, bytes_accessed=1000, transcendentals=0),
            name=name,
        )(*operands)

    return run


def per_device(
    n_rows,
    n_blk,
    pair_left,
    pair_right,
    pair_middle,
    cotangent,
    left_weight,
    right_weight,
    gate_weight,
    output_weight,
):
    n_i, k_left, width = pair_left.shape
    n_j, k_right, _ = pair_right.shape
    n_k = k_left * n_blk
    right_raw = [pair_right] + [exchange(pair_right, "rows", n_rows, s) for s in range(1, n_rows)]
    middle_shape = (n_i, n_j, width)
    gate, middle_in, head_back, tri_up = call(
        middle_kernel,
        "middle",
        [shape(middle_shape, f32), shape(middle_shape, bf16), shape(middle_shape, bf16), shape(middle_shape, f32)],
        after=1,
    )(pair_middle, cotangent, gate_weight, output_weight, behind(cost=10**9))
    right_act, right_in, *right_flip = call(
        functools.partial(right_kernel, n_rows, n_blk, k_left),
        "right",
        [shape((n_j * n_k, width), f32), shape((n_rows, n_j, k_right, width), bf16)]
        + [shape((k_left, n_j, width), f32)] * n_blk,
    )(*right_raw, right_weight)
    left_raw = gather_left(pair_left, n_blk, (right_in, middle_in))
    left_act, left_in, total = [], [], []
    act_shape = shape(pair_left.shape, f32)
    in_shape = shape(pair_left.shape, bf16)
    for s in range(n_blk - 1):
        act, inputs, total = call(
            functools.partial(left_kernel, len(left_raw[s]), s == 0),
            "left",
            [act_shape, in_shape, shape(middle_shape, f32)],
        )(*left_raw[s], left_weight, right_flip[s], *total)
        left_act.append(act)
        left_in.append(inputs)
        total = [total]
    act, inputs, tri_in, tri_back = call(
        functools.partial(triangle_kernel, len(left_raw[-1]), n_blk > 1),
        "triangle",
        [act_shape, in_shape, shape(middle_shape, bf16), shape(middle_shape, f32)],
    )(*left_raw[-1], left_weight, right_flip[-1], tri_up, *total)
    left_act.append(act)
    left_in.append(inputs)
    half = n_blk // 2
    left_out = []
    for first in (half, 0):
        some = call(
            functools.partial(left_back_kernel, first, n_blk),
            "left_back",
            [shape(pair_left.shape, bf16)] * half,
            after=0,
        )(tri_back, right_act)
        left_out = [*some, *left_out]
    left_back = [left_out[0]] + [exchange(left_out[s], "blk", n_blk, s) for s in range(1, n_blk)]
    right_stack = shape((n_rows // 2,) + pair_right.shape, bf16)
    keep, send = call(
        functools.partial(right_back_kernel, n_rows, n_blk),
        "right_back",
        [right_stack, right_stack],
        scratch=[pltpu.VMEM((n_j, n_k, width), bf16)],
        after=1,
    )(tri_back, *left_act, left_out[0])
    kept, came, sent = halving_sum(keep, send, "rows", n_rows, (behind(*left_back[1:], cost=LEFT_COST),))
    update, pre_back, gate_part, output_part = call(
        heads_kernel,
        "heads",
        [
            shape(middle_shape, bf16),
            shape(middle_shape, bf16),
            shape(gate_weight.shape, f32),
            shape(output_weight.shape, f32),
        ],
        after=1,
    )(tri_in, output_weight, gate, middle_in, head_back, cotangent, left_out[0])
    parts = (n_rows // 2, width // n_rows, 6 * width)
    keep, send = call(
        functools.partial(weights_kernel, n_rows, n_blk),
        "weights",
        [shape(parts, f32), shape(parts, bf16)],
        scratch=[pltpu.VMEM((width, 6 * width), f32)],
    )(right_in, left_weight, right_weight, gate_part, output_part, *left_in, *left_out, keep, send)
    grad_middle, done_middle = call(
        grad_middle_kernel, "grad_middle", [shape(middle_shape, bf16), MARK], after=1
    )(pair_middle, pre_back, gate_weight, send)
    keep, part, _ = halving_sum(keep, send, "rows", n_rows, (done_middle,))
    part = combine([keep, part], (behind(sent),))
    grad_left, grad_right, done_sides = call(
        functools.partial(side_kernel, n_blk),
        "sides",
        [shape(pair_left.shape, bf16), shape(pair_right.shape, bf16), MARK],
    )(pair_left, pair_right, left_weight, right_weight, *left_back, kept, came)
    part = combine([part] + [exchange(part, "blk", n_blk, s) for s in range(1, n_blk)], (done_sides,))
    pieces = [part] + [exchange(part, "rows", n_rows, s) for s in range(1, n_rows)]
    deltas = call(
        functools.partial(deltas_kernel, n_rows),
        "deltas",
        [shape(x.shape, f32) for x in (left_weight, right_weight, gate_weight, output_weight)],
    )(*pieces)
    return (
        update,
        grad_left,
        grad_right,
        grad_middle,
        *deltas,
    )


def solution(mesh):
    sides = P(("rep", "rows"), "blk", None)
    right = P(("rep", "blk"), "rows", None)
    return jax.shard_map(
        functools.partial(per_device, mesh.shape["rows"], mesh.shape["blk"]),
        mesh=mesh,
        in_specs=(sides, right, sides, sides, P(), P(), P(), P()),
        out_specs=(sides, sides, right, sides) + (P("rep", None),) * 4,
        check_vma=False,
    )
```

```python
import functools
import math

import jax
import jax.numpy as jnp
from jax import lax
from jax.experimental import pallas as pl
from jax.experimental.pallas import tpu as pltpu
from jax.sharding import PartitionSpec as P

epsilon = 1e-05
f32 = jnp.float32
bf16 = jnp.bfloat16
SCOPED = 6 * 1024 * 1024
LEFT_COST = 2 * 10**8
MARK = jax.ShapeDtypeStruct((8, 128), jnp.float32)


def sigmoid(x):
    return 0.5 * jnp.tanh(0.5 * x) + 0.5


def dot(a, b):
    return lax.dot_general(a, b, (((1,), (0,)), ((), ())), preferred_element_type=f32)


def dot_nt(a, b):
    return lax.dot_general(a, b, (((1,), (1,)), ((), ())), preferred_element_type=f32)


def dot_tn(a, b):
    return lax.dot_general(a, b, (((0,), (0,)), ((), ())), preferred_element_type=f32)


def split(values):
    high = values.astype(bf16)
    return jnp.concatenate([high, (values - high.astype(f32)).astype(bf16)], axis=-1)


def row_mean(parts, width):
    return dot(parts, jnp.full((parts.shape[-1], width), 1.0 / width, bf16))


def normalize(values, mean):
    centred = values - mean
    inverse = lax.rsqrt(row_mean(split(centred * centred), values.shape[-1]) + epsilon)
    return (centred * inverse, inverse)


def normalize_raw(raw):
    return normalize(raw.astype(f32), row_mean(raw, raw.shape[-1]))


def normalize_back(normed, inverse, upstream):
    width = upstream.shape[-1]
    first = row_mean(split(upstream), width)
    second = row_mean(split(upstream * normed), width)
    return inverse * (upstream - first - normed * second)


def gated(inputs, weight):
    pre = dot(inputs, weight)
    width = weight.shape[1] // 2
    return pre[:, :width], sigmoid(pre[:, width:])


def joined_grad(back, lin, sw):
    return jnp.concatenate([back * sw, back * lin * sw * (1.0 - sw)], axis=-1).astype(bf16)


def middle_kernel(middle, cotangent, gate_weight, output_weight, _, gate, middle_in, head_back, tri_up):
    n_i, n_j, width = middle.shape
    step = 16

    def body(at, _):
        rows = pl.ds(at * step, step)
        normed, _ = normalize_raw(middle[rows].reshape(step * n_j, width))
        inputs = normed.astype(bf16)
        opened = sigmoid(dot(inputs, gate_weight[...]))
        back = (cotangent[rows].astype(f32).reshape(step * n_j, width) * opened).astype(bf16)
        gate[rows] = opened.reshape(step, n_j, width)
        middle_in[rows] = inputs.reshape(step, n_j, width)
        head_back[rows] = back.reshape(step, n_j, width)
        up = dot_nt(back, output_weight[...])
        tri_up[rows] = (up - row_mean(split(up), width)).reshape(step, n_j, width)
        return 0

    lax.fori_loop(0, n_i // step, body, 0, unroll=2)


def right_kernel(n_rows, n_blk, k_left, *refs):
    raw, (weight, act_out, in_out, *flip_out) = refs[:n_rows], refs[n_rows:]
    n_j, k_right, width = raw[0].shape
    n_k = k_left * n_blk
    unit = math.gcd(k_left, k_right)
    step = n_j
    for s in range(n_rows):

        def body(at, _, s=s):
            rows = pl.ds(at * step, step)
            normed, _ = normalize_raw(raw[s][rows].reshape(step * k_right, width))
            inputs = normed.astype(bf16)
            in_out[s, rows] = inputs.reshape(step, k_right, width)
            lin, sw = gated(inputs, weight[...])
            act = (sw * lin).astype(bf16).astype(f32).reshape(step, k_right, width)
            for part in range(k_right // unit):
                at_k = place(n_blk, k_left, k_right, s, part)
                for j in range(step):
                    start = pl.multiple_of((at * step + j) * n_k + at_k, unit)
                    act_out[pl.ds(start, unit), :] = act[j, part * unit : (part + 1) * unit]
            return 0

        lax.fori_loop(0, n_j // step, body, 0, unroll=True)

    for s in range(n_blk):

        def flip(k, _, s=s):
            flip_out[s][k] = act_out[pl.ds(s * k_left + k, n_j, stride=n_k), :]
            return 0

        lax.fori_loop(0, k_left, flip, 0, unroll=True)


def place(n_blk, k_left, k_right, piece, part):
    unit = math.gcd(k_left, k_right)
    vertex = lax.bitwise_xor(lax.axis_index("rows"), piece) * k_right + part * unit
    block = vertex // k_left
    at = lax.bitwise_xor(lax.axis_index("blk"), block) * k_left + vertex - block * k_left
    return pl.multiple_of(at, unit)


def project_left(raws, weight, act_out, in_out):
    n_i, k_left, width = raws[0].shape
    step = 32

    def body(at, _):
        rows = pl.ds(at * step, step)
        raw = raws[0][rows]
        for other in raws[1:]:
            raw = (raw.astype(f32) + other[rows].astype(f32)).astype(bf16)
        normed, _ = normalize_raw(raw.reshape(step * k_left, width))
        inputs = normed.astype(bf16)
        in_out[rows] = inputs.reshape(step, k_left, width)
        lin, sw = gated(inputs, weight[...])
        act_out[rows] = (sw * lin).astype(bf16).astype(f32).reshape(step, k_left, width)
        return 0

    lax.fori_loop(0, n_i // step, body, 0, unroll=2)


def add_vertices(rows, act, flip):
    total = act[rows, 0:1, :] * flip[0][None]
    for k in range(1, act.shape[1]):
        total = total + act[rows, k : k + 1, :] * flip[k][None]
    return total


def left_kernel(n_raw, first, *refs):
    raw, (weight, flip, *refs) = refs[:n_raw], refs[n_raw:]
    total_in, (act_out, in_out, total_out) = refs[: 0 if first else 1], refs[0 if first else 1 :]
    n_i, n_j, width = total_out.shape
    step = 8
    project_left(raw, weight, act_out, in_out)

    def body(at, _):
        rows = pl.ds(at * step, step)
        total = add_vertices(rows, act_out, flip)
        total_out[rows] = total if first else total_in[0][rows] + total
        return 0

    lax.fori_loop(0, n_i // step, body, 0)


def triangle_kernel(n_raw, has_total, *refs):
    raw, (left_w, flip, tri_up, *refs) = refs[:n_raw], refs[n_raw:]
    total_in, refs = refs[: 1 if has_total else 0], refs[1 if has_total else 0 :]
    act_out, in_out, tri_in, tri_back = refs
    n_i, n_j, width = tri_in.shape
    step = 8
    project_left(raw, left_w, act_out, in_out)

    def triangle_rows(at, _):
        rows = pl.ds(at * step, step)
        total = add_vertices(rows, act_out, flip)
        if has_total:
            total = total + total_in[0][rows]
        flat = step * n_j
        total = total.reshape(flat, width)
        normed, inverse = normalize(total, row_mean(split(total), width))
        tri_in[rows] = normed.astype(bf16).reshape(step, n_j, width)
        up = tri_up[rows].reshape(flat, width)
        second = row_mean(split(up * normed), width)
        back = inverse * (up - normed * second)
        tri_back[rows] = back.astype(bf16).astype(f32).reshape(step, n_j, width)
        return 0

    lax.fori_loop(0, n_i // step, triangle_rows, 0, unroll=4)


def heads_kernel(tri_in, out_w, gate, middle_in, head_back, cotangent, _, *refs):
    update, pre_back, gate_part, output_part = refs
    n_i, n_j, width = update.shape
    step = 8
    gate_part[...] = jnp.zeros_like(gate_part)
    output_part[...] = jnp.zeros_like(output_part)

    def body(at, _):
        rows = pl.ds(at * step, step)
        flat = step * n_j
        inputs = tri_in[rows].reshape(flat, width)
        head = dot(inputs, out_w[...])
        opened = gate[rows].reshape(flat, width)
        update[rows] = (opened * head).astype(bf16).reshape(step, n_j, width)
        upstream = cotangent[rows].astype(f32).reshape(flat, width)
        pre = (upstream * head * opened * (1.0 - opened)).astype(bf16)
        pre_back[rows] = pre.reshape(step, n_j, width)
        gate_part[...] += dot_tn(middle_in[rows].reshape(flat, width), pre)
        output_part[...] += dot_tn(inputs, head_back[rows].reshape(flat, width))
        return 0

    lax.fori_loop(0, n_i // step, body, 0, unroll=2)


def vertex_step(n_k, unit):
    size = unit
    while size * 2 <= 64 and n_k % (size * 2) == 0:
        size *= 2
    return size


def left_back_kernel(first, n_blk, tri_back, right_act, *left_out):
    n_i, n_j, width = tri_back.shape
    k_left = left_out[0].shape[1]
    n_k = k_left * n_blk
    last = (first + len(left_out)) * k_left
    k_step = k_left * math.gcd(len(left_out), max(1, 64 // k_left))
    few = max(1, 256 // k_step)
    for k0 in range(first * k_left, last, k_step):

        def rows_sum(at, _, k0=k0):
            rows = pl.ds(at * few, few)
            total = jnp.zeros((few, k_step, width), f32)
            for j in range(n_j):
                start = j * n_k + k0
                total = total + tri_back[rows, j : j + 1, :] * right_act[start : start + k_step, :][None]
            total = total.astype(bf16)
            for s in range(k_step // k_left):
                left_out[k0 // k_left - first + s][rows] = total[:, s * k_left : (s + 1) * k_left]
            return 0

        lax.fori_loop(0, n_i // few, rows_sum, 0)


def right_back_kernel(n_rows, n_blk, tri_back, *refs):
    left_act, refs = refs[:n_blk], refs[n_blk + 1 :]
    keep, send, right_sum = refs
    n_i, n_j, width = tri_back.shape
    k_left = left_act[0].shape[1]
    n_k = k_left * n_blk
    k_right = keep.shape[2]
    unit = math.gcd(k_left, k_right)
    few = 4
    k_step = vertex_step(n_k, k_left)
    for k0 in range(0, n_k, k_step):
        blocks = range(k0 // k_left, (k0 + k_step) // k_left)

        def rows_sum(at, _, k0=k0, blocks=blocks):
            eight = pl.ds(pl.multiple_of(at * 8, 8), 8)
            for half in range(0, 8, few):

                def add(i, totals):
                    some = tri_back[i, eight, :][half : half + few][:, None]
                    return tuple(
                        total + some * left_act[s][i][None] for s, total in zip(blocks, totals)
                    )

                zeros = tuple(jnp.zeros((few, k_left, width), f32) for _ in blocks)
                totals = lax.fori_loop(0, n_i, add, zeros, unroll=16)
                for s, total in zip(blocks, totals):
                    right_sum[pl.ds(at * 8 + half, few), s * k_left : (s + 1) * k_left, :] = total.astype(bf16)
            return 0

        lax.fori_loop(0, n_j // 8, rows_sum, 0)
    for s in range(n_rows):
        for part in range(k_right // unit):
            out = send if s % 2 else keep
            out[s // 2, :, part * unit : (part + 1) * unit, :] = right_sum[
                :, pl.ds(place(n_blk, k_left, k_right, s, part), unit), :
            ]


def weights_kernel(n_rows, n_blk, right_in, left_w, right_w, gate_part, output_part, *refs):
    left_in, refs = refs[:n_blk], refs[n_blk:]
    left_out, refs = refs[:n_blk], refs[n_blk:]
    keep, send, keep_out, send_out, total = refs
    right_out = [(send if s % 2 else keep).at[s // 2] for s in range(n_rows)]
    right_ins = [right_in.at[s] for s in range(n_rows)]
    width = gate_part.shape[0]
    total[:, 4 * width : 5 * width] = gate_part[...]
    total[:, 5 * width :] = output_part[...]
    for inputs_refs, weight, backs, first in (
        (left_in, left_w, left_out, 0),
        (right_ins, right_w, right_out, 2 * width),
    ):
        columns = slice(first, first + 2 * width)
        total[:, columns] = jnp.zeros((width, 2 * width), f32)
        n, k, _ = inputs_refs[0].shape
        step = 16
        flat = step * k
        for inputs_ref, back_ref in zip(inputs_refs, backs):

            def body(at, _, inputs_ref=inputs_ref, back_ref=back_ref, weight=weight, columns=columns, flat=flat):
                rows = pl.ds(at * step, step)
                inputs = inputs_ref[rows].reshape(flat, width)
                lin, sw = gated(inputs, weight[...])
                back = back_ref[rows].reshape(flat, width).astype(f32)
                total[:, columns] += dot_tn(inputs, joined_grad(back, lin, sw))
                return 0

            lax.fori_loop(0, n // step, body, 0, unroll=2)
    size = width // n_rows
    for s in range(n_rows):
        start = pl.multiple_of(lax.bitwise_xor(lax.axis_index("rows"), s) * size, size)
        piece = total[pl.ds(start, size), :]
        if s % 2:
            send_out[s // 2] = piece.astype(bf16)
        else:
            keep_out[s // 2] = piece


def grad_middle_kernel(middle, pre_back, gate_weight, _, grad_middle, mark):
    mark[...] = jnp.zeros_like(mark)
    n_i, n_j, width = middle.shape
    step = 16

    def body(at, _):
        rows = pl.ds(at * step, step)
        flat = step * n_j
        normed, inverse = normalize_raw(middle[rows].reshape(flat, width))
        up = dot_nt(pre_back[rows].reshape(flat, width), gate_weight[...])
        grad_middle[rows] = normalize_back(normed, inverse, up).astype(bf16).reshape(step, n_j, width)
        return 0

    lax.fori_loop(0, n_i // step, body, 0, unroll=2)


def side_kernel(raw, weight, *refs):
    backs, (grad, mark) = refs[:-2], refs[-2:]
    mark[...] = jnp.zeros_like(mark)
    n, k, width = raw.shape
    step = 32
    flat = step * k

    def body(at, _):
        rows = pl.ds(at * step, step)
        normed, inverse = normalize_raw(raw[rows].reshape(flat, width))
        lin, sw = gated(normed.astype(bf16), weight[...])
        back = backs[0][rows].astype(f32)
        for other in backs[1:]:
            back = back + other[rows].astype(f32)
        up = dot_nt(joined_grad(back.reshape(flat, width), lin, sw), weight[...])
        grad[rows] = normalize_back(normed, inverse, up).astype(bf16).reshape(step, k, width)
        return 0

    lax.fori_loop(0, n // step, body, 0, unroll=2 if n // step % 2 == 0 else 1)


def exchange(x, axis, n, bit):
    return lax.ppermute(x, axis, [(a, a ^ bit) for a in range(n)])


def halve_kernel(keep, came, *refs):
    kept, send = refs[-2:]
    for at in range(keep.shape[0]):
        total = keep[at].astype(f32) + came[at].astype(f32)
        if at % 2:
            send[at // 2] = total.astype(bf16)
        else:
            kept[at // 2] = total


def halving_sum(keep, send, axis, n, after):
    came = exchange(send, axis, n, 1)
    bit = 2
    while bit < n:
        half = (keep.shape[0] // 2,) + keep.shape[1:]
        keep, send = call(halve_kernel, "halve", [shape(half, f32), shape(half, bf16)], after=len(after))(
            keep, came, *after
        )
        came = exchange(send, axis, n, bit)
        bit *= 2
    return keep, came, send


def forward_kernel(*refs):
    for source, target in zip(refs[:2], refs[-2:]):
        target[...] = source[...]


def gather_left(block, n, after):
    if n != 4:
        return [(block,)] + [(exchange(block, "blk", n, s),) for s in range(1, n)]
    across = exchange(block, "blk", n, 2)
    beside = exchange(block, "blk", n, 1)
    passed, own = call(forward_kernel, "forward", [shape(block.shape, block.dtype)] * 2, after=len(after))(across, block, *after)
    outer = lax.ppermute(passed, "blk", [(1, 0), (2, 3)])
    inner = lax.ppermute(own, "blk", [(1, 2), (2, 1)])
    return [(block,), (beside,), (across,), (outer, inner)]


def order_kernel(*refs):
    refs[-1][...] = jnp.zeros_like(refs[-1])


def behind(*arrays, cost=2 * 10**10):
    (mark,) = call(order_kernel, "order", [MARK], after=len(arrays), cost=cost)(*arrays)
    return mark


def combine_kernel(n, *refs):
    total = refs[0][0].astype(f32)
    for at in range(1, refs[0].shape[0]):
        total = total + refs[0][at].astype(f32)
    for other in refs[1:n]:
        total = total + other[0].astype(f32)
    refs[-1][0] = total.astype(bf16)


def combine(pieces, after=()):
    (total,) = call(
        functools.partial(combine_kernel, len(pieces)),
        "combine",
        [shape((1,) + pieces[0].shape[1:], bf16)],
        after=len(after),
    )(*pieces, *after)
    return total


def deltas_kernel(n_rows, *refs):
    pieces, outs = [ref.at[0] for ref in refs[:n_rows]], refs[n_rows + 1 :]
    size = pieces[0].shape[0]
    for s, piece in enumerate(pieces):
        start = pl.multiple_of(lax.bitwise_xor(lax.axis_index("rows"), s) * size, size)
        first = 0
        for out in outs:
            last = first + out.shape[1]
            out[pl.ds(start, size), :] = piece[:, first:last].astype(f32)
            first = last


def shape(dims, kind):
    return jax.ShapeDtypeStruct(tuple(dims), kind)


def call(kernel, name, outs, scratch=(), after=0, cost=1000):
    def run(*operands):
        spaces = [pltpu.VMEM] * (len(operands) - after) + [pl.ANY] * after
        held = sum(math.prod(x.shape) * 4 for x in scratch)
        return pl.pallas_call(
            kernel,
            in_specs=[pl.BlockSpec(memory_space=space) for space in spaces],
            out_specs=[pl.BlockSpec(memory_space=pltpu.VMEM)] * len(outs),
            out_shape=outs,
            scratch_shapes=list(scratch),
            compiler_params=pltpu.CompilerParams(vmem_limit_bytes=held + SCOPED),
            cost_estimate=pl.CostEstimate(flops=cost, bytes_accessed=1000, transcendentals=0),
            name=name,
        )(*operands)

    return run


def per_device(
    n_rows,
    n_blk,
    pair_left,
    pair_right,
    pair_middle,
    cotangent,
    left_weight,
    right_weight,
    gate_weight,
    output_weight,
):
    n_i, k_left, width = pair_left.shape
    n_j, k_right, _ = pair_right.shape
    n_k = k_left * n_blk
    right_raw = [pair_right] + [exchange(pair_right, "rows", n_rows, s) for s in range(1, n_rows)]
    middle_shape = (n_i, n_j, width)
    gate, middle_in, head_back, tri_up = call(
        middle_kernel,
        "middle",
        [shape(middle_shape, f32), shape(middle_shape, bf16), shape(middle_shape, bf16), shape(middle_shape, f32)],
        after=1,
    )(pair_middle, cotangent, gate_weight, output_weight, behind(cost=10**9))
    right_act, right_in, *right_flip = call(
        functools.partial(right_kernel, n_rows, n_blk, k_left),
        "right",
        [shape((n_j * n_k, width), f32), shape((n_rows, n_j, k_right, width), bf16)]
        + [shape((k_left, n_j, width), f32)] * n_blk,
    )(*right_raw, right_weight)
    left_raw = gather_left(pair_left, n_blk, (right_in, middle_in))
    left_act, left_in, total = [], [], []
    act_shape = shape(pair_left.shape, f32)
    in_shape = shape(pair_left.shape, bf16)
    for s in range(n_blk - 1):
        act, inputs, total = call(
            functools.partial(left_kernel, len(left_raw[s]), s == 0),
            "left",
            [act_shape, in_shape, shape(middle_shape, f32)],
        )(*left_raw[s], left_weight, right_flip[s], *total)
        left_act.append(act)
        left_in.append(inputs)
        total = [total]
    act, inputs, tri_in, tri_back = call(
        functools.partial(triangle_kernel, len(left_raw[-1]), n_blk > 1),
        "triangle",
        [act_shape, in_shape, shape(middle_shape, bf16), shape(middle_shape, f32)],
    )(*left_raw[-1], left_weight, right_flip[-1], tri_up, *total)
    left_act.append(act)
    left_in.append(inputs)
    half = n_blk // 2
    left_out = []
    for first in (half, 0):
        some = call(
            functools.partial(left_back_kernel, first, n_blk),
            "left_back",
            [shape(pair_left.shape, bf16)] * half,
            after=0,
        )(tri_back, right_act)
        left_out = [*some, *left_out]
    left_back = [left_out[0]] + [exchange(left_out[s], "blk", n_blk, s) for s in range(1, n_blk)]
    right_stack = shape((n_rows // 2,) + pair_right.shape, bf16)
    keep, send = call(
        functools.partial(right_back_kernel, n_rows, n_blk),
        "right_back",
        [right_stack, right_stack],
        scratch=[pltpu.VMEM((n_j, n_k, width), bf16)],
        after=1,
    )(tri_back, *left_act, left_out[0])
    kept, came, sent = halving_sum(keep, send, "rows", n_rows, (behind(*left_back[1:], cost=LEFT_COST),))
    update, pre_back, gate_part, output_part = call(
        heads_kernel,
        "heads",
        [
            shape(middle_shape, bf16),
            shape(middle_shape, bf16),
            shape(gate_weight.shape, f32),
            shape(output_weight.shape, f32),
        ],
        after=1,
    )(tri_in, output_weight, gate, middle_in, head_back, cotangent, left_out[0])
    parts = (n_rows // 2, width // n_rows, 6 * width)
    keep, send = call(
        functools.partial(weights_kernel, n_rows, n_blk),
        "weights",
        [shape(parts, f32), shape(parts, bf16)],
        scratch=[pltpu.VMEM((width, 6 * width), f32)],
    )(right_in, left_weight, right_weight, gate_part, output_part, *left_in, *left_out, keep, send)
    grad_middle, done_middle = call(
        grad_middle_kernel, "grad_middle", [shape(middle_shape, bf16), MARK], after=1
    )(pair_middle, pre_back, gate_weight, send)
    keep, part, _ = halving_sum(keep, send, "rows", n_rows, (done_middle,))
    part = combine([keep, part], (behind(sent),))
    grad_left, done_left = call(side_kernel, "left_side", [shape(pair_left.shape, bf16), MARK])(
        pair_left, left_weight, *left_back
    )
    part = combine([part] + [exchange(part, "blk", n_blk, s) for s in range(1, n_blk)], (done_left,))
    pieces = [part] + [exchange(part, "rows", n_rows, s) for s in range(1, n_rows)]
    grad_right, done_right = call(side_kernel, "right_side", [shape(pair_right.shape, bf16), MARK])(
        pair_right, right_weight, kept.reshape(pair_right.shape), came.reshape(pair_right.shape)
    )
    deltas = call(
        functools.partial(deltas_kernel, n_rows),
        "deltas",
        [shape(x.shape, f32) for x in (left_weight, right_weight, gate_weight, output_weight)],
        after=1,
    )(*pieces, done_right)
    return (
        update,
        grad_left,
        grad_right,
        grad_middle,
        *deltas,
    )


def solution(mesh):
    sides = P(("rep", "rows"), "blk", None)
    right = P(("rep", "blk"), "rows", None)
    return jax.shard_map(
        functools.partial(per_device, mesh.shape["rows"], mesh.shape["blk"]),
        mesh=mesh,
        in_specs=(sides, right, sides, sides, P(), P(), P(), P()),
        out_specs=(sides, sides, right, sides) + (P("rep", None),) * 4,
        check_vma=False,
    )
```

```python
import functools
import math

import jax
import jax.numpy as jnp
from jax import lax
from jax.experimental import pallas as pl
from jax.experimental.pallas import tpu as pltpu
from jax.sharding import PartitionSpec as P

epsilon = 1e-05
f32 = jnp.float32
bf16 = jnp.bfloat16
SCOPED = 6 * 1024 * 1024
LEFT_COST = 2 * 10**8
MARK = jax.ShapeDtypeStruct((8, 128), jnp.float32)


def sigmoid(x):
    return 0.5 * jnp.tanh(0.5 * x) + 0.5


def dot(a, b):
    return lax.dot_general(a, b, (((1,), (0,)), ((), ())), preferred_element_type=f32)


def dot_nt(a, b):
    return lax.dot_general(a, b, (((1,), (1,)), ((), ())), preferred_element_type=f32)


def dot_tn(a, b):
    return lax.dot_general(a, b, (((0,), (0,)), ((), ())), preferred_element_type=f32)


def split(values):
    high = values.astype(bf16)
    return jnp.concatenate([high, (values - high.astype(f32)).astype(bf16)], axis=-1)


def row_mean(parts, width):
    return dot(parts, jnp.full((parts.shape[-1], width), 1.0 / width, bf16))


def normalize(values, mean):
    centred = values - mean
    inverse = lax.rsqrt(row_mean(split(centred * centred), values.shape[-1]) + epsilon)
    return (centred * inverse, inverse)


def normalize_raw(raw):
    return normalize(raw.astype(f32), row_mean(raw, raw.shape[-1]))


def normalize_back(normed, inverse, upstream):
    width = upstream.shape[-1]
    first = row_mean(split(upstream), width)
    second = row_mean(split(upstream * normed), width)
    return inverse * (upstream - first - normed * second)


def gated(inputs, weight):
    pre = dot(inputs, weight)
    width = weight.shape[1] // 2
    return pre[:, :width], sigmoid(pre[:, width:])


def joined_grad(back, lin, sw):
    return jnp.concatenate([back * sw, back * lin * sw * (1.0 - sw)], axis=-1).astype(bf16)


def middle_kernel(middle, cotangent, gate_weight, output_weight, _, gate, middle_in, head_back, tri_up):
    n_i, n_j, width = middle.shape
    step = 16

    def body(at, _):
        rows = pl.ds(at * step, step)
        normed, _ = normalize_raw(middle[rows].reshape(step * n_j, width))
        inputs = normed.astype(bf16)
        opened = sigmoid(dot(inputs, gate_weight[...]))
        back = (cotangent[rows].astype(f32).reshape(step * n_j, width) * opened).astype(bf16)
        gate[rows] = opened.reshape(step, n_j, width)
        middle_in[rows] = inputs.reshape(step, n_j, width)
        head_back[rows] = back.reshape(step, n_j, width)
        up = dot_nt(back, output_weight[...])
        tri_up[rows] = (up - row_mean(split(up), width)).reshape(step, n_j, width)
        return 0

    lax.fori_loop(0, n_i // step, body, 0, unroll=2)


def right_kernel(n_rows, n_blk, k_left, *refs):
    raw, (weight, act_out, in_out, *flip_out) = refs[:n_rows], refs[n_rows:]
    n_j, k_right, width = raw[0].shape
    n_k = k_left * n_blk
    unit = math.gcd(k_left, k_right)
    step = n_j
    for s in range(n_rows):

        def body(at, _, s=s):
            rows = pl.ds(at * step, step)
            normed, _ = normalize_raw(raw[s][rows].reshape(step * k_right, width))
            inputs = normed.astype(bf16)
            in_out[s, rows] = inputs.reshape(step, k_right, width)
            lin, sw = gated(inputs, weight[...])
            act = (sw * lin).astype(bf16).astype(f32).reshape(step, k_right, width)
            for part in range(k_right // unit):
                at_k = place(n_blk, k_left, k_right, s, part)
                for j in range(step):
                    start = pl.multiple_of((at * step + j) * n_k + at_k, unit)
                    act_out[pl.ds(start, unit), :] = act[j, part * unit : (part + 1) * unit]
            return 0

        lax.fori_loop(0, n_j // step, body, 0, unroll=True)

    for s in range(n_blk):

        def flip(k, _, s=s):
            flip_out[s][k] = act_out[pl.ds(s * k_left + k, n_j, stride=n_k), :]
            return 0

        lax.fori_loop(0, k_left, flip, 0, unroll=True)


def place(n_blk, k_left, k_right, piece, part):
    unit = math.gcd(k_left, k_right)
    vertex = lax.bitwise_xor(lax.axis_index("rows"), piece) * k_right + part * unit
    block = vertex // k_left
    at = lax.bitwise_xor(lax.axis_index("blk"), block) * k_left + vertex - block * k_left
    return pl.multiple_of(at, unit)


def project_left(raws, weight, act_out, in_out):
    n_i, k_left, width = raws[0].shape
    step = 32

    def body(at, _):
        rows = pl.ds(at * step, step)
        raw = raws[0][rows]
        if len(raws) > 1:
            place = jnp.full(raw.shape, lax.axis_index("blk"), jnp.int32)
            inner = jnp.logical_or(place == 1, place == 2)
            raw = jnp.where(inner, raws[1][rows].astype(f32), raw.astype(f32)).astype(bf16)
        normed, _ = normalize_raw(raw.reshape(step * k_left, width))
        inputs = normed.astype(bf16)
        in_out[rows] = inputs.reshape(step, k_left, width)
        lin, sw = gated(inputs, weight[...])
        act_out[rows] = (sw * lin).astype(bf16).astype(f32).reshape(step, k_left, width)
        return 0

    lax.fori_loop(0, n_i // step, body, 0, unroll=2)


def add_vertices(rows, act, flip):
    total = act[rows, 0:1, :] * flip[0][None]
    for k in range(1, act.shape[1]):
        total = total + act[rows, k : k + 1, :] * flip[k][None]
    return total


def left_kernel(n_raw, first, *refs):
    raw, (weight, flip, *refs) = refs[:n_raw], refs[n_raw:]
    total_in, (act_out, in_out, total_out) = refs[: 0 if first else 1], refs[0 if first else 1 :]
    n_i, n_j, width = total_out.shape
    step = 8
    project_left(raw, weight, act_out, in_out)

    def body(at, _):
        rows = pl.ds(at * step, step)
        total = add_vertices(rows, act_out, flip)
        total_out[rows] = total if first else total_in[0][rows] + total
        return 0

    lax.fori_loop(0, n_i // step, body, 0)


def triangle_kernel(n_raw, has_total, *refs):
    raw, (left_w, flip, tri_up, *refs) = refs[:n_raw], refs[n_raw:]
    total_in, refs = refs[: 1 if has_total else 0], refs[1 if has_total else 0 :]
    act_out, in_out, tri_in, tri_back = refs
    n_i, n_j, width = tri_in.shape
    step = 8
    project_left(raw, left_w, act_out, in_out)

    def triangle_rows(at, _):
        rows = pl.ds(at * step, step)
        total = add_vertices(rows, act_out, flip)
        if has_total:
            total = total + total_in[0][rows]
        flat = step * n_j
        total = total.reshape(flat, width)
        normed, inverse = normalize(total, row_mean(split(total), width))
        tri_in[rows] = normed.astype(bf16).reshape(step, n_j, width)
        up = tri_up[rows].reshape(flat, width)
        second = row_mean(split(up * normed), width)
        back = inverse * (up - normed * second)
        tri_back[rows] = back.astype(bf16).astype(f32).reshape(step, n_j, width)
        return 0

    lax.fori_loop(0, n_i // step, triangle_rows, 0, unroll=4)


def heads_kernel(tri_in, out_w, gate, middle_in, head_back, cotangent, _, *refs):
    update, pre_back, gate_part, output_part = refs
    n_i, n_j, width = update.shape
    step = 16
    gate_part[...] = jnp.zeros_like(gate_part)
    output_part[...] = jnp.zeros_like(output_part)

    def body(at, _):
        rows = pl.ds(at * step, step)
        flat = step * n_j
        inputs = tri_in[rows].reshape(flat, width)
        head = dot(inputs, out_w[...])
        opened = gate[rows].reshape(flat, width)
        update[rows] = (opened * head).astype(bf16).reshape(step, n_j, width)
        upstream = cotangent[rows].astype(f32).reshape(flat, width)
        pre = (upstream * head * opened * (1.0 - opened)).astype(bf16)
        pre_back[rows] = pre.reshape(step, n_j, width)
        gate_part[...] += dot_tn(middle_in[rows].reshape(flat, width), pre)
        output_part[...] += dot_tn(inputs, head_back[rows].reshape(flat, width))
        return 0

    lax.fori_loop(0, n_i // step, body, 0, unroll=2)


def vertex_step(n_k, unit):
    size = unit
    while size * 2 <= 64 and n_k % (size * 2) == 0:
        size *= 2
    return size


def left_back_kernel(first, n_blk, tri_back, right_act, *left_out):
    n_i, n_j, width = tri_back.shape
    k_left = left_out[0].shape[1]
    n_k = k_left * n_blk
    last = (first + len(left_out)) * k_left
    k_step = k_left * math.gcd(len(left_out), max(1, 64 // k_left))
    few = max(1, 256 // k_step)
    for k0 in range(first * k_left, last, k_step):

        def rows_sum(at, _, k0=k0):
            rows = pl.ds(at * few, few)
            total = jnp.zeros((few, k_step, width), f32)
            for j in range(n_j):
                start = j * n_k + k0
                total = total + tri_back[rows, j : j + 1, :] * right_act[start : start + k_step, :][None]
            total = total.astype(bf16)
            for s in range(k_step // k_left):
                left_out[k0 // k_left - first + s][rows] = total[:, s * k_left : (s + 1) * k_left]
            return 0

        lax.fori_loop(0, n_i // few, rows_sum, 0)


def right_back_kernel(n_rows, n_blk, tri_back, *refs):
    left_act, refs = refs[:n_blk], refs[n_blk + 1 :]
    keep, send, right_sum = refs
    n_i, n_j, width = tri_back.shape
    k_left = left_act[0].shape[1]
    n_k = k_left * n_blk
    k_right = keep.shape[2]
    unit = math.gcd(k_left, k_right)
    few = 4
    k_step = vertex_step(n_k, k_left)
    for k0 in range(0, n_k, k_step):
        blocks = range(k0 // k_left, (k0 + k_step) // k_left)

        def rows_sum(at, _, k0=k0, blocks=blocks):
            eight = pl.ds(pl.multiple_of(at * 8, 8), 8)
            for half in range(0, 8, few):

                def add(i, totals):
                    some = tri_back[i, eight, :][half : half + few][:, None]
                    return tuple(
                        total + some * left_act[s][i][None] for s, total in zip(blocks, totals)
                    )

                zeros = tuple(jnp.zeros((few, k_left, width), f32) for _ in blocks)
                totals = lax.fori_loop(0, n_i, add, zeros, unroll=16)
                for s, total in zip(blocks, totals):
                    right_sum[pl.ds(at * 8 + half, few), s * k_left : (s + 1) * k_left, :] = total.astype(bf16)
            return 0

        lax.fori_loop(0, n_j // 8, rows_sum, 0)
    for s in range(n_rows):
        for part in range(k_right // unit):
            out = send if s % 2 else keep
            out[s // 2, :, part * unit : (part + 1) * unit, :] = right_sum[
                :, pl.ds(place(n_blk, k_left, k_right, s, part), unit), :
            ]


def weights_kernel(n_rows, n_blk, right_in, left_w, right_w, gate_part, output_part, *refs):
    left_in, refs = refs[:n_blk], refs[n_blk:]
    left_out, refs = refs[:n_blk], refs[n_blk:]
    keep, send, keep_out, send_out, total = refs
    right_out = [(send if s % 2 else keep).at[s // 2] for s in range(n_rows)]
    right_ins = [right_in.at[s] for s in range(n_rows)]
    width = gate_part.shape[0]
    total[:, 4 * width : 5 * width] = gate_part[...]
    total[:, 5 * width :] = output_part[...]
    for inputs_refs, weight, backs, first in (
        (left_in, left_w, left_out, 0),
        (right_ins, right_w, right_out, 2 * width),
    ):
        columns = slice(first, first + 2 * width)
        total[:, columns] = jnp.zeros((width, 2 * width), f32)
        n, k, _ = inputs_refs[0].shape
        step = 32
        flat = step * k
        for inputs_ref, back_ref in zip(inputs_refs, backs):

            def body(at, _, inputs_ref=inputs_ref, back_ref=back_ref, weight=weight, columns=columns, flat=flat):
                rows = pl.ds(at * step, step)
                inputs = inputs_ref[rows].reshape(flat, width)
                lin, sw = gated(inputs, weight[...])
                back = back_ref[rows].reshape(flat, width).astype(f32)
                total[:, columns] += dot_tn(inputs, joined_grad(back, lin, sw))
                return 0

            lax.fori_loop(0, n // step, body, 0, unroll=True)
    size = width // n_rows
    for s in range(n_rows):
        start = pl.multiple_of(lax.bitwise_xor(lax.axis_index("rows"), s) * size, size)
        piece = total[pl.ds(start, size), :]
        if s % 2:
            send_out[s // 2] = piece.astype(bf16)
        else:
            keep_out[s // 2] = piece


def grad_middle_kernel(middle, pre_back, gate_weight, _, grad_middle, mark):
    mark[...] = jnp.zeros_like(mark)
    n_i, n_j, width = middle.shape
    step = 16

    def body(at, _):
        rows = pl.ds(at * step, step)
        flat = step * n_j
        normed, inverse = normalize_raw(middle[rows].reshape(flat, width))
        up = dot_nt(pre_back[rows].reshape(flat, width), gate_weight[...])
        grad_middle[rows] = normalize_back(normed, inverse, up).astype(bf16).reshape(step, n_j, width)
        return 0

    lax.fori_loop(0, n_i // step, body, 0, unroll=2)


def side_kernel(raw, weight, *refs):
    backs, (grad, mark) = refs[:-2], refs[-2:]
    mark[...] = jnp.zeros_like(mark)
    n, k, width = raw.shape
    step = 32
    flat = step * k

    def body(at, _):
        rows = pl.ds(at * step, step)
        normed, inverse = normalize_raw(raw[rows].reshape(flat, width))
        lin, sw = gated(normed.astype(bf16), weight[...])
        back = backs[0][rows].astype(f32)
        for other in backs[1:]:
            back = back + other[rows].astype(f32)
        up = dot_nt(joined_grad(back.reshape(flat, width), lin, sw), weight[...])
        grad[rows] = normalize_back(normed, inverse, up).astype(bf16).reshape(step, k, width)
        return 0

    lax.fori_loop(0, n // step, body, 0, unroll=2 if n // step % 2 == 0 else 1)


def exchange(x, axis, n, bit):
    return lax.ppermute(x, axis, [(a, a ^ bit) for a in range(n)])


def halve_kernel(keep, came, *refs):
    kept, send = refs[-2:]
    for at in range(keep.shape[0]):
        total = keep[at].astype(f32) + came[at].astype(f32)
        if at % 2:
            send[at // 2] = total.astype(bf16)
        else:
            kept[at // 2] = total


def halving_sum(keep, send, axis, n, after):
    came = exchange(send, axis, n, 1)
    bit = 2
    while bit < n:
        half = (keep.shape[0] // 2,) + keep.shape[1:]
        keep, send = call(halve_kernel, "halve", [shape(half, f32), shape(half, bf16)], after=len(after))(
            keep, came, *after
        )
        came = exchange(send, axis, n, bit)
        bit *= 2
    return keep, came, send


def forward_kernel(*refs):
    for source, target in zip(refs[:2], refs[-2:]):
        target[...] = source[...]


def gather_left(block, n, after):
    if n != 4:
        return [(block,)] + [(exchange(block, "blk", n, s),) for s in range(1, n)]
    across = exchange(block, "blk", n, 2)
    beside = exchange(block, "blk", n, 1)
    passed, own = call(forward_kernel, "forward", [shape(block.shape, block.dtype)] * 2, after=len(after))(across, block, *after)
    outer = exchange(passed, "blk", n, 1)
    inner = lax.ppermute(own, "blk", [(0, 0), (1, 2), (2, 1), (3, 3)])
    return [(block,), (beside,), (across,), (outer, inner)]


def order_kernel(*refs):
    refs[-1][...] = jnp.zeros_like(refs[-1])


def behind(*arrays, cost=2 * 10**10):
    (mark,) = call(order_kernel, "order", [MARK], after=len(arrays), cost=cost)(*arrays)
    return mark


def combine_kernel(n, *refs):
    total = refs[0][0].astype(f32)
    for at in range(1, refs[0].shape[0]):
        total = total + refs[0][at].astype(f32)
    for other in refs[1:n]:
        total = total + other[0].astype(f32)
    refs[-1][0] = total.astype(bf16)


def combine(pieces, after=()):
    (total,) = call(
        functools.partial(combine_kernel, len(pieces)),
        "combine",
        [shape((1,) + pieces[0].shape[1:], bf16)],
        after=len(after),
    )(*pieces, *after)
    return total


def deltas_kernel(n_rows, *refs):
    pieces, outs = [ref.at[0] for ref in refs[:n_rows]], refs[n_rows + 1 :]
    size = pieces[0].shape[0]
    for s, piece in enumerate(pieces):
        start = pl.multiple_of(lax.bitwise_xor(lax.axis_index("rows"), s) * size, size)
        first = 0
        for out in outs:
            last = first + out.shape[1]
            out[pl.ds(start, size), :] = piece[:, first:last].astype(f32)
            first = last


def shape(dims, kind):
    return jax.ShapeDtypeStruct(tuple(dims), kind)


def call(kernel, name, outs, scratch=(), after=0, cost=1000):
    def run(*operands):
        spaces = [pltpu.VMEM] * (len(operands) - after) + [pl.ANY] * after
        held = sum(math.prod(x.shape) * 4 for x in scratch)
        return pl.pallas_call(
            kernel,
            in_specs=[pl.BlockSpec(memory_space=space) for space in spaces],
            out_specs=[pl.BlockSpec(memory_space=pltpu.VMEM)] * len(outs),
            out_shape=outs,
            scratch_shapes=list(scratch),
            compiler_params=pltpu.CompilerParams(vmem_limit_bytes=held + SCOPED),
            cost_estimate=pl.CostEstimate(flops=cost, bytes_accessed=1000, transcendentals=0),
            name=name,
        )(*operands)

    return run


def per_device(
    n_rows,
    n_blk,
    pair_left,
    pair_right,
    pair_middle,
    cotangent,
    left_weight,
    right_weight,
    gate_weight,
    output_weight,
):
    n_i, k_left, width = pair_left.shape
    n_j, k_right, _ = pair_right.shape
    n_k = k_left * n_blk
    right_raw = [pair_right] + [exchange(pair_right, "rows", n_rows, s) for s in range(1, n_rows)]
    middle_shape = (n_i, n_j, width)
    gate, middle_in, head_back, tri_up = call(
        middle_kernel,
        "middle",
        [shape(middle_shape, f32), shape(middle_shape, bf16), shape(middle_shape, bf16), shape(middle_shape, f32)],
        after=1,
    )(pair_middle, cotangent, gate_weight, output_weight, behind(cost=10**9))
    right_act, right_in, *right_flip = call(
        functools.partial(right_kernel, n_rows, n_blk, k_left),
        "right",
        [shape((n_j * n_k, width), f32), shape((n_rows, n_j, k_right, width), bf16)]
        + [shape((k_left, n_j, width), f32)] * n_blk,
    )(*right_raw, right_weight)
    left_raw = gather_left(pair_left, n_blk, (right_in, middle_in))
    left_act, left_in, total = [], [], []
    act_shape = shape(pair_left.shape, f32)
    in_shape = shape(pair_left.shape, bf16)
    for s in range(n_blk - 1):
        act, inputs, total = call(
            functools.partial(left_kernel, len(left_raw[s]), s == 0),
            "left",
            [act_shape, in_shape, shape(middle_shape, f32)],
        )(*left_raw[s], left_weight, right_flip[s], *total)
        left_act.append(act)
        left_in.append(inputs)
        total = [total]
    act, inputs, tri_in, tri_back = call(
        functools.partial(triangle_kernel, len(left_raw[-1]), n_blk > 1),
        "triangle",
        [act_shape, in_shape, shape(middle_shape, bf16), shape(middle_shape, f32)],
    )(*left_raw[-1], left_weight, right_flip[-1], tri_up, *total)
    left_act.append(act)
    left_in.append(inputs)
    half = n_blk // 2
    left_out = []
    for first in (half, 0):
        some = call(
            functools.partial(left_back_kernel, first, n_blk),
            "left_back",
            [shape(pair_left.shape, bf16)] * half,
            after=0,
        )(tri_back, right_act)
        left_out = [*some, *left_out]
    left_back = [left_out[0]] + [exchange(left_out[s], "blk", n_blk, s) for s in range(1, n_blk)]
    right_stack = shape((n_rows // 2,) + pair_right.shape, bf16)
    keep, send = call(
        functools.partial(right_back_kernel, n_rows, n_blk),
        "right_back",
        [right_stack, right_stack],
        scratch=[pltpu.VMEM((n_j, n_k, width), bf16)],
        after=1,
    )(tri_back, *left_act, left_out[0])
    kept, came, sent = halving_sum(keep, send, "rows", n_rows, (behind(*left_back[1:], cost=LEFT_COST),))
    update, pre_back, gate_part, output_part = call(
        heads_kernel,
        "heads",
        [
            shape(middle_shape, bf16),
            shape(middle_shape, bf16),
            shape(gate_weight.shape, f32),
            shape(output_weight.shape, f32),
        ],
        after=1,
    )(tri_in, output_weight, gate, middle_in, head_back, cotangent, left_out[0])
    parts = (n_rows // 2, width // n_rows, 6 * width)
    keep, send = call(
        functools.partial(weights_kernel, n_rows, n_blk),
        "weights",
        [shape(parts, f32), shape(parts, bf16)],
        scratch=[pltpu.VMEM((width, 6 * width), f32)],
    )(right_in, left_weight, right_weight, gate_part, output_part, *left_in, *left_out, keep, send)
    grad_middle, done_middle = call(
        grad_middle_kernel, "grad_middle", [shape(middle_shape, bf16), MARK], after=1
    )(pair_middle, pre_back, gate_weight, send)
    keep, part, _ = halving_sum(keep, send, "rows", n_rows, (done_middle,))
    part = combine([keep, part], (behind(sent),))
    grad_left, done_left = call(side_kernel, "left_side", [shape(pair_left.shape, bf16), MARK])(
        pair_left, left_weight, *left_back
    )
    part = combine([part] + [exchange(part, "blk", n_blk, s) for s in range(1, n_blk)], (done_left,))
    pieces = [part] + [exchange(part, "rows", n_rows, s) for s in range(1, n_rows)]
    grad_right, done_right = call(side_kernel, "right_side", [shape(pair_right.shape, bf16), MARK])(
        pair_right, right_weight, kept.reshape(pair_right.shape), came.reshape(pair_right.shape)
    )
    deltas = call(
        functools.partial(deltas_kernel, n_rows),
        "deltas",
        [shape(x.shape, f32) for x in (left_weight, right_weight, gate_weight, output_weight)],
        after=1,
    )(*pieces, done_right)
    return (
        update,
        grad_left,
        grad_right,
        grad_middle,
        *deltas,
    )


def solution(mesh):
    sides = P(("rep", "rows"), "blk", None)
    right = P(("rep", "blk"), "rows", None)
    return jax.shard_map(
        functools.partial(per_device, mesh.shape["rows"], mesh.shape["blk"]),
        mesh=mesh,
        in_specs=(sides, right, sides, sides, P(), P(), P(), P()),
        out_specs=(sides, sides, right, sides) + (P("rep", None),) * 4,
        check_vma=False,
    )
```

```python
import functools
import math

import jax
import jax.numpy as jnp
from jax import lax
from jax.experimental import pallas as pl
from jax.experimental.pallas import tpu as pltpu
from jax.sharding import PartitionSpec as P

epsilon = 1e-05
f32 = jnp.float32
bf16 = jnp.bfloat16
SCOPED = 6 * 1024 * 1024
LEFT_COST = 2 * 10**8
MARK = jax.ShapeDtypeStruct((8, 128), jnp.float32)


def sigmoid(x):
    return 0.5 * jnp.tanh(0.5 * x) + 0.5


def dot(a, b):
    return lax.dot_general(a, b, (((1,), (0,)), ((), ())), preferred_element_type=f32)


def dot_nt(a, b):
    return lax.dot_general(a, b, (((1,), (1,)), ((), ())), preferred_element_type=f32)


def dot_tn(a, b):
    return lax.dot_general(a, b, (((0,), (0,)), ((), ())), preferred_element_type=f32)


def split(values):
    high = values.astype(bf16)
    return jnp.concatenate([high, (values - high.astype(f32)).astype(bf16)], axis=-1)


def row_mean(parts, width):
    return dot(parts, jnp.full((parts.shape[-1], width), 1.0 / width, bf16))


def normalize(values, mean):
    centred = values - mean
    inverse = lax.rsqrt(row_mean(split(centred * centred), values.shape[-1]) + epsilon)
    return (centred * inverse, inverse)


def normalize_raw(raw):
    return normalize(raw.astype(f32), row_mean(raw, raw.shape[-1]))


def normalize_back(normed, inverse, upstream):
    width = upstream.shape[-1]
    first = row_mean(split(upstream), width)
    second = row_mean(split(upstream * normed), width)
    return inverse * (upstream - first - normed * second)


def gated(inputs, weight):
    pre = dot(inputs, weight)
    width = weight.shape[1] // 2
    return pre[:, :width], sigmoid(pre[:, width:])


def joined_grad(back, lin, sw):
    return jnp.concatenate([back * sw, back * lin * sw * (1.0 - sw)], axis=-1).astype(bf16)


def middle_kernel(middle, cotangent, gate_weight, output_weight, _, gate, middle_in, head_back, tri_up):
    n_i, n_j, width = middle.shape
    step = 16

    def body(at, _):
        rows = pl.ds(at * step, step)
        normed, _ = normalize_raw(middle[rows].reshape(step * n_j, width))
        inputs = normed.astype(bf16)
        opened = sigmoid(dot(inputs, gate_weight[...]))
        back = (cotangent[rows].astype(f32).reshape(step * n_j, width) * opened).astype(bf16)
        gate[rows] = opened.reshape(step, n_j, width)
        middle_in[rows] = inputs.reshape(step, n_j, width)
        head_back[rows] = back.reshape(step, n_j, width)
        up = dot_nt(back, output_weight[...])
        tri_up[rows] = (up - row_mean(split(up), width)).reshape(step, n_j, width)
        return 0

    lax.fori_loop(0, n_i // step, body, 0, unroll=True)


def right_kernel(n_rows, n_blk, k_left, *refs):
    raw, (weight, act_out, in_out, *flip_out) = refs[:n_rows], refs[n_rows:]
    n_j, k_right, width = raw[0].shape
    n_k = k_left * n_blk
    unit = math.gcd(k_left, k_right)
    step = n_j
    for s in range(n_rows):

        def body(at, _, s=s):
            rows = pl.ds(at * step, step)
            normed, _ = normalize_raw(raw[s][rows].reshape(step * k_right, width))
            inputs = normed.astype(bf16)
            in_out[s, rows] = inputs.reshape(step, k_right, width)
            lin, sw = gated(inputs, weight[...])
            act = (sw * lin).astype(bf16).astype(f32).reshape(step, k_right, width)
            for part in range(k_right // unit):
                at_k = place(n_blk, k_left, k_right, s, part)
                for j in range(step):
                    start = pl.multiple_of((at * step + j) * n_k + at_k, unit)
                    act_out[pl.ds(start, unit), :] = act[j, part * unit : (part + 1) * unit]
            return 0

        lax.fori_loop(0, n_j // step, body, 0, unroll=True)

    for s in range(n_blk):

        def flip(k, _, s=s):
            flip_out[s][k] = act_out[pl.ds(s * k_left + k, n_j, stride=n_k), :]
            return 0

        lax.fori_loop(0, k_left, flip, 0, unroll=True)


def place(n_blk, k_left, k_right, piece, part):
    unit = math.gcd(k_left, k_right)
    vertex = lax.bitwise_xor(lax.axis_index("rows"), piece) * k_right + part * unit
    block = vertex // k_left
    at = lax.bitwise_xor(lax.axis_index("blk"), block) * k_left + vertex - block * k_left
    return pl.multiple_of(at, unit)


def project_left(raws, weight, act_out, in_out):
    n_i, k_left, width = raws[0].shape
    step = 32

    def body(at, _):
        rows = pl.ds(at * step, step)
        raw = raws[0][rows]
        if len(raws) > 1:
            place = jnp.full(raw.shape, lax.axis_index("blk"), jnp.int32)
            inner = jnp.logical_or(place == 1, place == 2)
            raw = jnp.where(inner, raws[1][rows].astype(f32), raw.astype(f32)).astype(bf16)
        normed, _ = normalize_raw(raw.reshape(step * k_left, width))
        inputs = normed.astype(bf16)
        in_out[rows] = inputs.reshape(step, k_left, width)
        lin, sw = gated(inputs, weight[...])
        act_out[rows] = (sw * lin).astype(bf16).astype(f32).reshape(step, k_left, width)
        return 0

    lax.fori_loop(0, n_i // step, body, 0, unroll=True)


def add_vertices(rows, act, flip):
    total = act[rows, 0:1, :] * flip[0][None]
    for k in range(1, act.shape[1]):
        total = total + act[rows, k : k + 1, :] * flip[k][None]
    return total


def left_kernel(n_raw, first, *refs):
    raw, (weight, flip, *refs) = refs[:n_raw], refs[n_raw:]
    total_in, (act_out, in_out, total_out) = refs[: 0 if first else 1], refs[0 if first else 1 :]
    n_i, n_j, width = total_out.shape
    step = 8
    project_left(raw, weight, act_out, in_out)

    def body(at, _):
        rows = pl.ds(at * step, step)
        total = add_vertices(rows, act_out, flip)
        total_out[rows] = total if first else total_in[0][rows] + total
        return 0

    lax.fori_loop(0, n_i // step, body, 0, unroll=2)


def triangle_kernel(n_raw, has_total, *refs):
    raw, (left_w, flip, tri_up, *refs) = refs[:n_raw], refs[n_raw:]
    total_in, refs = refs[: 1 if has_total else 0], refs[1 if has_total else 0 :]
    act_out, in_out, tri_in, tri_back = refs
    n_i, n_j, width = tri_in.shape
    step = 8
    project_left(raw, left_w, act_out, in_out)

    def triangle_rows(at, _):
        rows = pl.ds(at * step, step)
        total = add_vertices(rows, act_out, flip)
        if has_total:
            total = total + total_in[0][rows]
        flat = step * n_j
        total = total.reshape(flat, width)
        normed, inverse = normalize(total, row_mean(split(total), width))
        tri_in[rows] = normed.astype(bf16).reshape(step, n_j, width)
        up = tri_up[rows].reshape(flat, width)
        second = row_mean(split(up * normed), width)
        back = inverse * (up - normed * second)
        tri_back[rows] = back.astype(bf16).astype(f32).reshape(step, n_j, width)
        return 0

    lax.fori_loop(0, n_i // step, triangle_rows, 0, unroll=True)


def heads_kernel(tri_in, out_w, gate, middle_in, head_back, cotangent, _, *refs):
    update, pre_back, gate_part, output_part = refs
    n_i, n_j, width = update.shape
    step = 16
    gate_part[...] = jnp.zeros_like(gate_part)
    output_part[...] = jnp.zeros_like(output_part)

    def body(at, _):
        rows = pl.ds(at * step, step)
        flat = step * n_j
        inputs = tri_in[rows].reshape(flat, width)
        head = dot(inputs, out_w[...])
        opened = gate[rows].reshape(flat, width)
        update[rows] = (opened * head).astype(bf16).reshape(step, n_j, width)
        upstream = cotangent[rows].astype(f32).reshape(flat, width)
        pre = (upstream * head * opened * (1.0 - opened)).astype(bf16)
        pre_back[rows] = pre.reshape(step, n_j, width)
        gate_part[...] += dot_tn(middle_in[rows].reshape(flat, width), pre)
        output_part[...] += dot_tn(inputs, head_back[rows].reshape(flat, width))
        return 0

    lax.fori_loop(0, n_i // step, body, 0, unroll=True)


def vertex_step(n_k, unit):
    size = unit
    while size * 2 <= 64 and n_k % (size * 2) == 0:
        size *= 2
    return size


def left_back_kernel(first, n_blk, tri_back, right_act, *left_out):
    n_i, n_j, width = tri_back.shape
    k_left = left_out[0].shape[1]
    n_k = k_left * n_blk
    last = (first + len(left_out)) * k_left
    k_step = k_left * math.gcd(len(left_out), max(1, 64 // k_left))
    few = max(1, 256 // k_step)
    for k0 in range(first * k_left, last, k_step):

        def rows_sum(at, _, k0=k0):
            rows = pl.ds(at * few, few)
            total = jnp.zeros((few, k_step, width), f32)
            for j in range(n_j):
                start = j * n_k + k0
                total = total + tri_back[rows, j : j + 1, :] * right_act[start : start + k_step, :][None]
            total = total.astype(bf16)
            for s in range(k_step // k_left):
                left_out[k0 // k_left - first + s][rows] = total[:, s * k_left : (s + 1) * k_left]
            return 0

        lax.fori_loop(0, n_i // few, rows_sum, 0, unroll=2)


def right_back_kernel(n_rows, n_blk, tri_back, *refs):
    left_act, refs = refs[:n_blk], refs[n_blk + 1 :]
    keep, send, right_sum = refs
    n_i, n_j, width = tri_back.shape
    k_left = left_act[0].shape[1]
    n_k = k_left * n_blk
    k_right = keep.shape[2]
    unit = math.gcd(k_left, k_right)
    few = 4
    k_step = vertex_step(n_k, k_left)
    for k0 in range(0, n_k, k_step):
        blocks = range(k0 // k_left, (k0 + k_step) // k_left)

        def rows_sum(at, _, k0=k0, blocks=blocks):
            eight = pl.ds(pl.multiple_of(at * 8, 8), 8)
            for half in range(0, 8, few):

                def add(i, totals):
                    some = tri_back[i, eight, :][half : half + few][:, None]
                    return tuple(
                        total + some * left_act[s][i][None] for s, total in zip(blocks, totals)
                    )

                zeros = tuple(jnp.zeros((few, k_left, width), f32) for _ in blocks)
                totals = lax.fori_loop(0, n_i, add, zeros, unroll=32)
                for s, total in zip(blocks, totals):
                    right_sum[pl.ds(at * 8 + half, few), s * k_left : (s + 1) * k_left, :] = total.astype(bf16)
            return 0

        lax.fori_loop(0, n_j // 8, rows_sum, 0)
    for s in range(n_rows):
        for part in range(k_right // unit):
            out = send if s % 2 else keep
            out[s // 2, :, part * unit : (part + 1) * unit, :] = right_sum[
                :, pl.ds(place(n_blk, k_left, k_right, s, part), unit), :
            ]


def weights_kernel(n_rows, n_blk, right_in, left_w, right_w, gate_part, output_part, *refs):
    left_in, refs = refs[:n_blk], refs[n_blk:]
    left_out, refs = refs[:n_blk], refs[n_blk:]
    keep, send, keep_out, send_out, total = refs
    right_out = [(send if s % 2 else keep).at[s // 2] for s in range(n_rows)]
    right_ins = [right_in.at[s] for s in range(n_rows)]
    width = gate_part.shape[0]
    total[:, 4 * width : 5 * width] = gate_part[...]
    total[:, 5 * width :] = output_part[...]
    for inputs_refs, weight, backs, first in (
        (left_in, left_w, left_out, 0),
        (right_ins, right_w, right_out, 2 * width),
    ):
        columns = slice(first, first + 2 * width)
        total[:, columns] = jnp.zeros((width, 2 * width), f32)
        n, k, _ = inputs_refs[0].shape
        step = 32
        flat = step * k
        for inputs_ref, back_ref in zip(inputs_refs, backs):

            def body(at, _, inputs_ref=inputs_ref, back_ref=back_ref, weight=weight, columns=columns, flat=flat):
                rows = pl.ds(at * step, step)
                inputs = inputs_ref[rows].reshape(flat, width)
                lin, sw = gated(inputs, weight[...])
                back = back_ref[rows].reshape(flat, width).astype(f32)
                total[:, columns] += dot_tn(inputs, joined_grad(back, lin, sw))
                return 0

            lax.fori_loop(0, n // step, body, 0, unroll=True)
    size = width // n_rows
    for s in range(n_rows):
        start = pl.multiple_of(lax.bitwise_xor(lax.axis_index("rows"), s) * size, size)
        piece = total[pl.ds(start, size), :]
        if s % 2:
            send_out[s // 2] = piece.astype(bf16)
        else:
            keep_out[s // 2] = piece


def grad_middle_kernel(middle, pre_back, gate_weight, _, grad_middle, mark):
    mark[...] = jnp.zeros_like(mark)
    n_i, n_j, width = middle.shape
    step = 16

    def body(at, _):
        rows = pl.ds(at * step, step)
        flat = step * n_j
        normed, inverse = normalize_raw(middle[rows].reshape(flat, width))
        up = dot_nt(pre_back[rows].reshape(flat, width), gate_weight[...])
        grad_middle[rows] = normalize_back(normed, inverse, up).astype(bf16).reshape(step, n_j, width)
        return 0

    lax.fori_loop(0, n_i // step, body, 0, unroll=True)


def side_kernel(raw, weight, *refs):
    backs, (grad, mark) = refs[:-2], refs[-2:]
    mark[...] = jnp.zeros_like(mark)
    n, k, width = raw.shape
    step = 32
    flat = step * k

    def body(at, _):
        rows = pl.ds(at * step, step)
        normed, inverse = normalize_raw(raw[rows].reshape(flat, width))
        lin, sw = gated(normed.astype(bf16), weight[...])
        back = backs[0][rows].astype(f32)
        for other in backs[1:]:
            back = back + other[rows].astype(f32)
        up = dot_nt(joined_grad(back.reshape(flat, width), lin, sw), weight[...])
        grad[rows] = normalize_back(normed, inverse, up).astype(bf16).reshape(step, k, width)
        return 0

    lax.fori_loop(0, n // step, body, 0, unroll=True)


def exchange(x, axis, n, bit):
    return lax.ppermute(x, axis, [(a, a ^ bit) for a in range(n)])


def halve_kernel(keep, came, *refs):
    kept, send = refs[-2:]
    for at in range(keep.shape[0]):
        total = keep[at].astype(f32) + came[at].astype(f32)
        if at % 2:
            send[at // 2] = total.astype(bf16)
        else:
            kept[at // 2] = total


def halving_sum(keep, send, axis, n, after):
    came = exchange(send, axis, n, 1)
    bit = 2
    while bit < n:
        half = (keep.shape[0] // 2,) + keep.shape[1:]
        keep, send = call(halve_kernel, "halve", [shape(half, f32), shape(half, bf16)], after=len(after))(
            keep, came, *after
        )
        came = exchange(send, axis, n, bit)
        bit *= 2
    return keep, came, send


def forward_kernel(*refs):
    for source, target in zip(refs[:2], refs[-2:]):
        target[...] = source[...]


def gather_left(block, n, after):
    if n != 4:
        return [(block,)] + [(exchange(block, "blk", n, s),) for s in range(1, n)]
    across = exchange(block, "blk", n, 2)
    beside = exchange(block, "blk", n, 1)
    passed, own = call(forward_kernel, "forward", [shape(block.shape, block.dtype)] * 2, after=len(after))(across, block, *after)
    outer = exchange(passed, "blk", n, 1)
    inner = lax.ppermute(own, "blk", [(0, 0), (1, 2), (2, 1), (3, 3)])
    return [(block,), (beside,), (across,), (outer, inner)]


def order_kernel(*refs):
    refs[-1][...] = jnp.zeros_like(refs[-1])


def behind(*arrays, cost=2 * 10**10):
    (mark,) = call(order_kernel, "order", [MARK], after=len(arrays), cost=cost)(*arrays)
    return mark


def combine_kernel(n, *refs):
    total = refs[0][0].astype(f32)
    for at in range(1, refs[0].shape[0]):
        total = total + refs[0][at].astype(f32)
    for other in refs[1:n]:
        total = total + other[0].astype(f32)
    refs[-1][0] = total.astype(bf16)


def combine(pieces, after=()):
    (total,) = call(
        functools.partial(combine_kernel, len(pieces)),
        "combine",
        [shape((1,) + pieces[0].shape[1:], bf16)],
        after=len(after),
    )(*pieces, *after)
    return total


def everywhere_sum(part, axis, n, after):
    bit = 1
    while bit < n:
        part = combine([part, exchange(part, axis, n, bit)], after[:1])
        after = after[1:]
        bit *= 2
    return part


def stack_kernel(own, came, both):
    both[0 : own.shape[0]] = own[...]
    both[own.shape[0] :] = came[...]


def gather_doubling(part, axis, n):
    came = exchange(part, axis, n, 1)
    bit = 2
    while bit < n:
        both = shape((2 * part.shape[0],) + part.shape[1:], part.dtype)
        (part,) = call(stack_kernel, "stack", [both])(part, came)
        came = exchange(part, axis, n, bit)
        bit *= 2
    return part, came


def deltas_kernel(*refs):
    stacks, outs = refs[:2], refs[2:]
    pieces = [stack.at[at] for stack in stacks for at in range(stack.shape[0])]
    size = pieces[0].shape[0]
    for s, piece in enumerate(pieces):
        start = pl.multiple_of(lax.bitwise_xor(lax.axis_index("rows"), s) * size, size)
        first = 0
        for out in outs:
            last = first + out.shape[1]
            out[pl.ds(start, size), :] = piece[:, first:last].astype(f32)
            first = last


def shape(dims, kind):
    return jax.ShapeDtypeStruct(tuple(dims), kind)


def call(kernel, name, outs, scratch=(), after=0, cost=1000):
    def run(*operands):
        spaces = [pltpu.VMEM] * (len(operands) - after) + [pl.ANY] * after
        held = sum(math.prod(x.shape) * 4 for x in scratch)
        return pl.pallas_call(
            kernel,
            in_specs=[pl.BlockSpec(memory_space=space) for space in spaces],
            out_specs=[pl.BlockSpec(memory_space=pltpu.VMEM)] * len(outs),
            out_shape=outs,
            scratch_shapes=list(scratch),
            compiler_params=pltpu.CompilerParams(vmem_limit_bytes=held + SCOPED),
            cost_estimate=pl.CostEstimate(flops=cost, bytes_accessed=1000, transcendentals=0),
            name=name,
        )(*operands)

    return run


def per_device(
    n_rows,
    n_blk,
    pair_left,
    pair_right,
    pair_middle,
    cotangent,
    left_weight,
    right_weight,
    gate_weight,
    output_weight,
):
    n_i, k_left, width = pair_left.shape
    n_j, k_right, _ = pair_right.shape
    n_k = k_left * n_blk
    right_raw = [pair_right] + [exchange(pair_right, "rows", n_rows, s) for s in range(1, n_rows)]
    middle_shape = (n_i, n_j, width)
    gate, middle_in, head_back, tri_up = call(
        middle_kernel,
        "middle",
        [shape(middle_shape, f32), shape(middle_shape, bf16), shape(middle_shape, bf16), shape(middle_shape, f32)],
        after=1,
    )(pair_middle, cotangent, gate_weight, output_weight, behind(cost=10**9))
    right_act, right_in, *right_flip = call(
        functools.partial(right_kernel, n_rows, n_blk, k_left),
        "right",
        [shape((n_j * n_k, width), f32), shape((n_rows, n_j, k_right, width), bf16)]
        + [shape((k_left, n_j, width), f32)] * n_blk,
    )(*right_raw, right_weight)
    left_raw = gather_left(pair_left, n_blk, (right_in, middle_in))
    left_act, left_in, total = [], [], []
    act_shape = shape(pair_left.shape, f32)
    in_shape = shape(pair_left.shape, bf16)
    for s in range(n_blk - 1):
        act, inputs, total = call(
            functools.partial(left_kernel, len(left_raw[s]), s == 0),
            "left",
            [act_shape, in_shape, shape(middle_shape, f32)],
        )(*left_raw[s], left_weight, right_flip[s], *total)
        left_act.append(act)
        left_in.append(inputs)
        total = [total]
    act, inputs, tri_in, tri_back = call(
        functools.partial(triangle_kernel, len(left_raw[-1]), n_blk > 1),
        "triangle",
        [act_shape, in_shape, shape(middle_shape, bf16), shape(middle_shape, f32)],
    )(*left_raw[-1], left_weight, right_flip[-1], tri_up, *total)
    left_act.append(act)
    left_in.append(inputs)
    half = n_blk // 2
    left_out = []
    for first in (half, 0):
        some = call(
            functools.partial(left_back_kernel, first, n_blk),
            "left_back",
            [shape(pair_left.shape, bf16)] * half,
            after=0,
        )(tri_back, right_act)
        left_out = [*some, *left_out]
    left_back = [left_out[0]] + [exchange(left_out[s], "blk", n_blk, s) for s in range(1, n_blk)]
    right_stack = shape((n_rows // 2,) + pair_right.shape, bf16)
    keep, send = call(
        functools.partial(right_back_kernel, n_rows, n_blk),
        "right_back",
        [right_stack, right_stack],
        scratch=[pltpu.VMEM((n_j, n_k, width), bf16)],
        after=1,
    )(tri_back, *left_act, left_out[0])
    kept, came, sent = halving_sum(keep, send, "rows", n_rows, (behind(*left_back[1:], cost=LEFT_COST),))
    update, pre_back, gate_part, output_part = call(
        heads_kernel,
        "heads",
        [
            shape(middle_shape, bf16),
            shape(middle_shape, bf16),
            shape(gate_weight.shape, f32),
            shape(output_weight.shape, f32),
        ],
        after=1,
    )(tri_in, output_weight, gate, middle_in, head_back, cotangent, left_out[0])
    parts = (n_rows // 2, width // n_rows, 6 * width)
    keep, send = call(
        functools.partial(weights_kernel, n_rows, n_blk),
        "weights",
        [shape(parts, f32), shape(parts, bf16)],
        scratch=[pltpu.VMEM((width, 6 * width), f32)],
    )(right_in, left_weight, right_weight, gate_part, output_part, *left_in, *left_out, keep, send)
    grad_middle, done_middle = call(
        grad_middle_kernel, "grad_middle", [shape(middle_shape, bf16), MARK], after=1
    )(pair_middle, pre_back, gate_weight, send)
    keep, part, _ = halving_sum(keep, send, "rows", n_rows, (done_middle,))
    part = combine([keep, part], (behind(sent),))
    grad_left, done_left = call(side_kernel, "left_side", [shape(pair_left.shape, bf16), MARK])(
        pair_left, left_weight, *left_back
    )
    grad_right, done_right = call(side_kernel, "right_side", [shape(pair_right.shape, bf16), MARK])(
        pair_right, right_weight, kept.reshape(pair_right.shape), came.reshape(pair_right.shape)
    )
    part = everywhere_sum(part, "blk", n_blk, (done_left, done_right))
    pieces = gather_doubling(part, "rows", n_rows)
    deltas = call(
        deltas_kernel,
        "deltas",
        [shape(x.shape, f32) for x in (left_weight, right_weight, gate_weight, output_weight)],
    )(*pieces)
    return (
        update,
        grad_left,
        grad_right,
        grad_middle,
        *deltas,
    )


def solution(mesh):
    sides = P(("rep", "rows"), "blk", None)
    right = P(("rep", "blk"), "rows", None)
    return jax.shard_map(
        functools.partial(per_device, mesh.shape["rows"], mesh.shape["blk"]),
        mesh=mesh,
        in_specs=(sides, right, sides, sides, P(), P(), P(), P()),
        out_specs=(sides, sides, right, sides) + (P("rep", None),) * 4,
        check_vma=False,
    )
```

```python
import functools
import math

import jax
import jax.numpy as jnp
from jax import lax
from jax.experimental import pallas as pl
from jax.experimental.pallas import tpu as pltpu
from jax.sharding import PartitionSpec as P

epsilon = 1e-05
f32 = jnp.float32
bf16 = jnp.bfloat16
SCOPED = 6 * 1024 * 1024
LEFT_COST = 2 * 10**8
MARK = jax.ShapeDtypeStruct((8, 128), jnp.float32)


def sigmoid(x):
    return 0.5 * jnp.tanh(0.5 * x) + 0.5


def dot(a, b):
    return lax.dot_general(a, b, (((1,), (0,)), ((), ())), preferred_element_type=f32)


def dot_nt(a, b):
    return lax.dot_general(a, b, (((1,), (1,)), ((), ())), preferred_element_type=f32)


def dot_tn(a, b):
    return lax.dot_general(a, b, (((0,), (0,)), ((), ())), preferred_element_type=f32)


def split(values):
    high = values.astype(bf16)
    return jnp.concatenate([high, (values - high.astype(f32)).astype(bf16)], axis=-1)


def row_mean(parts, width):
    return dot(parts, jnp.full((parts.shape[-1], width), 1.0 / width, bf16))


def normalize(values, mean):
    centred = values - mean
    inverse = lax.rsqrt(row_mean(split(centred * centred), values.shape[-1]) + epsilon)
    return (centred * inverse, inverse)


def normalize_raw(raw):
    return normalize(raw.astype(f32), row_mean(raw, raw.shape[-1]))


def normalize_back(normed, inverse, upstream):
    width = upstream.shape[-1]
    first = row_mean(split(upstream), width)
    second = row_mean(split(upstream * normed), width)
    return inverse * (upstream - first - normed * second)


def gated(inputs, weight):
    pre = dot(inputs, weight)
    width = weight.shape[1] // 2
    return pre[:, :width], sigmoid(pre[:, width:])


def joined_grad(back, lin, sw):
    return jnp.concatenate([back * sw, back * lin * sw * (1.0 - sw)], axis=-1).astype(bf16)


def middle_kernel(middle, cotangent, gate_weight, output_weight, _, gate, middle_in, head_back, tri_up):
    n_i, n_j, width = middle.shape
    step = 16

    def body(at, _):
        rows = pl.ds(at * step, step)
        normed, _ = normalize_raw(middle[rows].reshape(step * n_j, width))
        inputs = normed.astype(bf16)
        opened = sigmoid(dot(inputs, gate_weight[...]))
        back = (cotangent[rows].astype(f32).reshape(step * n_j, width) * opened).astype(bf16)
        gate[rows] = opened.reshape(step, n_j, width)
        middle_in[rows] = inputs.reshape(step, n_j, width)
        head_back[rows] = back.reshape(step, n_j, width)
        up = dot_nt(back, output_weight[...])
        tri_up[rows] = (up - row_mean(split(up), width)).reshape(step, n_j, width)
        return 0

    lax.fori_loop(0, n_i // step, body, 0, unroll=True)


def right_kernel(n_rows, n_blk, k_left, *refs):
    raw = [stack.at[at] for stack in refs[:2] for at in range(stack.shape[0])]
    weight, act_out, in_out, *flip_out = refs[2:]
    n_j, k_right, width = raw[0].shape
    n_k = k_left * n_blk
    unit = math.gcd(k_left, k_right)
    step = n_j
    for s in range(n_rows):

        def body(at, _, s=s):
            rows = pl.ds(at * step, step)
            normed, _ = normalize_raw(raw[s][rows].reshape(step * k_right, width))
            inputs = normed.astype(bf16)
            in_out[s, rows] = inputs.reshape(step, k_right, width)
            lin, sw = gated(inputs, weight[...])
            act = (sw * lin).astype(bf16).astype(f32).reshape(step, k_right, width)
            for part in range(k_right // unit):
                at_k = place(n_blk, k_left, k_right, s, part)
                for j in range(step):
                    start = pl.multiple_of((at * step + j) * n_k + at_k, unit)
                    act_out[pl.ds(start, unit), :] = act[j, part * unit : (part + 1) * unit]
            return 0

        lax.fori_loop(0, n_j // step, body, 0, unroll=True)

    for s in range(n_blk):

        def flip(k, _, s=s):
            flip_out[s][k] = act_out[pl.ds(s * k_left + k, n_j, stride=n_k), :]
            return 0

        lax.fori_loop(0, k_left, flip, 0, unroll=True)


def place(n_blk, k_left, k_right, piece, part):
    unit = math.gcd(k_left, k_right)
    vertex = lax.bitwise_xor(lax.axis_index("rows"), piece) * k_right + part * unit
    block = vertex // k_left
    at = lax.bitwise_xor(lax.axis_index("blk"), block) * k_left + vertex - block * k_left
    return pl.multiple_of(at, unit)


def project_left(raws, weight, act_out, in_out):
    n_i, k_left, width = raws[0].shape
    step = 32

    def body(at, _):
        rows = pl.ds(at * step, step)
        raw = raws[0][rows]
        if len(raws) > 1:
            place = jnp.full(raw.shape, lax.axis_index("blk"), jnp.int32)
            inner = jnp.logical_or(place == 1, place == 2)
            raw = jnp.where(inner, raws[1][rows].astype(f32), raw.astype(f32)).astype(bf16)
        normed, _ = normalize_raw(raw.reshape(step * k_left, width))
        inputs = normed.astype(bf16)
        in_out[rows] = inputs.reshape(step, k_left, width)
        lin, sw = gated(inputs, weight[...])
        act_out[rows] = (sw * lin).astype(bf16).astype(f32).reshape(step, k_left, width)
        return 0

    lax.fori_loop(0, n_i // step, body, 0, unroll=True)


def add_vertices(rows, act, flip):
    total = act[rows, 0:1, :] * flip[0][None]
    for k in range(1, act.shape[1]):
        total = total + act[rows, k : k + 1, :] * flip[k][None]
    return total


def left_kernel(n_raw, first, *refs):
    raw, (weight, flip, *refs) = refs[:n_raw], refs[n_raw:]
    total_in, (act_out, in_out, total_out) = refs[: 0 if first else 1], refs[0 if first else 1 :]
    n_i, n_j, width = total_out.shape
    step = 8
    project_left(raw, weight, act_out, in_out)

    def body(at, _):
        rows = pl.ds(at * step, step)
        total = add_vertices(rows, act_out, flip)
        total_out[rows] = total if first else total_in[0][rows] + total
        return 0

    lax.fori_loop(0, n_i // step, body, 0, unroll=2)


def triangle_kernel(n_raw, has_total, *refs):
    raw, (left_w, flip, tri_up, *refs) = refs[:n_raw], refs[n_raw:]
    total_in, refs = refs[: 1 if has_total else 0], refs[1 if has_total else 0 :]
    act_out, in_out, tri_in, tri_back = refs
    n_i, n_j, width = tri_in.shape
    step = 8
    project_left(raw, left_w, act_out, in_out)

    def triangle_rows(at, _):
        rows = pl.ds(at * step, step)
        total = add_vertices(rows, act_out, flip)
        if has_total:
            total = total + total_in[0][rows]
        flat = step * n_j
        total = total.reshape(flat, width)
        normed, inverse = normalize(total, row_mean(split(total), width))
        tri_in[rows] = normed.astype(bf16).reshape(step, n_j, width)
        up = tri_up[rows].reshape(flat, width)
        second = row_mean(split(up * normed), width)
        back = inverse * (up - normed * second)
        tri_back[rows] = back.astype(bf16).astype(f32).reshape(step, n_j, width)
        return 0

    lax.fori_loop(0, n_i // step, triangle_rows, 0, unroll=True)


def heads_kernel(tri_in, out_w, gate, middle_in, head_back, cotangent, _, *refs):
    update, pre_back, gate_part, output_part = refs
    n_i, n_j, width = update.shape
    step = 16
    gate_part[...] = jnp.zeros_like(gate_part)
    output_part[...] = jnp.zeros_like(output_part)

    def body(at, _):
        rows = pl.ds(at * step, step)
        flat = step * n_j
        inputs = tri_in[rows].reshape(flat, width)
        head = dot(inputs, out_w[...])
        opened = gate[rows].reshape(flat, width)
        update[rows] = (opened * head).astype(bf16).reshape(step, n_j, width)
        upstream = cotangent[rows].astype(f32).reshape(flat, width)
        pre = (upstream * head * opened * (1.0 - opened)).astype(bf16)
        pre_back[rows] = pre.reshape(step, n_j, width)
        gate_part[...] += dot_tn(middle_in[rows].reshape(flat, width), pre)
        output_part[...] += dot_tn(inputs, head_back[rows].reshape(flat, width))
        return 0

    lax.fori_loop(0, n_i // step, body, 0, unroll=True)


def vertex_step(n_k, unit):
    size = unit
    while size * 2 <= 64 and n_k % (size * 2) == 0:
        size *= 2
    return size


def left_back_kernel(first, n_blk, tri_back, right_act, *left_out):
    n_i, n_j, width = tri_back.shape
    k_left = left_out[0].shape[1]
    n_k = k_left * n_blk
    last = (first + len(left_out)) * k_left
    k_step = k_left * math.gcd(len(left_out), max(1, 64 // k_left))
    few = max(1, 256 // k_step)
    for k0 in range(first * k_left, last, k_step):

        def rows_sum(at, _, k0=k0):
            rows = pl.ds(at * few, few)
            total = jnp.zeros((few, k_step, width), f32)
            for j in range(n_j):
                start = j * n_k + k0
                total = total + tri_back[rows, j : j + 1, :] * right_act[start : start + k_step, :][None]
            total = total.astype(bf16)
            for s in range(k_step // k_left):
                left_out[k0 // k_left - first + s][rows] = total[:, s * k_left : (s + 1) * k_left]
            return 0

        lax.fori_loop(0, n_i // few, rows_sum, 0, unroll=2)


def right_back_kernel(n_rows, n_blk, tri_back, *refs):
    left_act, refs = refs[:n_blk], refs[n_blk + 1 :]
    keep, send, right_sum = refs
    n_i, n_j, width = tri_back.shape
    k_left = left_act[0].shape[1]
    n_k = k_left * n_blk
    k_right = keep.shape[2]
    unit = math.gcd(k_left, k_right)
    few = 4
    k_step = vertex_step(n_k, k_left)
    for k0 in range(0, n_k, k_step):
        blocks = range(k0 // k_left, (k0 + k_step) // k_left)

        def rows_sum(at, _, k0=k0, blocks=blocks):
            eight = pl.ds(pl.multiple_of(at * 8, 8), 8)
            for half in range(0, 8, few):

                def add(i, totals):
                    some = tri_back[i, eight, :][half : half + few][:, None]
                    return tuple(
                        total + some * left_act[s][i][None] for s, total in zip(blocks, totals)
                    )

                zeros = tuple(jnp.zeros((few, k_left, width), f32) for _ in blocks)
                totals = lax.fori_loop(0, n_i, add, zeros, unroll=32)
                for s, total in zip(blocks, totals):
                    right_sum[pl.ds(at * 8 + half, few), s * k_left : (s + 1) * k_left, :] = total.astype(bf16)
            return 0

        lax.fori_loop(0, n_j // 8, rows_sum, 0)
    for s in range(n_rows):
        for part in range(k_right // unit):
            out = send if s % 2 else keep
            out[s // 2, :, part * unit : (part + 1) * unit, :] = right_sum[
                :, pl.ds(place(n_blk, k_left, k_right, s, part), unit), :
            ]


def weights_kernel(n_rows, n_blk, right_in, left_w, right_w, gate_part, output_part, *refs):
    left_in, refs = refs[:n_blk], refs[n_blk:]
    left_out, refs = refs[:n_blk], refs[n_blk:]
    keep, send, keep_out, send_out, total = refs
    right_out = [(send if s % 2 else keep).at[s // 2] for s in range(n_rows)]
    right_ins = [right_in.at[s] for s in range(n_rows)]
    width = gate_part.shape[0]
    total[:, 4 * width : 5 * width] = gate_part[...]
    total[:, 5 * width :] = output_part[...]
    for inputs_refs, weight, backs, first in (
        (left_in, left_w, left_out, 0),
        (right_ins, right_w, right_out, 2 * width),
    ):
        columns = slice(first, first + 2 * width)
        total[:, columns] = jnp.zeros((width, 2 * width), f32)
        n, k, _ = inputs_refs[0].shape
        step = 32
        flat = step * k
        for inputs_ref, back_ref in zip(inputs_refs, backs):

            def body(at, _, inputs_ref=inputs_ref, back_ref=back_ref, weight=weight, columns=columns, flat=flat):
                rows = pl.ds(at * step, step)
                inputs = inputs_ref[rows].reshape(flat, width)
                lin, sw = gated(inputs, weight[...])
                back = back_ref[rows].reshape(flat, width).astype(f32)
                total[:, columns] += dot_tn(inputs, joined_grad(back, lin, sw))
                return 0

            lax.fori_loop(0, n // step, body, 0, unroll=True)
    size = width // n_rows
    for s in range(n_rows):
        start = pl.multiple_of(lax.bitwise_xor(lax.axis_index("rows"), s) * size, size)
        piece = total[pl.ds(start, size), :]
        if s % 2:
            send_out[s // 2] = piece.astype(bf16)
        else:
            keep_out[s // 2] = piece


def grad_middle_kernel(middle, pre_back, gate_weight, _, grad_middle, mark):
    mark[...] = jnp.zeros_like(mark)
    n_i, n_j, width = middle.shape
    step = 16

    def body(at, _):
        rows = pl.ds(at * step, step)
        flat = step * n_j
        normed, inverse = normalize_raw(middle[rows].reshape(flat, width))
        up = dot_nt(pre_back[rows].reshape(flat, width), gate_weight[...])
        grad_middle[rows] = normalize_back(normed, inverse, up).astype(bf16).reshape(step, n_j, width)
        return 0

    lax.fori_loop(0, n_i // step, body, 0, unroll=True)


def side_kernel(raw, weight, *refs):
    backs, (grad, mark) = refs[:-2], refs[-2:]
    mark[...] = jnp.zeros_like(mark)
    n, k, width = raw.shape
    step = 32
    flat = step * k

    def body(at, _):
        rows = pl.ds(at * step, step)
        normed, inverse = normalize_raw(raw[rows].reshape(flat, width))
        lin, sw = gated(normed.astype(bf16), weight[...])
        back = backs[0][rows].astype(f32)
        for other in backs[1:]:
            back = back + other[rows].astype(f32)
        up = dot_nt(joined_grad(back.reshape(flat, width), lin, sw), weight[...])
        grad[rows] = normalize_back(normed, inverse, up).astype(bf16).reshape(step, k, width)
        return 0

    lax.fori_loop(0, n // step, body, 0, unroll=True)


def exchange(x, axis, n, bit):
    return lax.ppermute(x, axis, [(a, a ^ bit) for a in range(n)])


def halve_kernel(keep, came, *refs):
    kept, send = refs[-2:]
    for at in range(keep.shape[0]):
        total = keep[at].astype(f32) + came[at].astype(f32)
        if at % 2:
            send[at // 2] = total.astype(bf16)
        else:
            kept[at // 2] = total


def halving_sum(keep, send, axis, n, after):
    came = exchange(send, axis, n, 1)
    bit = 2
    while bit < n:
        half = (keep.shape[0] // 2,) + keep.shape[1:]
        keep, send = call(halve_kernel, "halve", [shape(half, f32), shape(half, bf16)], after=len(after))(
            keep, came, *after
        )
        came = exchange(send, axis, n, bit)
        bit *= 2
    return keep, came, send


def forward_kernel(*refs):
    for source, target in zip(refs[:2], refs[-2:]):
        target[...] = source[...]


def gather_left(block, n, after):
    if n != 4:
        return [(block,)] + [(exchange(block, "blk", n, s),) for s in range(1, n)]
    across = exchange(block, "blk", n, 2)
    beside = exchange(block, "blk", n, 1)
    passed, own = call(forward_kernel, "forward", [shape(block.shape, block.dtype)] * 2, after=len(after))(across, block, *after)
    outer = exchange(passed, "blk", n, 1)
    inner = lax.ppermute(own, "blk", [(0, 0), (1, 2), (2, 1), (3, 3)])
    return [(block,), (beside,), (across,), (outer, inner)]


def order_kernel(*refs):
    refs[-1][...] = jnp.zeros_like(refs[-1])


def behind(*arrays, cost=2 * 10**10):
    (mark,) = call(order_kernel, "order", [MARK], after=len(arrays), cost=cost)(*arrays)
    return mark


def combine_kernel(n, *refs):
    totals = [ref[0].astype(f32) for ref in refs[:n]]
    while len(totals) > 1:
        pairs = [a + b for a, b in zip(totals[::2], totals[1::2])]
        totals = pairs + totals[2 * len(pairs) :]
    refs[-1][0] = totals[0].astype(bf16)


def combine(pieces, after=()):
    (total,) = call(
        functools.partial(combine_kernel, len(pieces)),
        "combine",
        [shape((1,) + pieces[0].shape[1:], bf16)],
        after=len(after),
    )(*pieces, *after)
    return total


def stack_kernel(own, came, both):
    both[0 : own.shape[0]] = own[...]
    both[own.shape[0] :] = came[...]


def gather_doubling(part, axis, n):
    came = exchange(part, axis, n, 1)
    bit = 2
    while bit < n:
        both = shape((2 * part.shape[0],) + part.shape[1:], part.dtype)
        (part,) = call(stack_kernel, "stack", [both])(part, came)
        came = exchange(part, axis, n, bit)
        bit *= 2
    return part, came


def deltas_kernel(n_rows, *refs):
    pieces, outs = [ref.at[0] for ref in refs[:n_rows]], refs[n_rows + 1 :]
    size = pieces[0].shape[0]
    for s, piece in enumerate(pieces):
        start = pl.multiple_of(lax.bitwise_xor(lax.axis_index("rows"), s) * size, size)
        first = 0
        for out in outs:
            last = first + out.shape[1]
            out[pl.ds(start, size), :] = piece[:, first:last].astype(f32)
            first = last


def shape(dims, kind):
    return jax.ShapeDtypeStruct(tuple(dims), kind)


def call(kernel, name, outs, scratch=(), after=0, cost=1000):
    def run(*operands):
        spaces = [pltpu.VMEM] * (len(operands) - after) + [pl.ANY] * after
        held = sum(math.prod(x.shape) * 4 for x in scratch)
        return pl.pallas_call(
            kernel,
            in_specs=[pl.BlockSpec(memory_space=space) for space in spaces],
            out_specs=[pl.BlockSpec(memory_space=pltpu.VMEM)] * len(outs),
            out_shape=outs,
            scratch_shapes=list(scratch),
            compiler_params=pltpu.CompilerParams(vmem_limit_bytes=held + SCOPED),
            cost_estimate=pl.CostEstimate(flops=cost, bytes_accessed=1000, transcendentals=0),
            name=name,
        )(*operands)

    return run


def per_device(
    n_rows,
    n_blk,
    pair_left,
    pair_right,
    pair_middle,
    cotangent,
    left_weight,
    right_weight,
    gate_weight,
    output_weight,
):
    n_i, k_left, width = pair_left.shape
    n_j, k_right, _ = pair_right.shape
    n_k = k_left * n_blk
    right_raw = gather_doubling(pair_right[None], "rows", n_rows)
    middle_shape = (n_i, n_j, width)
    gate, middle_in, head_back, tri_up = call(
        middle_kernel,
        "middle",
        [shape(middle_shape, f32), shape(middle_shape, bf16), shape(middle_shape, bf16), shape(middle_shape, f32)],
        after=1,
    )(pair_middle, cotangent, gate_weight, output_weight, behind(cost=10**9))
    right_act, right_in, *right_flip = call(
        functools.partial(right_kernel, n_rows, n_blk, k_left),
        "right",
        [shape((n_j * n_k, width), f32), shape((n_rows, n_j, k_right, width), bf16)]
        + [shape((k_left, n_j, width), f32)] * n_blk,
    )(*right_raw, right_weight)
    left_raw = gather_left(pair_left, n_blk, (right_raw[0], middle_in))
    left_act, left_in, total = [], [], []
    act_shape = shape(pair_left.shape, f32)
    in_shape = shape(pair_left.shape, bf16)
    for s in range(n_blk - 1):
        act, inputs, total = call(
            functools.partial(left_kernel, len(left_raw[s]), s == 0),
            "left",
            [act_shape, in_shape, shape(middle_shape, f32)],
        )(*left_raw[s], left_weight, right_flip[s], *total)
        left_act.append(act)
        left_in.append(inputs)
        total = [total]
    act, inputs, tri_in, tri_back = call(
        functools.partial(triangle_kernel, len(left_raw[-1]), n_blk > 1),
        "triangle",
        [act_shape, in_shape, shape(middle_shape, bf16), shape(middle_shape, f32)],
    )(*left_raw[-1], left_weight, right_flip[-1], tri_up, *total)
    left_act.append(act)
    left_in.append(inputs)
    half = n_blk // 2
    left_out = []
    for first in (half, 0):
        some = call(
            functools.partial(left_back_kernel, first, n_blk),
            "left_back",
            [shape(pair_left.shape, bf16)] * half,
            after=0,
        )(tri_back, right_act)
        left_out = [*some, *left_out]
    left_back = [left_out[0]] + [exchange(left_out[s], "blk", n_blk, s) for s in range(1, n_blk)]
    right_stack = shape((n_rows // 2,) + pair_right.shape, bf16)
    keep, send = call(
        functools.partial(right_back_kernel, n_rows, n_blk),
        "right_back",
        [right_stack, right_stack],
        scratch=[pltpu.VMEM((n_j, n_k, width), bf16)],
        after=1,
    )(tri_back, *left_act, left_out[0])
    kept, came, sent = halving_sum(keep, send, "rows", n_rows, (behind(*left_back[1:], cost=LEFT_COST),))
    update, pre_back, gate_part, output_part = call(
        heads_kernel,
        "heads",
        [
            shape(middle_shape, bf16),
            shape(middle_shape, bf16),
            shape(gate_weight.shape, f32),
            shape(output_weight.shape, f32),
        ],
        after=1,
    )(tri_in, output_weight, gate, middle_in, head_back, cotangent, left_out[0])
    parts = (n_rows // 2, width // n_rows, 6 * width)
    keep, send = call(
        functools.partial(weights_kernel, n_rows, n_blk),
        "weights",
        [shape(parts, f32), shape(parts, bf16)],
        scratch=[pltpu.VMEM((width, 6 * width), f32)],
    )(right_in, left_weight, right_weight, gate_part, output_part, *left_in, *left_out, keep, send)
    grad_middle, done_middle = call(
        grad_middle_kernel, "grad_middle", [shape(middle_shape, bf16), MARK], after=1
    )(pair_middle, pre_back, gate_weight, send)
    keep, part, _ = halving_sum(keep, send, "rows", n_rows, (done_middle,))
    part = combine([keep, part], (behind(sent),))
    grad_left, done_left = call(side_kernel, "left_side", [shape(pair_left.shape, bf16), MARK])(
        pair_left, left_weight, *left_back
    )
    part = combine([part] + [exchange(part, "blk", n_blk, s) for s in range(1, n_blk)], (done_left,))
    pieces = [part] + [exchange(part, "rows", n_rows, s) for s in range(1, n_rows)]
    grad_right, done_right = call(side_kernel, "right_side", [shape(pair_right.shape, bf16), MARK])(
        pair_right, right_weight, kept.reshape(pair_right.shape), came.reshape(pair_right.shape)
    )
    deltas = call(
        functools.partial(deltas_kernel, n_rows),
        "deltas",
        [shape(x.shape, f32) for x in (left_weight, right_weight, gate_weight, output_weight)],
        after=1,
    )(*pieces, done_right)
    return (
        update,
        grad_left,
        grad_right,
        grad_middle,
        *deltas,
    )


def solution(mesh):
    sides = P(("rep", "rows"), "blk", None)
    right = P(("rep", "blk"), "rows", None)
    return jax.shard_map(
        functools.partial(per_device, mesh.shape["rows"], mesh.shape["blk"]),
        mesh=mesh,
        in_specs=(sides, right, sides, sides, P(), P(), P(), P()),
        out_specs=(sides, sides, right, sides) + (P("rep", None),) * 4,
        check_vma=False,
    )
```

```python
import functools
import math

import jax
import jax.numpy as jnp
from jax import lax
from jax.experimental import pallas as pl
from jax.experimental.pallas import tpu as pltpu
from jax.sharding import PartitionSpec as P

epsilon = 1e-05
f32 = jnp.float32
bf16 = jnp.bfloat16
SCOPED = 6 * 1024 * 1024
LEFT_COST = 2 * 10**8
MARK = jax.ShapeDtypeStruct((8, 128), jnp.float32)


def sigmoid(x):
    return 0.5 * jnp.tanh(0.5 * x) + 0.5


def dot(a, b):
    return lax.dot_general(a, b, (((1,), (0,)), ((), ())), preferred_element_type=f32)


def dot_nt(a, b):
    return lax.dot_general(a, b, (((1,), (1,)), ((), ())), preferred_element_type=f32)


def dot_tn(a, b):
    return lax.dot_general(a, b, (((0,), (0,)), ((), ())), preferred_element_type=f32)


def split(values):
    high = values.astype(bf16)
    return jnp.concatenate([high, (values - high.astype(f32)).astype(bf16)], axis=-1)


def row_mean(parts, width):
    return dot(parts, jnp.full((parts.shape[-1], width), 1.0 / width, bf16))


def normalize(values, mean):
    centred = values - mean
    inverse = lax.rsqrt(row_mean(split(centred * centred), values.shape[-1]) + epsilon)
    return (centred * inverse, inverse)


def normalize_raw(raw):
    return normalize(raw.astype(f32), row_mean(raw, raw.shape[-1]))


def normalize_back(normed, inverse, upstream):
    width = upstream.shape[-1]
    first = row_mean(split(upstream), width)
    second = row_mean(split(upstream * normed), width)
    return inverse * (upstream - first - normed * second)


def gated(inputs, weight):
    pre = dot(inputs, weight)
    width = weight.shape[1] // 2
    return pre[:, :width], sigmoid(pre[:, width:])


def joined_grad(back, lin, sw):
    return jnp.concatenate([back * sw, back * lin * sw * (1.0 - sw)], axis=-1).astype(bf16)


def middle_kernel(middle, cotangent, gate_weight, output_weight, _, gate, middle_in, head_back, tri_up):
    n_i, n_j, width = middle.shape
    step = 16

    def body(at, _):
        rows = pl.ds(at * step, step)
        normed, _ = normalize_raw(middle[rows].reshape(step * n_j, width))
        inputs = normed.astype(bf16)
        opened = sigmoid(dot(inputs, gate_weight[...]))
        back = (cotangent[rows].astype(f32).reshape(step * n_j, width) * opened).astype(bf16)
        gate[rows] = opened.reshape(step, n_j, width)
        middle_in[rows] = inputs.reshape(step, n_j, width)
        head_back[rows] = back.reshape(step, n_j, width)
        up = dot_nt(back, output_weight[...])
        tri_up[rows] = (up - row_mean(split(up), width)).reshape(step, n_j, width)
        return 0

    lax.fori_loop(0, n_i // step, body, 0, unroll=True)


def right_kernel(n_rows, n_blk, k_left, *refs):
    raw, (weight, act_out, in_out, *flip_out) = refs[:n_rows], refs[n_rows:]
    n_j, k_right, width = raw[0].shape
    n_k = k_left * n_blk
    unit = math.gcd(k_left, k_right)
    step = n_j
    for s in range(n_rows):

        def body(at, _, s=s):
            rows = pl.ds(at * step, step)
            normed, _ = normalize_raw(raw[s][rows].reshape(step * k_right, width))
            inputs = normed.astype(bf16)
            in_out[s, rows] = inputs.reshape(step, k_right, width)
            lin, sw = gated(inputs, weight[...])
            act = (sw * lin).astype(bf16).astype(f32).reshape(step, k_right, width)
            for part in range(k_right // unit):
                at_k = place(n_blk, k_left, k_right, s, part)
                for j in range(step):
                    start = pl.multiple_of((at * step + j) * n_k + at_k, unit)
                    act_out[pl.ds(start, unit), :] = act[j, part * unit : (part + 1) * unit]
            return 0

        lax.fori_loop(0, n_j // step, body, 0, unroll=True)

    for s in range(n_blk):

        def flip(k, _, s=s):
            flip_out[s][k] = act_out[pl.ds(s * k_left + k, n_j, stride=n_k), :]
            return 0

        lax.fori_loop(0, k_left, flip, 0, unroll=True)


def place(n_blk, k_left, k_right, piece, part):
    unit = math.gcd(k_left, k_right)
    vertex = lax.bitwise_xor(lax.axis_index("rows"), piece) * k_right + part * unit
    block = vertex // k_left
    at = lax.bitwise_xor(lax.axis_index("blk"), block) * k_left + vertex - block * k_left
    return pl.multiple_of(at, unit)


def project_left(raws, weight, act_out, in_out):
    n_i, k_left, width = raws[0].shape
    step = 32

    def body(at, _):
        rows = pl.ds(at * step, step)
        raw = raws[0][rows]
        if len(raws) > 1:
            place = jnp.full(raw.shape, lax.axis_index("blk"), jnp.int32)
            inner = jnp.logical_or(place == 1, place == 2)
            raw = jnp.where(inner, raws[1][rows].astype(f32), raw.astype(f32)).astype(bf16)
        normed, _ = normalize_raw(raw.reshape(step * k_left, width))
        inputs = normed.astype(bf16)
        in_out[rows] = inputs.reshape(step, k_left, width)
        lin, sw = gated(inputs, weight[...])
        act_out[rows] = (sw * lin).astype(bf16).astype(f32).reshape(step, k_left, width)
        return 0

    lax.fori_loop(0, n_i // step, body, 0, unroll=True)


def add_vertices(rows, act, flip):
    total = act[rows, 0:1, :] * flip[0][None]
    for k in range(1, act.shape[1]):
        total = total + act[rows, k : k + 1, :] * flip[k][None]
    return total


def left_kernel(n_raw, first, *refs):
    raw, (weight, flip, *refs) = refs[:n_raw], refs[n_raw:]
    total_in, (act_out, in_out, total_out) = refs[: 0 if first else 1], refs[0 if first else 1 :]
    n_i, n_j, width = total_out.shape
    step = 8
    project_left(raw, weight, act_out, in_out)

    def body(at, _):
        rows = pl.ds(at * step, step)
        total = add_vertices(rows, act_out, flip)
        total_out[rows] = total if first else total_in[0][rows] + total
        return 0

    lax.fori_loop(0, n_i // step, body, 0, unroll=2)


def triangle_kernel(n_raw, has_total, *refs):
    raw, (left_w, flip, tri_up, *refs) = refs[:n_raw], refs[n_raw:]
    total_in, refs = refs[: 1 if has_total else 0], refs[1 if has_total else 0 :]
    act_out, in_out, tri_in, tri_back = refs
    n_i, n_j, width = tri_in.shape
    step = 8
    project_left(raw, left_w, act_out, in_out)

    def triangle_rows(at, _):
        rows = pl.ds(at * step, step)
        total = add_vertices(rows, act_out, flip)
        if has_total:
            total = total + total_in[0][rows]
        flat = step * n_j
        total = total.reshape(flat, width)
        normed, inverse = normalize(total, row_mean(split(total), width))
        tri_in[rows] = normed.astype(bf16).reshape(step, n_j, width)
        up = tri_up[rows].reshape(flat, width)
        second = row_mean(split(up * normed), width)
        back = inverse * (up - normed * second)
        tri_back[rows] = back.astype(bf16).astype(f32).reshape(step, n_j, width)
        return 0

    lax.fori_loop(0, n_i // step, triangle_rows, 0, unroll=True)


def heads_kernel(tri_in, out_w, gate, middle_in, head_back, cotangent, _, *refs):
    update, pre_back, gate_part, output_part = refs
    n_i, n_j, width = update.shape
    step = 16
    gate_part[...] = jnp.zeros_like(gate_part)
    output_part[...] = jnp.zeros_like(output_part)

    def body(at, _):
        rows = pl.ds(at * step, step)
        flat = step * n_j
        inputs = tri_in[rows].reshape(flat, width)
        head = dot(inputs, out_w[...])
        opened = gate[rows].reshape(flat, width)
        update[rows] = (opened * head).astype(bf16).reshape(step, n_j, width)
        upstream = cotangent[rows].astype(f32).reshape(flat, width)
        pre = (upstream * head * opened * (1.0 - opened)).astype(bf16)
        pre_back[rows] = pre.reshape(step, n_j, width)
        gate_part[...] += dot_tn(middle_in[rows].reshape(flat, width), pre)
        output_part[...] += dot_tn(inputs, head_back[rows].reshape(flat, width))
        return 0

    lax.fori_loop(0, n_i // step, body, 0, unroll=True)


def vertex_step(n_k, unit):
    size = unit
    while size * 2 <= 64 and n_k % (size * 2) == 0:
        size *= 2
    return size


def left_back_kernel(first, n_blk, tri_back, right_act, *left_out):
    n_i, n_j, width = tri_back.shape
    k_left = left_out[0].shape[1]
    n_k = k_left * n_blk
    last = (first + len(left_out)) * k_left
    k_step = k_left * math.gcd(len(left_out), max(1, 64 // k_left))
    few = max(1, 256 // k_step)
    for k0 in range(first * k_left, last, k_step):

        def rows_sum(at, _, k0=k0):
            rows = pl.ds(at * few, few)
            total = jnp.zeros((few, k_step, width), f32)
            for j in range(n_j):
                start = j * n_k + k0
                total = total + tri_back[rows, j : j + 1, :] * right_act[start : start + k_step, :][None]
            total = total.astype(bf16)
            for s in range(k_step // k_left):
                left_out[k0 // k_left - first + s][rows] = total[:, s * k_left : (s + 1) * k_left]
            return 0

        lax.fori_loop(0, n_i // few, rows_sum, 0, unroll=2)


def right_back_kernel(n_rows, n_blk, tri_back, *refs):
    left_act, refs = refs[:n_blk], refs[n_blk + 1 :]
    keep, send, right_sum = refs
    n_i, n_j, width = tri_back.shape
    k_left = left_act[0].shape[1]
    n_k = k_left * n_blk
    k_right = keep.shape[2]
    unit = math.gcd(k_left, k_right)
    few = 4
    k_step = vertex_step(n_k, k_left)
    for k0 in range(0, n_k, k_step):
        blocks = range(k0 // k_left, (k0 + k_step) // k_left)

        def rows_sum(at, _, k0=k0, blocks=blocks):
            eight = pl.ds(pl.multiple_of(at * 8, 8), 8)
            for half in range(0, 8, few):

                def add(i, totals):
                    some = tri_back[i, eight, :][half : half + few][:, None]
                    return tuple(
                        total + some * left_act[s][i][None] for s, total in zip(blocks, totals)
                    )

                zeros = tuple(jnp.zeros((few, k_left, width), f32) for _ in blocks)
                totals = lax.fori_loop(0, n_i, add, zeros, unroll=True)
                for s, total in zip(blocks, totals):
                    right_sum[pl.ds(at * 8 + half, few), s * k_left : (s + 1) * k_left, :] = total.astype(bf16)
            return 0

        lax.fori_loop(0, n_j // 8, rows_sum, 0)
    for s in range(n_rows):
        for part in range(k_right // unit):
            out = send if s % 2 else keep
            out[s // 2, :, part * unit : (part + 1) * unit, :] = right_sum[
                :, pl.ds(place(n_blk, k_left, k_right, s, part), unit), :
            ]


def weights_kernel(n_rows, n_blk, right_in, left_w, right_w, gate_part, output_part, *refs):
    left_in, refs = refs[:n_blk], refs[n_blk:]
    left_out, refs = refs[:n_blk], refs[n_blk:]
    keep, send, keep_out, send_out, total = refs
    right_out = [(send if s % 2 else keep).at[s // 2] for s in range(n_rows)]
    right_ins = [right_in.at[s] for s in range(n_rows)]
    width = gate_part.shape[0]
    total[:, 4 * width : 5 * width] = gate_part[...]
    total[:, 5 * width :] = output_part[...]
    for inputs_refs, weight, backs, first in (
        (left_in, left_w, left_out, 0),
        (right_ins, right_w, right_out, 2 * width),
    ):
        columns = slice(first, first + 2 * width)
        total[:, columns] = jnp.zeros((width, 2 * width), f32)
        n, k, _ = inputs_refs[0].shape
        step = 32
        flat = step * k
        for inputs_ref, back_ref in zip(inputs_refs, backs):

            def body(at, _, inputs_ref=inputs_ref, back_ref=back_ref, weight=weight, columns=columns, flat=flat):
                rows = pl.ds(at * step, step)
                inputs = inputs_ref[rows].reshape(flat, width)
                lin, sw = gated(inputs, weight[...])
                back = back_ref[rows].reshape(flat, width).astype(f32)
                total[:, columns] += dot_tn(inputs, joined_grad(back, lin, sw))
                return 0

            lax.fori_loop(0, n // step, body, 0, unroll=True)
    size = width // n_rows
    for s in range(n_rows):
        start = pl.multiple_of(lax.bitwise_xor(lax.axis_index("rows"), s) * size, size)
        piece = total[pl.ds(start, size), :]
        if s % 2:
            send_out[s // 2] = piece.astype(bf16)
        else:
            keep_out[s // 2] = piece


def grad_middle_kernel(middle, pre_back, gate_weight, _, grad_middle, mark):
    mark[...] = jnp.zeros_like(mark)
    n_i, n_j, width = middle.shape
    step = 16

    def body(at, _):
        rows = pl.ds(at * step, step)
        flat = step * n_j
        normed, inverse = normalize_raw(middle[rows].reshape(flat, width))
        up = dot_nt(pre_back[rows].reshape(flat, width), gate_weight[...])
        grad_middle[rows] = normalize_back(normed, inverse, up).astype(bf16).reshape(step, n_j, width)
        return 0

    lax.fori_loop(0, n_i // step, body, 0, unroll=True)


def side_kernel(raw, weight, *refs):
    backs, (grad, mark) = refs[:-2], refs[-2:]
    mark[...] = jnp.zeros_like(mark)
    n, k, width = raw.shape
    step = 32
    flat = step * k

    def body(at, _):
        rows = pl.ds(at * step, step)
        normed, inverse = normalize_raw(raw[rows].reshape(flat, width))
        lin, sw = gated(normed.astype(bf16), weight[...])
        back = backs[0][rows].astype(f32)
        for other in backs[1:]:
            back = back + other[rows].astype(f32)
        up = dot_nt(joined_grad(back.reshape(flat, width), lin, sw), weight[...])
        grad[rows] = normalize_back(normed, inverse, up).astype(bf16).reshape(step, k, width)
        return 0

    lax.fori_loop(0, n // step, body, 0, unroll=True)


def exchange(x, axis, n, bit):
    return lax.ppermute(x, axis, [(a, a ^ bit) for a in range(n)])


def halve_kernel(keep, came, *refs):
    kept, send = refs[-2:]
    for at in range(keep.shape[0]):
        total = keep[at].astype(f32) + came[at].astype(f32)
        if at % 2:
            send[at // 2] = total.astype(bf16)
        else:
            kept[at // 2] = total


def halving_sum(keep, send, axis, n, after):
    came = exchange(send, axis, n, 1)
    bit = 2
    while bit < n:
        half = (keep.shape[0] // 2,) + keep.shape[1:]
        keep, send = call(halve_kernel, "halve", [shape(half, f32), shape(half, bf16)], after=len(after))(
            keep, came, *after
        )
        came = exchange(send, axis, n, bit)
        bit *= 2
    return keep, came, send


def forward_kernel(source, *refs):
    refs[-1][...] = source[...]


def forwarded(block, after):
    (copy,) = call(forward_kernel, "forward", [shape(block.shape, block.dtype)], after=len(after))(block, *after)
    return copy


def outer_block(across, after):
    return exchange(forwarded(across, after), "blk", 4, 1)


def inner_block(block, after):
    return lax.ppermute(forwarded(block, after), "blk", [(0, 0), (1, 2), (2, 1), (3, 3)])


def order_kernel(*refs):
    refs[-1][...] = jnp.zeros_like(refs[-1])


def behind(*arrays, cost=2 * 10**10):
    (mark,) = call(order_kernel, "order", [MARK], after=len(arrays), cost=cost)(*arrays)
    return mark


def combine_kernel(n, *refs):
    totals = [ref[0].astype(f32) for ref in refs[:n]]
    while len(totals) > 1:
        pairs = [a + b for a, b in zip(totals[::2], totals[1::2])]
        totals = pairs + totals[2 * len(pairs) :]
    refs[-1][0] = totals[0].astype(bf16)


def combine(pieces, after=()):
    (total,) = call(
        functools.partial(combine_kernel, len(pieces)),
        "combine",
        [shape((1,) + pieces[0].shape[1:], bf16)],
        after=len(after),
    )(*pieces, *after)
    return total


def deltas_kernel(n_rows, *refs):
    pieces, outs = [ref.at[0] for ref in refs[:n_rows]], refs[n_rows + 1 :]
    size = pieces[0].shape[0]
    for s, piece in enumerate(pieces):
        start = pl.multiple_of(lax.bitwise_xor(lax.axis_index("rows"), s) * size, size)
        first = 0
        for out in outs:
            last = first + out.shape[1]
            out[pl.ds(start, size), :] = piece[:, first:last].astype(f32)
            first = last


def shape(dims, kind):
    return jax.ShapeDtypeStruct(tuple(dims), kind)


def call(kernel, name, outs, scratch=(), after=0, cost=1000):
    def run(*operands):
        spaces = [pltpu.VMEM] * (len(operands) - after) + [pl.ANY] * after
        held = sum(math.prod(x.shape) * 4 for x in scratch)
        return pl.pallas_call(
            kernel,
            in_specs=[pl.BlockSpec(memory_space=space) for space in spaces],
            out_specs=[pl.BlockSpec(memory_space=pltpu.VMEM)] * len(outs),
            out_shape=outs,
            scratch_shapes=list(scratch),
            compiler_params=pltpu.CompilerParams(vmem_limit_bytes=held + SCOPED),
            cost_estimate=pl.CostEstimate(flops=cost, bytes_accessed=1000, transcendentals=0),
            name=name,
        )(*operands)

    return run


def per_device(
    n_rows,
    n_blk,
    pair_left,
    pair_right,
    pair_middle,
    cotangent,
    left_weight,
    right_weight,
    gate_weight,
    output_weight,
):
    n_i, k_left, width = pair_left.shape
    n_j, k_right, _ = pair_right.shape
    n_k = k_left * n_blk
    right_raw = [pair_right] + [exchange(pair_right, "rows", n_rows, s) for s in range(1, n_rows)]
    middle_shape = (n_i, n_j, width)
    gate, middle_in, head_back, tri_up = call(
        middle_kernel,
        "middle",
        [shape(middle_shape, f32), shape(middle_shape, bf16), shape(middle_shape, bf16), shape(middle_shape, f32)],
        after=1,
    )(pair_middle, cotangent, gate_weight, output_weight, behind(cost=10**9))
    right_act, right_in, *right_flip = call(
        functools.partial(right_kernel, n_rows, n_blk, k_left),
        "right",
        [shape((n_j * n_k, width), f32), shape((n_rows, n_j, k_right, width), bf16)]
        + [shape((k_left, n_j, width), f32)] * n_blk,
    )(*right_raw, right_weight)
    left_raw = [[pair_left]] + [[exchange(pair_left, "blk", n_blk, s)] for s in range(1, 3 if n_blk == 4 else n_blk)]
    if n_blk == 4:
        left_raw.append([outer_block(left_raw[2][0], (right_in, middle_in))])
    left_act, left_in, total = [], [], []
    act_shape = shape(pair_left.shape, f32)
    in_shape = shape(pair_left.shape, bf16)
    for s in range(n_blk - 1):
        act, inputs, total = call(
            functools.partial(left_kernel, len(left_raw[s]), s == 0),
            "left",
            [act_shape, in_shape, shape(middle_shape, f32)],
        )(*left_raw[s], left_weight, right_flip[s], *total)
        left_act.append(act)
        left_in.append(inputs)
        total = [total]
        if n_blk == 4 and s == 0:
            left_raw[3].append(inner_block(pair_left, (act,)))
    act, inputs, tri_in, tri_back = call(
        functools.partial(triangle_kernel, len(left_raw[-1]), n_blk > 1),
        "triangle",
        [act_shape, in_shape, shape(middle_shape, bf16), shape(middle_shape, f32)],
    )(*left_raw[-1], left_weight, right_flip[-1], tri_up, *total)
    left_act.append(act)
    left_in.append(inputs)
    half = n_blk // 2
    left_out = []
    for first in (half, 0):
        some = call(
            functools.partial(left_back_kernel, first, n_blk),
            "left_back",
            [shape(pair_left.shape, bf16)] * half,
            after=0,
        )(tri_back, right_act)
        left_out = [*some, *left_out]
    left_back = [left_out[0]] + [exchange(left_out[s], "blk", n_blk, s) for s in range(1, n_blk)]
    right_stack = shape((n_rows // 2,) + pair_right.shape, bf16)
    keep, send = call(
        functools.partial(right_back_kernel, n_rows, n_blk),
        "right_back",
        [right_stack, right_stack],
        scratch=[pltpu.VMEM((n_j, n_k, width), bf16)],
        after=1,
    )(tri_back, *left_act, left_out[0])
    kept, came, sent = halving_sum(keep, send, "rows", n_rows, (behind(*left_back[1:], cost=LEFT_COST),))
    update, pre_back, gate_part, output_part = call(
        heads_kernel,
        "heads",
        [
            shape(middle_shape, bf16),
            shape(middle_shape, bf16),
            shape(gate_weight.shape, f32),
            shape(output_weight.shape, f32),
        ],
        after=1,
    )(tri_in, output_weight, gate, middle_in, head_back, cotangent, left_out[0])
    parts = (n_rows // 2, width // n_rows, 6 * width)
    keep, send = call(
        functools.partial(weights_kernel, n_rows, n_blk),
        "weights",
        [shape(parts, f32), shape(parts, bf16)],
        scratch=[pltpu.VMEM((width, 6 * width), f32)],
    )(right_in, left_weight, right_weight, gate_part, output_part, *left_in, *left_out, keep, send)
    grad_middle, done_middle = call(
        grad_middle_kernel, "grad_middle", [shape(middle_shape, bf16), MARK], after=1
    )(pair_middle, pre_back, gate_weight, send)
    keep, part, _ = halving_sum(keep, send, "rows", n_rows, (done_middle,))
    part = combine([keep, part], (behind(sent),))
    grad_left, done_left = call(side_kernel, "left_side", [shape(pair_left.shape, bf16), MARK])(
        pair_left, left_weight, *left_back
    )
    part = combine([part] + [exchange(part, "blk", n_blk, s) for s in range(1, n_blk)], (done_left,))
    pieces = [part] + [exchange(part, "rows", n_rows, s) for s in range(1, n_rows)]
    grad_right, done_right = call(side_kernel, "right_side", [shape(pair_right.shape, bf16), MARK])(
        pair_right, right_weight, kept.reshape(pair_right.shape), came.reshape(pair_right.shape)
    )
    deltas = call(
        functools.partial(deltas_kernel, n_rows),
        "deltas",
        [shape(x.shape, f32) for x in (left_weight, right_weight, gate_weight, output_weight)],
        after=1,
    )(*pieces, done_right)
    return (
        update,
        grad_left,
        grad_right,
        grad_middle,
        *deltas,
    )


def solution(mesh):
    sides = P(("rep", "rows"), "blk", None)
    right = P(("rep", "blk"), "rows", None)
    return jax.shard_map(
        functools.partial(per_device, mesh.shape["rows"], mesh.shape["blk"]),
        mesh=mesh,
        in_specs=(sides, right, sides, sides, P(), P(), P(), P()),
        out_specs=(sides, sides, right, sides) + (P("rep", None),) * 4,
        check_vma=False,
    )
```

```python
import functools
import math

import jax
import jax.numpy as jnp
from jax import lax
from jax.experimental import pallas as pl
from jax.experimental.pallas import tpu as pltpu
from jax.sharding import PartitionSpec as P

epsilon = 1e-05
f32 = jnp.float32
bf16 = jnp.bfloat16
SCOPED = 6 * 1024 * 1024
LEFT_COST = 2 * 10**8
MARK = jax.ShapeDtypeStruct((8, 128), jnp.float32)


def sigmoid(x):
    return 0.5 * jnp.tanh(0.5 * x) + 0.5


def dot(a, b):
    return lax.dot_general(a, b, (((1,), (0,)), ((), ())), preferred_element_type=f32)


def dot_nt(a, b):
    return lax.dot_general(a, b, (((1,), (1,)), ((), ())), preferred_element_type=f32)


def dot_tn(a, b):
    return lax.dot_general(a, b, (((0,), (0,)), ((), ())), preferred_element_type=f32)


def split(values):
    high = values.astype(bf16)
    return jnp.concatenate([high, (values - high.astype(f32)).astype(bf16)], axis=-1)


def row_mean(parts, width):
    return dot(parts, jnp.full((parts.shape[-1], width), 1.0 / width, bf16))


def normalize(values, mean):
    centred = values - mean
    inverse = lax.rsqrt(row_mean(split(centred * centred), values.shape[-1]) + epsilon)
    return (centred * inverse, inverse)


def normalize_raw(raw):
    return normalize(raw.astype(f32), row_mean(raw, raw.shape[-1]))


def normalize_back(normed, inverse, upstream):
    width = upstream.shape[-1]
    first = row_mean(split(upstream), width)
    second = row_mean(split(upstream * normed), width)
    return inverse * (upstream - first - normed * second)


def gated(inputs, weight):
    pre = dot(inputs, weight)
    width = weight.shape[1] // 2
    return pre[:, :width], sigmoid(pre[:, width:])


def joined_grad(back, lin, sw):
    return jnp.concatenate([back * sw, back * lin * sw * (1.0 - sw)], axis=-1).astype(bf16)


def middle_kernel(middle, cotangent, gate_weight, output_weight, _, gate, middle_in, head_back, tri_up):
    n_i, n_j, width = middle.shape
    step = 16

    def body(at, _):
        rows = pl.ds(at * step, step)
        normed, _ = normalize_raw(middle[rows].reshape(step * n_j, width))
        inputs = normed.astype(bf16)
        opened = sigmoid(dot(inputs, gate_weight[...]))
        back = (cotangent[rows].astype(f32).reshape(step * n_j, width) * opened).astype(bf16)
        gate[rows] = opened.reshape(step, n_j, width)
        middle_in[rows] = inputs.reshape(step, n_j, width)
        head_back[rows] = back.reshape(step, n_j, width)
        up = dot_nt(back, output_weight[...])
        tri_up[rows] = (up - row_mean(split(up), width)).reshape(step, n_j, width)
        return 0

    lax.fori_loop(0, n_i // step, body, 0, unroll=True)


def right_kernel(n_rows, n_blk, k_left, *refs):
    raw, (weight, _, _, act_out, in_out, *flip_out) = refs[:n_rows], refs[n_rows:]
    n_j, k_right, width = raw[0].shape
    n_k = k_left * n_blk
    unit = math.gcd(k_left, k_right)
    step = n_j
    for s in range(n_rows):

        def body(at, _, s=s):
            rows = pl.ds(at * step, step)
            normed, _ = normalize_raw(raw[s][rows].reshape(step * k_right, width))
            inputs = normed.astype(bf16)
            in_out[s, rows] = inputs.reshape(step, k_right, width)
            lin, sw = gated(inputs, weight[...])
            act = (sw * lin).astype(bf16).astype(f32).reshape(step, k_right, width)
            for part in range(k_right // unit):
                at_k = place(n_blk, k_left, k_right, s, part)
                for j in range(step):
                    start = pl.multiple_of((at * step + j) * n_k + at_k, unit)
                    act_out[pl.ds(start, unit), :] = act[j, part * unit : (part + 1) * unit]
            return 0

        lax.fori_loop(0, n_j // step, body, 0, unroll=True)

    for s in range(n_blk):

        def flip(k, _, s=s):
            flip_out[s][k] = act_out[pl.ds(s * k_left + k, n_j, stride=n_k), :]
            return 0

        lax.fori_loop(0, k_left, flip, 0, unroll=True)


def place(n_blk, k_left, k_right, piece, part):
    unit = math.gcd(k_left, k_right)
    vertex = lax.bitwise_xor(lax.axis_index("rows"), piece) * k_right + part * unit
    block = vertex // k_left
    at = lax.bitwise_xor(lax.axis_index("blk"), block) * k_left + vertex - block * k_left
    return pl.multiple_of(at, unit)


def project_left(raws, weight, act_out, in_out):
    n_i, k_left, width = raws[0].shape
    step = 32

    def body(at, _):
        rows = pl.ds(at * step, step)
        raw = raws[0][rows]
        if len(raws) > 1:
            place = jnp.full(raw.shape, lax.axis_index("blk"), jnp.int32)
            inner = jnp.logical_or(place == 1, place == 2)
            raw = jnp.where(inner, raws[1][rows].astype(f32), raw.astype(f32)).astype(bf16)
        normed, _ = normalize_raw(raw.reshape(step * k_left, width))
        inputs = normed.astype(bf16)
        in_out[rows] = inputs.reshape(step, k_left, width)
        lin, sw = gated(inputs, weight[...])
        act_out[rows] = (sw * lin).astype(bf16).astype(f32).reshape(step, k_left, width)
        return 0

    lax.fori_loop(0, n_i // step, body, 0, unroll=True)


def add_vertices(rows, act, flip):
    total = act[rows, 0:1, :] * flip[0][None]
    for k in range(1, act.shape[1]):
        total = total + act[rows, k : k + 1, :] * flip[k][None]
    return total


def own_kernel(raw, weight, act_out, in_out):
    project_left([raw], weight, act_out, in_out)


def own_sum_kernel(act, flip, total):
    step = 8

    def body(at, _):
        rows = pl.ds(at * step, step)
        total[rows] = add_vertices(rows, act, flip)
        return 0

    lax.fori_loop(0, total.shape[0] // step, body, 0, unroll=2)


def left_kernel(raw, weight, flip, total_in, act_out, in_out, total_out):
    n_i, n_j, width = total_out.shape
    step = 8
    project_left([raw], weight, act_out, in_out)

    def body(at, _):
        rows = pl.ds(at * step, step)
        total_out[rows] = total_in[rows] + add_vertices(rows, act_out, flip)
        return 0

    lax.fori_loop(0, n_i // step, body, 0, unroll=2)


def triangle_kernel(n_raw, *refs):
    raw, (left_w, flip, tri_up, *refs) = refs[:n_raw], refs[n_raw:]
    total_in, act_out, in_out, tri_in, tri_back = refs
    n_i, n_j, width = tri_in.shape
    step = 8
    project_left(raw, left_w, act_out, in_out)

    def triangle_rows(at, _):
        rows = pl.ds(at * step, step)
        total = total_in[rows] + add_vertices(rows, act_out, flip)
        flat = step * n_j
        total = total.reshape(flat, width)
        normed, inverse = normalize(total, row_mean(split(total), width))
        tri_in[rows] = normed.astype(bf16).reshape(step, n_j, width)
        up = tri_up[rows].reshape(flat, width)
        second = row_mean(split(up * normed), width)
        back = inverse * (up - normed * second)
        tri_back[rows] = back.astype(bf16).astype(f32).reshape(step, n_j, width)
        return 0

    lax.fori_loop(0, n_i // step, triangle_rows, 0, unroll=True)


def heads_kernel(tri_in, out_w, gate, middle_in, head_back, cotangent, _, *refs):
    update, pre_back, gate_part, output_part = refs
    n_i, n_j, width = update.shape
    step = 16
    gate_part[...] = jnp.zeros_like(gate_part)
    output_part[...] = jnp.zeros_like(output_part)

    def body(at, _):
        rows = pl.ds(at * step, step)
        flat = step * n_j
        inputs = tri_in[rows].reshape(flat, width)
        head = dot(inputs, out_w[...])
        opened = gate[rows].reshape(flat, width)
        update[rows] = (opened * head).astype(bf16).reshape(step, n_j, width)
        upstream = cotangent[rows].astype(f32).reshape(flat, width)
        pre = (upstream * head * opened * (1.0 - opened)).astype(bf16)
        pre_back[rows] = pre.reshape(step, n_j, width)
        gate_part[...] += dot_tn(middle_in[rows].reshape(flat, width), pre)
        output_part[...] += dot_tn(inputs, head_back[rows].reshape(flat, width))
        return 0

    lax.fori_loop(0, n_i // step, body, 0, unroll=True)


def vertex_step(n_k, unit):
    size = unit
    while size * 2 <= 64 and n_k % (size * 2) == 0:
        size *= 2
    return size


def left_back_kernel(first, n_blk, tri_back, right_act, *left_out):
    n_i, n_j, width = tri_back.shape
    k_left = left_out[0].shape[1]
    n_k = k_left * n_blk
    last = (first + len(left_out)) * k_left
    k_step = k_left * math.gcd(len(left_out), max(1, 64 // k_left))
    few = max(1, 256 // k_step)
    for k0 in range(first * k_left, last, k_step):

        def rows_sum(at, _, k0=k0):
            rows = pl.ds(at * few, few)
            total = jnp.zeros((few, k_step, width), f32)
            for j in range(n_j):
                start = j * n_k + k0
                total = total + tri_back[rows, j : j + 1, :] * right_act[start : start + k_step, :][None]
            total = total.astype(bf16)
            for s in range(k_step // k_left):
                left_out[k0 // k_left - first + s][rows] = total[:, s * k_left : (s + 1) * k_left]
            return 0

        lax.fori_loop(0, n_i // few, rows_sum, 0, unroll=2)


def right_back_kernel(n_rows, n_blk, tri_back, *refs):
    left_act, refs = refs[:n_blk], refs[n_blk + 1 :]
    keep, send, right_sum = refs
    n_i, n_j, width = tri_back.shape
    k_left = left_act[0].shape[1]
    n_k = k_left * n_blk
    k_right = keep.shape[2]
    unit = math.gcd(k_left, k_right)
    few = 4
    k_step = vertex_step(n_k, k_left)
    for k0 in range(0, n_k, k_step):
        blocks = range(k0 // k_left, (k0 + k_step) // k_left)
        for first in range(0, n_j, few):

            def add(i, totals, first=first, blocks=blocks):
                acts = [left_act[s][i] for s in blocks]
                added = []
                for at in range(few):
                    row = tri_back[i, first + at : first + at + 1, :]
                    added += [total + row * act for total, act in zip(totals[at * len(acts) :], acts)]
                return tuple(added)

            zeros = (jnp.zeros((k_left, width), f32),) * (few * len(blocks))
            totals = lax.fori_loop(0, n_i, add, zeros, unroll=16)
            for at in range(few):
                for s, total in zip(blocks, totals[at * len(blocks) :]):
                    right_sum[first + at, s * k_left : (s + 1) * k_left, :] = total.astype(bf16)
    for s in range(n_rows):
        for part in range(k_right // unit):
            out = send if s % 2 else keep
            out[s // 2, :, part * unit : (part + 1) * unit, :] = right_sum[
                :, pl.ds(place(n_blk, k_left, k_right, s, part), unit), :
            ]


def weights_kernel(n_rows, n_blk, right_in, left_w, right_w, gate_part, output_part, *refs):
    left_in, refs = refs[:n_blk], refs[n_blk:]
    left_out, refs = refs[:n_blk], refs[n_blk:]
    keep, send, keep_out, send_out, total = refs
    right_out = [(send if s % 2 else keep).at[s // 2] for s in range(n_rows)]
    right_ins = [right_in.at[s] for s in range(n_rows)]
    width = gate_part.shape[0]
    total[:, 4 * width : 5 * width] = gate_part[...]
    total[:, 5 * width :] = output_part[...]
    for inputs_refs, weight, backs, first in (
        (left_in, left_w, left_out, 0),
        (right_ins, right_w, right_out, 2 * width),
    ):
        columns = slice(first, first + 2 * width)
        total[:, columns] = jnp.zeros((width, 2 * width), f32)
        n, k, _ = inputs_refs[0].shape
        step = 32
        flat = step * k
        for inputs_ref, back_ref in zip(inputs_refs, backs):

            def body(at, _, inputs_ref=inputs_ref, back_ref=back_ref, weight=weight, columns=columns, flat=flat):
                rows = pl.ds(at * step, step)
                inputs = inputs_ref[rows].reshape(flat, width)
                lin, sw = gated(inputs, weight[...])
                back = back_ref[rows].reshape(flat, width).astype(f32)
                total[:, columns] += dot_tn(inputs, joined_grad(back, lin, sw))
                return 0

            lax.fori_loop(0, n // step, body, 0, unroll=True)
    size = width // n_rows
    for s in range(n_rows):
        start = pl.multiple_of(lax.bitwise_xor(lax.axis_index("rows"), s) * size, size)
        piece = total[pl.ds(start, size), :]
        if s % 2:
            send_out[s // 2] = piece.astype(bf16)
        else:
            keep_out[s // 2] = piece


def grad_middle_kernel(middle, pre_back, gate_weight, _, grad_middle, mark):
    mark[...] = jnp.zeros_like(mark)
    n_i, n_j, width = middle.shape
    step = 16

    def body(at, _):
        rows = pl.ds(at * step, step)
        flat = step * n_j
        normed, inverse = normalize_raw(middle[rows].reshape(flat, width))
        up = dot_nt(pre_back[rows].reshape(flat, width), gate_weight[...])
        grad_middle[rows] = normalize_back(normed, inverse, up).astype(bf16).reshape(step, n_j, width)
        return 0

    lax.fori_loop(0, n_i // step, body, 0, unroll=True)


def side_kernel(raw, weight, *refs):
    backs, (grad, mark) = refs[:-2], refs[-2:]
    mark[...] = jnp.zeros_like(mark)
    n, k, width = raw.shape
    step = 32
    flat = step * k

    def body(at, _):
        rows = pl.ds(at * step, step)
        normed, inverse = normalize_raw(raw[rows].reshape(flat, width))
        lin, sw = gated(normed.astype(bf16), weight[...])
        back = backs[0][rows].astype(f32)
        for other in backs[1:]:
            back = back + other[rows].astype(f32)
        up = dot_nt(joined_grad(back.reshape(flat, width), lin, sw), weight[...])
        grad[rows] = normalize_back(normed, inverse, up).astype(bf16).reshape(step, k, width)
        return 0

    lax.fori_loop(0, n // step, body, 0, unroll=True)


def exchange(x, axis, n, bit):
    return lax.ppermute(x, axis, [(a, a ^ bit) for a in range(n)])


def halve_kernel(keep, came, *refs):
    kept, send = refs[-2:]
    for at in range(keep.shape[0]):
        total = keep[at].astype(f32) + came[at].astype(f32)
        if at % 2:
            send[at // 2] = total.astype(bf16)
        else:
            kept[at // 2] = total


def halving_sum(keep, send, axis, n, after):
    came = exchange(send, axis, n, 1)
    bit = 2
    while bit < n:
        half = (keep.shape[0] // 2,) + keep.shape[1:]
        keep, send = call(halve_kernel, "halve", [shape(half, f32), shape(half, bf16)], after=len(after))(
            keep, came, *after
        )
        came = exchange(send, axis, n, bit)
        bit *= 2
    return keep, came, send


def forward_kernel(source, *refs):
    refs[-1][...] = source[...]


def forwarded(block, after):
    (copy,) = call(forward_kernel, "forward", [shape(block.shape, block.dtype)], after=len(after))(block, *after)
    return copy


def outer_block(across, after):
    return exchange(forwarded(across, after), "blk", 4, 1)


def inner_block(block, after):
    return lax.ppermute(forwarded(block, after), "blk", [(0, 0), (1, 2), (2, 1), (3, 3)])


def order_kernel(*refs):
    refs[-1][...] = jnp.zeros_like(refs[-1])


def behind(*arrays, cost=2 * 10**10):
    (mark,) = call(order_kernel, "order", [MARK], after=len(arrays), cost=cost)(*arrays)
    return mark


def combine_kernel(n, *refs):
    totals = [ref[0].astype(f32) for ref in refs[:n]]
    while len(totals) > 1:
        pairs = [a + b for a, b in zip(totals[::2], totals[1::2])]
        totals = pairs + totals[2 * len(pairs) :]
    refs[-1][0] = totals[0].astype(bf16)


def combine(pieces, after=()):
    (total,) = call(
        functools.partial(combine_kernel, len(pieces)),
        "combine",
        [shape((1,) + pieces[0].shape[1:], bf16)],
        after=len(after),
    )(*pieces, *after)
    return total


def deltas_kernel(n_rows, *refs):
    pieces, outs = [ref.at[0] for ref in refs[:n_rows]], refs[n_rows + 1 :]
    size = pieces[0].shape[0]
    for s, piece in enumerate(pieces):
        start = pl.multiple_of(lax.bitwise_xor(lax.axis_index("rows"), s) * size, size)
        first = 0
        for out in outs:
            last = first + out.shape[1]
            out[pl.ds(start, size), :] = piece[:, first:last].astype(f32)
            first = last


def shape(dims, kind):
    return jax.ShapeDtypeStruct(tuple(dims), kind)


def call(kernel, name, outs, scratch=(), after=0, cost=1000):
    def run(*operands):
        spaces = [pltpu.VMEM] * (len(operands) - after) + [pl.ANY] * after
        held = sum(math.prod(x.shape) * 4 for x in scratch)
        return pl.pallas_call(
            kernel,
            in_specs=[pl.BlockSpec(memory_space=space) for space in spaces],
            out_specs=[pl.BlockSpec(memory_space=pltpu.VMEM)] * len(outs),
            out_shape=outs,
            scratch_shapes=list(scratch),
            compiler_params=pltpu.CompilerParams(vmem_limit_bytes=held + SCOPED),
            cost_estimate=pl.CostEstimate(flops=cost, bytes_accessed=1000, transcendentals=0),
            name=name,
        )(*operands)

    return run


def per_device(
    n_rows,
    n_blk,
    pair_left,
    pair_right,
    pair_middle,
    cotangent,
    left_weight,
    right_weight,
    gate_weight,
    output_weight,
):
    n_i, k_left, width = pair_left.shape
    n_j, k_right, _ = pair_right.shape
    n_k = k_left * n_blk
    right_raw = [pair_right] + [exchange(pair_right, "rows", n_rows, s) for s in range(1, n_rows)]
    middle_shape = (n_i, n_j, width)
    gate, middle_in, head_back, tri_up = call(
        middle_kernel,
        "middle",
        [shape(middle_shape, f32), shape(middle_shape, bf16), shape(middle_shape, bf16), shape(middle_shape, f32)],
        after=1,
    )(pair_middle, cotangent, gate_weight, output_weight, behind(cost=10**9))
    act_shape = shape(pair_left.shape, f32)
    in_shape = shape(pair_left.shape, bf16)
    own_act, own_in = call(own_kernel, "own", [act_shape, in_shape], after=0)(pair_left, left_weight)
    right_act, right_in, *right_flip = call(
        functools.partial(right_kernel, n_rows, n_blk, k_left),
        "right",
        [shape((n_j * n_k, width), f32), shape((n_rows, n_j, k_right, width), bf16)]
        + [shape((k_left, n_j, width), f32)] * n_blk,
        after=2,
    )(*right_raw, right_weight, own_act, middle_in)
    left_raw = [[pair_left]] + [[exchange(pair_left, "blk", n_blk, s)] for s in range(1, 3 if n_blk == 4 else n_blk)]
    if n_blk == 4:
        left_raw.append([outer_block(left_raw[2][0], (right_in, middle_in))])
    total = call(own_sum_kernel, "own_sum", [shape(middle_shape, f32)])(own_act, right_flip[0])
    if n_blk == 4:
        left_raw[3].append(inner_block(pair_left, tuple(total)))
    left_act, left_in = [own_act], [own_in]
    for s in range(1, n_blk - 1):
        act, inputs, *total = call(
            left_kernel,
            "left",
            [act_shape, in_shape, shape(middle_shape, f32)],
        )(*left_raw[s], left_weight, right_flip[s], *total)
        left_act.append(act)
        left_in.append(inputs)
    act, inputs, tri_in, tri_back = call(
        functools.partial(triangle_kernel, len(left_raw[-1])),
        "triangle",
        [act_shape, in_shape, shape(middle_shape, bf16), shape(middle_shape, f32)],
    )(*left_raw[-1], left_weight, right_flip[-1], tri_up, *total)
    left_act.append(act)
    left_in.append(inputs)
    half = n_blk // 2
    left_out = []
    for first in (half, 0):
        some = call(
            functools.partial(left_back_kernel, first, n_blk),
            "left_back",
            [shape(pair_left.shape, bf16)] * half,
            after=0,
        )(tri_back, right_act)
        left_out = [*some, *left_out]
    left_back = [left_out[0]] + [exchange(left_out[s], "blk", n_blk, s) for s in range(1, n_blk)]
    right_stack = shape((n_rows // 2,) + pair_right.shape, bf16)
    keep, send = call(
        functools.partial(right_back_kernel, n_rows, n_blk),
        "right_back",
        [right_stack, right_stack],
        scratch=[pltpu.VMEM((n_j, n_k, width), bf16)],
        after=1,
    )(tri_back, *left_act, left_out[0])
    kept, came, sent = halving_sum(keep, send, "rows", n_rows, (behind(*left_back[1:], cost=LEFT_COST),))
    update, pre_back, gate_part, output_part = call(
        heads_kernel,
        "heads",
        [
            shape(middle_shape, bf16),
            shape(middle_shape, bf16),
            shape(gate_weight.shape, f32),
            shape(output_weight.shape, f32),
        ],
        after=1,
    )(tri_in, output_weight, gate, middle_in, head_back, cotangent, left_out[0])
    parts = (n_rows // 2, width // n_rows, 6 * width)
    keep, send = call(
        functools.partial(weights_kernel, n_rows, n_blk),
        "weights",
        [shape(parts, f32), shape(parts, bf16)],
        scratch=[pltpu.VMEM((width, 6 * width), f32)],
    )(right_in, left_weight, right_weight, gate_part, output_part, *left_in, *left_out, keep, send)
    grad_middle, done_middle = call(
        grad_middle_kernel, "grad_middle", [shape(middle_shape, bf16), MARK], after=1
    )(pair_middle, pre_back, gate_weight, send)
    keep, part, _ = halving_sum(keep, send, "rows", n_rows, (done_middle,))
    part = combine([keep, part], (behind(sent),))
    grad_left, done_left = call(side_kernel, "left_side", [shape(pair_left.shape, bf16), MARK])(
        pair_left, left_weight, *left_back
    )
    part = combine([part] + [exchange(part, "blk", n_blk, s) for s in range(1, n_blk)], (done_left,))
    pieces = [part] + [exchange(part, "rows", n_rows, s) for s in range(1, n_rows)]
    grad_right, done_right = call(side_kernel, "right_side", [shape(pair_right.shape, bf16), MARK])(
        pair_right, right_weight, kept.reshape(pair_right.shape), came.reshape(pair_right.shape)
    )
    deltas = call(
        functools.partial(deltas_kernel, n_rows),
        "deltas",
        [shape(x.shape, f32) for x in (left_weight, right_weight, gate_weight, output_weight)],
        after=1,
    )(*pieces, done_right)
    return (
        update,
        grad_left,
        grad_right,
        grad_middle,
        *deltas,
    )


def solution(mesh):
    sides = P(("rep", "rows"), "blk", None)
    right = P(("rep", "blk"), "rows", None)
    return jax.shard_map(
        functools.partial(per_device, mesh.shape["rows"], mesh.shape["blk"]),
        mesh=mesh,
        in_specs=(sides, right, sides, sides, P(), P(), P(), P()),
        out_specs=(sides, sides, right, sides) + (P("rep", None),) * 4,
        check_vma=False,
    )
```

```python
import functools
import math

import jax
import jax.numpy as jnp
from jax import lax
from jax.experimental import pallas as pl
from jax.experimental.pallas import tpu as pltpu
from jax.sharding import PartitionSpec as P

epsilon = 1e-05
f32 = jnp.float32
bf16 = jnp.bfloat16
SCOPED = 6 * 1024 * 1024
LEFT_COST = 2 * 10**8
MARK = jax.ShapeDtypeStruct((8, 128), jnp.float32)


def sigmoid(x):
    return 0.5 * jnp.tanh(0.5 * x) + 0.5


def dot(a, b):
    return lax.dot_general(a, b, (((1,), (0,)), ((), ())), preferred_element_type=f32)


def dot_nt(a, b):
    return lax.dot_general(a, b, (((1,), (1,)), ((), ())), preferred_element_type=f32)


def dot_tn(a, b):
    return lax.dot_general(a, b, (((0,), (0,)), ((), ())), preferred_element_type=f32)


def split(values):
    high = values.astype(bf16)
    return jnp.concatenate([high, (values - high.astype(f32)).astype(bf16)], axis=-1)


def row_mean(parts, width):
    return dot(parts, jnp.full((parts.shape[-1], width), 1.0 / width, bf16))


def normalize(values, mean):
    centred = values - mean
    inverse = lax.rsqrt(row_mean(split(centred * centred), values.shape[-1]) + epsilon)
    return (centred * inverse, inverse)


def normalize_raw(raw):
    return normalize(raw.astype(f32), row_mean(raw, raw.shape[-1]))


def normalize_back(normed, inverse, upstream):
    width = upstream.shape[-1]
    first = row_mean(split(upstream), width)
    second = row_mean(split(upstream * normed), width)
    return inverse * (upstream - first - normed * second)


def gated(inputs, weight):
    pre = dot(inputs, weight)
    width = weight.shape[1] // 2
    return pre[:, :width], sigmoid(pre[:, width:])


def joined_grad(back, lin, sw):
    return jnp.concatenate([back * sw, back * lin * sw * (1.0 - sw)], axis=-1).astype(bf16)


def middle_kernel(middle, cotangent, gate_weight, output_weight, _, gate, middle_in, head_back, tri_up):
    n_i, n_j, width = middle.shape
    step = 16

    def body(at, _):
        rows = pl.ds(at * step, step)
        normed, _ = normalize_raw(middle[rows].reshape(step * n_j, width))
        inputs = normed.astype(bf16)
        opened = sigmoid(dot(inputs, gate_weight[...]))
        back = (cotangent[rows].astype(f32).reshape(step * n_j, width) * opened).astype(bf16)
        gate[rows] = opened.reshape(step, n_j, width)
        middle_in[rows] = inputs.reshape(step, n_j, width)
        head_back[rows] = back.reshape(step, n_j, width)
        up = dot_nt(back, output_weight[...])
        tri_up[rows] = (up - row_mean(split(up), width)).reshape(step, n_j, width)
        return 0

    lax.fori_loop(0, n_i // step, body, 0, unroll=True)


def right_kernel(n_rows, n_blk, k_left, *refs):
    raw, (weight, _, _, act_out, in_out, *flip_out) = refs[:n_rows], refs[n_rows:]
    n_j, k_right, width = raw[0].shape
    n_k = k_left * n_blk
    unit = math.gcd(k_left, k_right)
    step = n_j
    for s in range(n_rows):

        def body(at, _, s=s):
            rows = pl.ds(at * step, step)
            normed, _ = normalize_raw(raw[s][rows].reshape(step * k_right, width))
            inputs = normed.astype(bf16)
            in_out[s, rows] = inputs.reshape(step, k_right, width)
            lin, sw = gated(inputs, weight[...])
            act = (sw * lin).astype(bf16).astype(f32).reshape(step, k_right, width)
            for part in range(k_right // unit):
                at_k = place(n_blk, k_left, k_right, s, part)
                for j in range(step):
                    start = pl.multiple_of((at * step + j) * n_k + at_k, unit)
                    act_out[pl.ds(start, unit), :] = act[j, part * unit : (part + 1) * unit]
            return 0

        lax.fori_loop(0, n_j // step, body, 0, unroll=True)

    for s in range(n_blk):

        def flip(k, _, s=s):
            flip_out[s][k] = act_out[pl.ds(s * k_left + k, n_j, stride=n_k), :]
            return 0

        lax.fori_loop(0, k_left, flip, 0, unroll=True)


def place(n_blk, k_left, k_right, piece, part):
    unit = math.gcd(k_left, k_right)
    vertex = lax.bitwise_xor(lax.axis_index("rows"), piece) * k_right + part * unit
    block = vertex // k_left
    at = lax.bitwise_xor(lax.axis_index("blk"), block) * k_left + vertex - block * k_left
    return pl.multiple_of(at, unit)


def project_left(raws, weight, act_out, in_out):
    n_i, k_left, width = raws[0].shape
    step = 32

    def body(at, _):
        rows = pl.ds(at * step, step)
        raw = raws[0][rows]
        if len(raws) > 1:
            place = jnp.full(raw.shape, lax.axis_index("blk"), jnp.int32)
            inner = jnp.logical_or(place == 1, place == 2)
            raw = jnp.where(inner, raws[1][rows].astype(f32), raw.astype(f32)).astype(bf16)
        normed, _ = normalize_raw(raw.reshape(step * k_left, width))
        inputs = normed.astype(bf16)
        in_out[rows] = inputs.reshape(step, k_left, width)
        lin, sw = gated(inputs, weight[...])
        act_out[rows] = (sw * lin).astype(bf16).astype(f32).reshape(step, k_left, width)
        return 0

    lax.fori_loop(0, n_i // step, body, 0, unroll=True)


def add_vertices(rows, act, flip):
    total = act[rows, 0:1, :] * flip[0][None]
    for k in range(1, act.shape[1]):
        total = total + act[rows, k : k + 1, :] * flip[k][None]
    return total


def own_kernel(raw, weight, _, act_out, in_out):
    project_left([raw], weight, act_out, in_out)


def own_sum_kernel(act, flip, total):
    step = 8

    def body(at, _):
        rows = pl.ds(at * step, step)
        total[rows] = add_vertices(rows, act, flip)
        return 0

    lax.fori_loop(0, total.shape[0] // step, body, 0, unroll=2)


def left_kernel(raw, weight, flip, total_in, act_out, in_out, total_out):
    n_i, n_j, width = total_out.shape
    step = 8
    project_left([raw], weight, act_out, in_out)

    def body(at, _):
        rows = pl.ds(at * step, step)
        total_out[rows] = total_in[rows] + add_vertices(rows, act_out, flip)
        return 0

    lax.fori_loop(0, n_i // step, body, 0, unroll=2)


def triangle_kernel(n_raw, *refs):
    raw, (left_w, flip, tri_up, *refs) = refs[:n_raw], refs[n_raw:]
    total_in, act_out, in_out, tri_in, tri_back = refs
    n_i, n_j, width = tri_in.shape
    step = 8
    project_left(raw, left_w, act_out, in_out)

    def triangle_rows(at, _):
        rows = pl.ds(at * step, step)
        total = total_in[rows] + add_vertices(rows, act_out, flip)
        flat = step * n_j
        total = total.reshape(flat, width)
        normed, inverse = normalize(total, row_mean(split(total), width))
        tri_in[rows] = normed.astype(bf16).reshape(step, n_j, width)
        up = tri_up[rows].reshape(flat, width)
        second = row_mean(split(up * normed), width)
        back = inverse * (up - normed * second)
        tri_back[rows] = back.astype(bf16).astype(f32).reshape(step, n_j, width)
        return 0

    lax.fori_loop(0, n_i // step, triangle_rows, 0, unroll=True)


def heads_kernel(tri_in, out_w, gate, middle_in, head_back, cotangent, _, *refs):
    update, pre_back, gate_part, output_part = refs
    n_i, n_j, width = update.shape
    step = 16
    gate_part[...] = jnp.zeros_like(gate_part)
    output_part[...] = jnp.zeros_like(output_part)

    def body(at, _):
        rows = pl.ds(at * step, step)
        flat = step * n_j
        inputs = tri_in[rows].reshape(flat, width)
        head = dot(inputs, out_w[...])
        opened = gate[rows].reshape(flat, width)
        update[rows] = (opened * head).astype(bf16).reshape(step, n_j, width)
        upstream = cotangent[rows].astype(f32).reshape(flat, width)
        pre = (upstream * head * opened * (1.0 - opened)).astype(bf16)
        pre_back[rows] = pre.reshape(step, n_j, width)
        gate_part[...] += dot_tn(middle_in[rows].reshape(flat, width), pre)
        output_part[...] += dot_tn(inputs, head_back[rows].reshape(flat, width))
        return 0

    lax.fori_loop(0, n_i // step, body, 0, unroll=True)


def vertex_step(n_k, unit):
    size = unit
    while size * 2 <= 64 and n_k % (size * 2) == 0:
        size *= 2
    return size


def left_back_kernel(first, n_blk, tri_back, right_act, *left_out):
    n_i, n_j, width = tri_back.shape
    k_left = left_out[0].shape[1]
    n_k = k_left * n_blk
    last = (first + len(left_out)) * k_left
    k_step = k_left * math.gcd(len(left_out), max(1, 64 // k_left))
    few = max(1, 256 // k_step)
    for k0 in range(first * k_left, last, k_step):

        def rows_sum(at, _, k0=k0):
            rows = pl.ds(at * few, few)
            total = jnp.zeros((few, k_step, width), f32)
            for j in range(n_j):
                start = j * n_k + k0
                total = total + tri_back[rows, j : j + 1, :] * right_act[start : start + k_step, :][None]
            total = total.astype(bf16)
            for s in range(k_step // k_left):
                left_out[k0 // k_left - first + s][rows] = total[:, s * k_left : (s + 1) * k_left]
            return 0

        lax.fori_loop(0, n_i // few, rows_sum, 0, unroll=2)


def right_back_kernel(n_rows, n_blk, tri_back, *refs):
    left_act, refs = refs[:n_blk], refs[n_blk + 1 :]
    keep, send, right_sum = refs
    n_i, n_j, width = tri_back.shape
    k_left = left_act[0].shape[1]
    n_k = k_left * n_blk
    k_right = keep.shape[2]
    unit = math.gcd(k_left, k_right)
    few = 4
    k_step = vertex_step(n_k, k_left)
    for k0 in range(0, n_k, k_step):
        blocks = range(k0 // k_left, (k0 + k_step) // k_left)
        for first in range(0, n_j, few):

            def add(i, totals, first=first, blocks=blocks):
                acts = [left_act[s][i] for s in blocks]
                added = []
                for at in range(few):
                    row = tri_back[i, first + at : first + at + 1, :]
                    added += [total + row * act for total, act in zip(totals[at * len(acts) :], acts)]
                return tuple(added)

            zeros = (jnp.zeros((k_left, width), f32),) * (few * len(blocks))
            totals = lax.fori_loop(0, n_i, add, zeros, unroll=16)
            for at in range(few):
                for s, total in zip(blocks, totals[at * len(blocks) :]):
                    right_sum[first + at, s * k_left : (s + 1) * k_left, :] = total.astype(bf16)
    for s in range(n_rows):
        for part in range(k_right // unit):
            out = send if s % 2 else keep
            out[s // 2, :, part * unit : (part + 1) * unit, :] = right_sum[
                :, pl.ds(place(n_blk, k_left, k_right, s, part), unit), :
            ]


def weights_kernel(n_rows, n_blk, right_in, left_w, right_w, gate_part, output_part, *refs):
    left_in, refs = refs[:n_blk], refs[n_blk:]
    left_out, refs = refs[:n_blk], refs[n_blk:]
    keep, send, keep_out, send_out, total = refs
    right_out = [(send if s % 2 else keep).at[s // 2] for s in range(n_rows)]
    right_ins = [right_in.at[s] for s in range(n_rows)]
    width = gate_part.shape[0]
    total[:, 4 * width : 5 * width] = gate_part[...]
    total[:, 5 * width :] = output_part[...]
    for inputs_refs, weight, backs, first in (
        (left_in, left_w, left_out, 0),
        (right_ins, right_w, right_out, 2 * width),
    ):
        columns = slice(first, first + 2 * width)
        total[:, columns] = jnp.zeros((width, 2 * width), f32)
        n, k, _ = inputs_refs[0].shape
        step = 32
        flat = step * k
        for inputs_ref, back_ref in zip(inputs_refs, backs):

            def body(at, _, inputs_ref=inputs_ref, back_ref=back_ref, weight=weight, columns=columns, flat=flat):
                rows = pl.ds(at * step, step)
                inputs = inputs_ref[rows].reshape(flat, width)
                lin, sw = gated(inputs, weight[...])
                back = back_ref[rows].reshape(flat, width).astype(f32)
                total[:, columns] += dot_tn(inputs, joined_grad(back, lin, sw))
                return 0

            lax.fori_loop(0, n // step, body, 0, unroll=True)
    size = width // n_rows
    for s in range(n_rows):
        start = pl.multiple_of(lax.bitwise_xor(lax.axis_index("rows"), s) * size, size)
        piece = total[pl.ds(start, size), :]
        if s % 2:
            send_out[s // 2] = piece.astype(bf16)
        else:
            keep_out[s // 2] = piece


def grad_middle_kernel(middle, pre_back, gate_weight, _, grad_middle, mark):
    mark[...] = jnp.zeros_like(mark)
    n_i, n_j, width = middle.shape
    step = 16

    def body(at, _):
        rows = pl.ds(at * step, step)
        flat = step * n_j
        normed, inverse = normalize_raw(middle[rows].reshape(flat, width))
        up = dot_nt(pre_back[rows].reshape(flat, width), gate_weight[...])
        grad_middle[rows] = normalize_back(normed, inverse, up).astype(bf16).reshape(step, n_j, width)
        return 0

    lax.fori_loop(0, n_i // step, body, 0, unroll=True)


def side_kernel(raw, weight, *refs):
    backs, (grad, mark) = refs[:-2], refs[-2:]
    mark[...] = jnp.zeros_like(mark)
    n, k, width = raw.shape
    step = 32
    flat = step * k

    def body(at, _):
        rows = pl.ds(at * step, step)
        normed, inverse = normalize_raw(raw[rows].reshape(flat, width))
        lin, sw = gated(normed.astype(bf16), weight[...])
        back = backs[0][rows].astype(f32)
        for other in backs[1:]:
            back = back + other[rows].astype(f32)
        up = dot_nt(joined_grad(back.reshape(flat, width), lin, sw), weight[...])
        grad[rows] = normalize_back(normed, inverse, up).astype(bf16).reshape(step, k, width)
        return 0

    lax.fori_loop(0, n // step, body, 0, unroll=True)


def exchange(x, axis, n, bit):
    return lax.ppermute(x, axis, [(a, a ^ bit) for a in range(n)])


def halve_kernel(keep, came, *refs):
    kept, send = refs[-2:]
    for at in range(keep.shape[0]):
        total = keep[at].astype(f32) + came[at].astype(f32)
        if at % 2:
            send[at // 2] = total.astype(bf16)
        else:
            kept[at // 2] = total


def halving_sum(keep, send, axis, n, after):
    came = exchange(send, axis, n, 1)
    bit = 2
    while bit < n:
        half = (keep.shape[0] // 2,) + keep.shape[1:]
        keep, send = call(halve_kernel, "halve", [shape(half, f32), shape(half, bf16)], after=len(after))(
            keep, came, *after
        )
        came = exchange(send, axis, n, bit)
        bit *= 2
    return keep, came, send


def forward_kernel(source, *refs):
    refs[-1][...] = source[...]


def forwarded(block, after):
    (copy,) = call(forward_kernel, "forward", [shape(block.shape, block.dtype)], after=len(after))(block, *after)
    return copy


def outer_block(across, after):
    return exchange(forwarded(across, after), "blk", 4, 1)


def inner_block(block, after):
    return lax.ppermute(forwarded(block, after), "blk", [(0, 0), (1, 2), (2, 1), (3, 3)])


def order_kernel(*refs):
    refs[-1][...] = jnp.zeros_like(refs[-1])


def behind(*arrays, cost=2 * 10**10):
    (mark,) = call(order_kernel, "order", [MARK], after=len(arrays), cost=cost)(*arrays)
    return mark


def combine_kernel(n, *refs):
    totals = [ref[0].astype(f32) for ref in refs[:n]]
    while len(totals) > 1:
        pairs = [a + b for a, b in zip(totals[::2], totals[1::2])]
        totals = pairs + totals[2 * len(pairs) :]
    refs[-1][0] = totals[0].astype(bf16)


def combine(pieces, after=()):
    (total,) = call(
        functools.partial(combine_kernel, len(pieces)),
        "combine",
        [shape((1,) + pieces[0].shape[1:], bf16)],
        after=len(after),
    )(*pieces, *after)
    return total


def deltas_kernel(n_rows, *refs):
    pieces, outs = [ref.at[0] for ref in refs[:n_rows]], refs[n_rows + 1 :]
    size = pieces[0].shape[0]
    for s, piece in enumerate(pieces):
        start = pl.multiple_of(lax.bitwise_xor(lax.axis_index("rows"), s) * size, size)
        first = 0
        for out in outs:
            last = first + out.shape[1]
            out[pl.ds(start, size), :] = piece[:, first:last].astype(f32)
            first = last


def shape(dims, kind):
    return jax.ShapeDtypeStruct(tuple(dims), kind)


def call(kernel, name, outs, scratch=(), after=0, cost=1000):
    def run(*operands):
        spaces = [pltpu.VMEM] * (len(operands) - after) + [pl.ANY] * after
        held = sum(math.prod(x.shape) * 4 for x in scratch)
        return pl.pallas_call(
            kernel,
            in_specs=[pl.BlockSpec(memory_space=space) for space in spaces],
            out_specs=[pl.BlockSpec(memory_space=pltpu.VMEM)] * len(outs),
            out_shape=outs,
            scratch_shapes=list(scratch),
            compiler_params=pltpu.CompilerParams(vmem_limit_bytes=held + SCOPED),
            cost_estimate=pl.CostEstimate(flops=cost, bytes_accessed=1000, transcendentals=0),
            name=name,
        )(*operands)

    return run


def per_device(
    n_rows,
    n_blk,
    pair_left,
    pair_right,
    pair_middle,
    cotangent,
    left_weight,
    right_weight,
    gate_weight,
    output_weight,
):
    n_i, k_left, width = pair_left.shape
    n_j, k_right, _ = pair_right.shape
    n_k = k_left * n_blk
    right_raw = [pair_right] + [exchange(pair_right, "rows", n_rows, s) for s in range(1, n_rows)]
    middle_shape = (n_i, n_j, width)
    begun = behind(cost=10**9)
    gate, middle_in, head_back, tri_up = call(
        middle_kernel,
        "middle",
        [shape(middle_shape, f32), shape(middle_shape, bf16), shape(middle_shape, bf16), shape(middle_shape, f32)],
        after=1,
    )(pair_middle, cotangent, gate_weight, output_weight, begun)
    act_shape = shape(pair_left.shape, f32)
    in_shape = shape(pair_left.shape, bf16)
    own_act, own_in = call(own_kernel, "own", [act_shape, in_shape], after=1)(pair_left, left_weight, begun)
    right_act, right_in, *right_flip = call(
        functools.partial(right_kernel, n_rows, n_blk, k_left),
        "right",
        [shape((n_j * n_k, width), f32), shape((n_rows, n_j, k_right, width), bf16)]
        + [shape((k_left, n_j, width), f32)] * n_blk,
        after=2,
    )(*right_raw, right_weight, own_act, middle_in)
    left_raw = [[pair_left]] + [[exchange(pair_left, "blk", n_blk, s)] for s in range(1, 3 if n_blk == 4 else n_blk)]
    if n_blk == 4:
        left_raw.append([outer_block(left_raw[2][0], (right_in, middle_in))])
    total = call(own_sum_kernel, "own_sum", [shape(middle_shape, f32)])(own_act, right_flip[0])
    if n_blk == 4:
        left_raw[3].append(inner_block(pair_left, tuple(total)))
    left_act, left_in = [own_act], [own_in]
    for s in range(1, n_blk - 1):
        act, inputs, *total = call(
            left_kernel,
            "left",
            [act_shape, in_shape, shape(middle_shape, f32)],
        )(*left_raw[s], left_weight, right_flip[s], *total)
        left_act.append(act)
        left_in.append(inputs)
    act, inputs, tri_in, tri_back = call(
        functools.partial(triangle_kernel, len(left_raw[-1])),
        "triangle",
        [act_shape, in_shape, shape(middle_shape, bf16), shape(middle_shape, f32)],
    )(*left_raw[-1], left_weight, right_flip[-1], tri_up, *total)
    left_act.append(act)
    left_in.append(inputs)
    half = n_blk // 2
    left_out = []
    for first in (half, 0):
        some = call(
            functools.partial(left_back_kernel, first, n_blk),
            "left_back",
            [shape(pair_left.shape, bf16)] * half,
            after=0,
        )(tri_back, right_act)
        left_out = [*some, *left_out]
    left_back = [left_out[0]] + [exchange(left_out[s], "blk", n_blk, s) for s in range(1, n_blk)]
    right_stack = shape((n_rows // 2,) + pair_right.shape, bf16)
    keep, send = call(
        functools.partial(right_back_kernel, n_rows, n_blk),
        "right_back",
        [right_stack, right_stack],
        scratch=[pltpu.VMEM((n_j, n_k, width), bf16)],
        after=1,
    )(tri_back, *left_act, left_out[0])
    kept, came, sent = halving_sum(keep, send, "rows", n_rows, (behind(*left_back[1:], cost=LEFT_COST),))
    update, pre_back, gate_part, output_part = call(
        heads_kernel,
        "heads",
        [
            shape(middle_shape, bf16),
            shape(middle_shape, bf16),
            shape(gate_weight.shape, f32),
            shape(output_weight.shape, f32),
        ],
        after=1,
    )(tri_in, output_weight, gate, middle_in, head_back, cotangent, left_out[0])
    parts = (n_rows // 2, width // n_rows, 6 * width)
    keep, send = call(
        functools.partial(weights_kernel, n_rows, n_blk),
        "weights",
        [shape(parts, f32), shape(parts, bf16)],
        scratch=[pltpu.VMEM((width, 6 * width), f32)],
    )(right_in, left_weight, right_weight, gate_part, output_part, *left_in, *left_out, keep, send)
    grad_middle, done_middle = call(
        grad_middle_kernel, "grad_middle", [shape(middle_shape, bf16), MARK], after=1
    )(pair_middle, pre_back, gate_weight, send)
    keep, part, _ = halving_sum(keep, send, "rows", n_rows, (done_middle,))
    part = combine([keep, part], (behind(sent),))
    grad_left, done_left = call(side_kernel, "left_side", [shape(pair_left.shape, bf16), MARK])(
        pair_left, left_weight, *left_back
    )
    part = combine([part] + [exchange(part, "blk", n_blk, s) for s in range(1, n_blk)], (done_left,))
    pieces = [part] + [exchange(part, "rows", n_rows, s) for s in range(1, n_rows)]
    grad_right, done_right = call(side_kernel, "right_side", [shape(pair_right.shape, bf16), MARK])(
        pair_right, right_weight, kept.reshape(pair_right.shape), came.reshape(pair_right.shape)
    )
    deltas = call(
        functools.partial(deltas_kernel, n_rows),
        "deltas",
        [shape(x.shape, f32) for x in (left_weight, right_weight, gate_weight, output_weight)],
        after=1,
    )(*pieces, done_right)
    return (
        update,
        grad_left,
        grad_right,
        grad_middle,
        *deltas,
    )


def solution(mesh):
    sides = P(("rep", "rows"), "blk", None)
    right = P(("rep", "blk"), "rows", None)
    return jax.shard_map(
        functools.partial(per_device, mesh.shape["rows"], mesh.shape["blk"]),
        mesh=mesh,
        in_specs=(sides, right, sides, sides, P(), P(), P(), P()),
        out_specs=(sides, sides, right, sides) + (P("rep", None),) * 4,
        check_vma=False,
    )
```

```python
import functools
import math

import jax
import jax.numpy as jnp
from jax import lax
from jax.experimental import pallas as pl
from jax.experimental.pallas import tpu as pltpu
from jax.sharding import PartitionSpec as P

epsilon = 1e-05
f32 = jnp.float32
bf16 = jnp.bfloat16
SCOPED = 6 * 1024 * 1024
LEFT_COST = 2 * 10**8
MARK = jax.ShapeDtypeStruct((8, 128), jnp.float32)


def sigmoid(x):
    return 0.5 * jnp.tanh(0.5 * x) + 0.5


def dot(a, b):
    return lax.dot_general(a, b, (((1,), (0,)), ((), ())), preferred_element_type=f32)


def dot_nt(a, b):
    return lax.dot_general(a, b, (((1,), (1,)), ((), ())), preferred_element_type=f32)


def dot_tn(a, b):
    return lax.dot_general(a, b, (((0,), (0,)), ((), ())), preferred_element_type=f32)


def split(values):
    high = values.astype(bf16)
    return jnp.concatenate([high, (values - high.astype(f32)).astype(bf16)], axis=-1)


def row_mean(parts, width):
    return dot(parts, jnp.full((parts.shape[-1], width), 1.0 / width, bf16))


def normalize(values, mean):
    centred = values - mean
    inverse = lax.rsqrt(row_mean(split(centred * centred), values.shape[-1]) + epsilon)
    return (centred * inverse, inverse)


def normalize_raw(raw):
    return normalize(raw.astype(f32), row_mean(raw, raw.shape[-1]))


def normalize_back(normed, inverse, upstream):
    width = upstream.shape[-1]
    first = row_mean(split(upstream), width)
    second = row_mean(split(upstream * normed), width)
    return inverse * (upstream - first - normed * second)


def gated(inputs, weight):
    pre = dot(inputs, weight)
    width = weight.shape[1] // 2
    return pre[:, :width], sigmoid(pre[:, width:])


def joined_grad(back, lin, sw):
    return jnp.concatenate([back * sw, back * lin * sw * (1.0 - sw)], axis=-1).astype(bf16)


def middle_kernel(middle, cotangent, gate_weight, output_weight, _, gate, middle_in, head_back, tri_up):
    n_i, n_j, width = middle.shape
    step = 16

    def body(at, _):
        rows = pl.ds(at * step, step)
        normed, _ = normalize_raw(middle[rows].reshape(step * n_j, width))
        inputs = normed.astype(bf16)
        opened = sigmoid(dot(inputs, gate_weight[...]))
        back = (cotangent[rows].astype(f32).reshape(step * n_j, width) * opened).astype(bf16)
        gate[rows] = opened.reshape(step, n_j, width)
        middle_in[rows] = inputs.reshape(step, n_j, width)
        head_back[rows] = back.reshape(step, n_j, width)
        up = dot_nt(back, output_weight[...])
        tri_up[rows] = (up - row_mean(split(up), width)).reshape(step, n_j, width)
        return 0

    lax.fori_loop(0, n_i // step, body, 0, unroll=True)


def right_kernel(n_rows, n_blk, k_left, *refs):
    raw, (weight, _, _, act_out, in_out, *flip_out) = refs[:n_rows], refs[n_rows:]
    n_j, k_right, width = raw[0].shape
    n_k = k_left * n_blk
    unit = math.gcd(k_left, k_right)
    step = n_j
    for s in range(n_rows):

        def body(at, _, s=s):
            rows = pl.ds(at * step, step)
            normed, _ = normalize_raw(raw[s][rows].reshape(step * k_right, width))
            inputs = normed.astype(bf16)
            in_out[s, rows] = inputs.reshape(step, k_right, width)
            lin, sw = gated(inputs, weight[...])
            act = (sw * lin).astype(bf16).astype(f32).reshape(step, k_right, width)
            for part in range(k_right // unit):
                at_k = place(n_blk, k_left, k_right, s, part)
                for j in range(step):
                    start = pl.multiple_of((at * step + j) * n_k + at_k, unit)
                    act_out[pl.ds(start, unit), :] = act[j, part * unit : (part + 1) * unit]
            return 0

        lax.fori_loop(0, n_j // step, body, 0, unroll=True)

    for s in range(n_blk):

        def flip(k, _, s=s):
            flip_out[s][k] = act_out[pl.ds(s * k_left + k, n_j, stride=n_k), :]
            return 0

        lax.fori_loop(0, k_left, flip, 0, unroll=True)


def place(n_blk, k_left, k_right, piece, part):
    unit = math.gcd(k_left, k_right)
    vertex = lax.bitwise_xor(lax.axis_index("rows"), piece) * k_right + part * unit
    block = vertex // k_left
    at = lax.bitwise_xor(lax.axis_index("blk"), block) * k_left + vertex - block * k_left
    return pl.multiple_of(at, unit)


def project_left(raws, weight, act_out, in_out):
    n_i, k_left, width = raws[0].shape
    step = 32

    def body(at, _):
        rows = pl.ds(at * step, step)
        raw = raws[0][rows]
        if len(raws) > 1:
            place = jnp.full(raw.shape, lax.axis_index("blk"), jnp.int32)
            inner = jnp.logical_or(place == 1, place == 2)
            raw = jnp.where(inner, raw.astype(f32), raws[1][rows].astype(f32)).astype(bf16)
        normed, _ = normalize_raw(raw.reshape(step * k_left, width))
        inputs = normed.astype(bf16)
        in_out[rows] = inputs.reshape(step, k_left, width)
        lin, sw = gated(inputs, weight[...])
        act_out[rows] = (sw * lin).astype(bf16).astype(f32).reshape(step, k_left, width)
        return 0

    lax.fori_loop(0, n_i // step, body, 0, unroll=True)


def add_vertices(rows, act, flip):
    total = act[rows, 0:1, :] * flip[0][None]
    for k in range(1, act.shape[1]):
        total = total + act[rows, k : k + 1, :] * flip[k][None]
    return total


def own_kernel(raw, weight, _, act_out, in_out):
    project_left([raw], weight, act_out, in_out)


def own_sum_kernel(act, flip, _, total):
    step = 8

    def body(at, _):
        rows = pl.ds(at * step, step)
        total[rows] = add_vertices(rows, act, flip)
        return 0

    lax.fori_loop(0, total.shape[0] // step, body, 0, unroll=2)


def left_kernel(raw, weight, flip, total_in, act_out, in_out, total_out):
    n_i, n_j, width = total_out.shape
    step = 8
    project_left([raw], weight, act_out, in_out)

    def body(at, _):
        rows = pl.ds(at * step, step)
        total_out[rows] = total_in[rows] + add_vertices(rows, act_out, flip)
        return 0

    lax.fori_loop(0, n_i // step, body, 0, unroll=2)


def triangle_kernel(n_raw, *refs):
    raw, (left_w, flip, tri_up, *refs) = refs[:n_raw], refs[n_raw:]
    total_in, act_out, in_out, tri_in, tri_back = refs
    n_i, n_j, width = tri_in.shape
    step = 8
    project_left(raw, left_w, act_out, in_out)

    def triangle_rows(at, _):
        rows = pl.ds(at * step, step)
        total = total_in[rows] + add_vertices(rows, act_out, flip)
        flat = step * n_j
        total = total.reshape(flat, width)
        normed, inverse = normalize(total, row_mean(split(total), width))
        tri_in[rows] = normed.astype(bf16).reshape(step, n_j, width)
        up = tri_up[rows].reshape(flat, width)
        second = row_mean(split(up * normed), width)
        back = inverse * (up - normed * second)
        tri_back[rows] = back.astype(bf16).astype(f32).reshape(step, n_j, width)
        return 0

    lax.fori_loop(0, n_i // step, triangle_rows, 0, unroll=True)


def heads_kernel(tri_in, out_w, gate, middle_in, head_back, cotangent, _, *refs):
    update, pre_back, gate_part, output_part = refs
    n_i, n_j, width = update.shape
    step = 16
    gate_part[...] = jnp.zeros_like(gate_part)
    output_part[...] = jnp.zeros_like(output_part)

    def body(at, _):
        rows = pl.ds(at * step, step)
        flat = step * n_j
        inputs = tri_in[rows].reshape(flat, width)
        head = dot(inputs, out_w[...])
        opened = gate[rows].reshape(flat, width)
        update[rows] = (opened * head).astype(bf16).reshape(step, n_j, width)
        upstream = cotangent[rows].astype(f32).reshape(flat, width)
        pre = (upstream * head * opened * (1.0 - opened)).astype(bf16)
        pre_back[rows] = pre.reshape(step, n_j, width)
        gate_part[...] += dot_tn(middle_in[rows].reshape(flat, width), pre)
        output_part[...] += dot_tn(inputs, head_back[rows].reshape(flat, width))
        return 0

    lax.fori_loop(0, n_i // step, body, 0, unroll=True)


def vertex_step(n_k, unit):
    size = unit
    while size * 2 <= 64 and n_k % (size * 2) == 0:
        size *= 2
    return size


def left_back_kernel(first, n_blk, tri_back, right_act, *left_out):
    n_i, n_j, width = tri_back.shape
    k_left = left_out[0].shape[1]
    n_k = k_left * n_blk
    last = (first + len(left_out)) * k_left
    k_step = k_left * math.gcd(len(left_out), max(1, 64 // k_left))
    few = max(1, 256 // k_step)
    for k0 in range(first * k_left, last, k_step):

        def rows_sum(at, _, k0=k0):
            rows = pl.ds(at * few, few)
            total = jnp.zeros((few, k_step, width), f32)
            for j in range(n_j):
                start = j * n_k + k0
                total = total + tri_back[rows, j : j + 1, :] * right_act[start : start + k_step, :][None]
            total = total.astype(bf16)
            for s in range(k_step // k_left):
                left_out[k0 // k_left - first + s][rows] = total[:, s * k_left : (s + 1) * k_left]
            return 0

        lax.fori_loop(0, n_i // few, rows_sum, 0, unroll=2)


def right_back_kernel(n_rows, n_blk, tri_back, *refs):
    left_act, refs = refs[:n_blk], refs[n_blk + 1 :]
    keep, send, right_sum = refs
    n_i, n_j, width = tri_back.shape
    k_left = left_act[0].shape[1]
    n_k = k_left * n_blk
    k_right = keep.shape[2]
    unit = math.gcd(k_left, k_right)
    few = 4
    k_step = vertex_step(n_k, k_left)
    for k0 in range(0, n_k, k_step):
        blocks = range(k0 // k_left, (k0 + k_step) // k_left)
        for first in range(0, n_j, few):

            def add(i, totals, first=first, blocks=blocks):
                acts = [left_act[s][i] for s in blocks]
                added = []
                for at in range(few):
                    row = tri_back[i, first + at : first + at + 1, :]
                    added += [total + row * act for total, act in zip(totals[at * len(acts) :], acts)]
                return tuple(added)

            zeros = (jnp.zeros((k_left, width), f32),) * (few * len(blocks))
            totals = lax.fori_loop(0, n_i, add, zeros, unroll=16)
            for at in range(few):
                for s, total in zip(blocks, totals[at * len(blocks) :]):
                    right_sum[first + at, s * k_left : (s + 1) * k_left, :] = total.astype(bf16)
    for s in range(n_rows):
        for part in range(k_right // unit):
            out = send if s % 2 else keep
            out[s // 2, :, part * unit : (part + 1) * unit, :] = right_sum[
                :, pl.ds(place(n_blk, k_left, k_right, s, part), unit), :
            ]


def weights_kernel(n_rows, n_blk, right_in, left_w, right_w, gate_part, output_part, *refs):
    left_in, refs = refs[:n_blk], refs[n_blk:]
    left_out, refs = refs[:n_blk], refs[n_blk:]
    keep, send, keep_out, send_out, total = refs
    right_out = [(send if s % 2 else keep).at[s // 2] for s in range(n_rows)]
    right_ins = [right_in.at[s] for s in range(n_rows)]
    width = gate_part.shape[0]
    total[:, 4 * width : 5 * width] = gate_part[...]
    total[:, 5 * width :] = output_part[...]
    for inputs_refs, weight, backs, first in (
        (left_in, left_w, left_out, 0),
        (right_ins, right_w, right_out, 2 * width),
    ):
        columns = slice(first, first + 2 * width)
        total[:, columns] = jnp.zeros((width, 2 * width), f32)
        n, k, _ = inputs_refs[0].shape
        step = 32
        flat = step * k
        for inputs_ref, back_ref in zip(inputs_refs, backs):

            def body(at, _, inputs_ref=inputs_ref, back_ref=back_ref, weight=weight, columns=columns, flat=flat):
                rows = pl.ds(at * step, step)
                inputs = inputs_ref[rows].reshape(flat, width)
                lin, sw = gated(inputs, weight[...])
                back = back_ref[rows].reshape(flat, width).astype(f32)
                total[:, columns] += dot_tn(inputs, joined_grad(back, lin, sw))
                return 0

            lax.fori_loop(0, n // step, body, 0, unroll=True)
    size = width // n_rows
    for s in range(n_rows):
        start = pl.multiple_of(lax.bitwise_xor(lax.axis_index("rows"), s) * size, size)
        piece = total[pl.ds(start, size), :]
        if s % 2:
            send_out[s // 2] = piece.astype(bf16)
        else:
            keep_out[s // 2] = piece


def grad_middle_kernel(middle, pre_back, gate_weight, _, grad_middle, mark):
    mark[...] = jnp.zeros_like(mark)
    n_i, n_j, width = middle.shape
    step = 16

    def body(at, _):
        rows = pl.ds(at * step, step)
        flat = step * n_j
        normed, inverse = normalize_raw(middle[rows].reshape(flat, width))
        up = dot_nt(pre_back[rows].reshape(flat, width), gate_weight[...])
        grad_middle[rows] = normalize_back(normed, inverse, up).astype(bf16).reshape(step, n_j, width)
        return 0

    lax.fori_loop(0, n_i // step, body, 0, unroll=True)


def side_kernel(raw, weight, *refs):
    backs, (grad, mark) = refs[:-2], refs[-2:]
    mark[...] = jnp.zeros_like(mark)
    n, k, width = raw.shape
    step = 32
    flat = step * k

    def body(at, _):
        rows = pl.ds(at * step, step)
        normed, inverse = normalize_raw(raw[rows].reshape(flat, width))
        lin, sw = gated(normed.astype(bf16), weight[...])
        back = backs[0][rows].astype(f32)
        for other in backs[1:]:
            back = back + other[rows].astype(f32)
        up = dot_nt(joined_grad(back.reshape(flat, width), lin, sw), weight[...])
        grad[rows] = normalize_back(normed, inverse, up).astype(bf16).reshape(step, k, width)
        return 0

    lax.fori_loop(0, n // step, body, 0, unroll=True)


def exchange(x, axis, n, bit):
    return lax.ppermute(x, axis, [(a, a ^ bit) for a in range(n)])


def halve_kernel(keep, came, *refs):
    kept, send = refs[-2:]
    for at in range(keep.shape[0]):
        total = keep[at].astype(f32) + came[at].astype(f32)
        if at % 2:
            send[at // 2] = total.astype(bf16)
        else:
            kept[at // 2] = total


def halving_sum(keep, send, axis, n, after):
    came = exchange(send, axis, n, 1)
    bit = 2
    while bit < n:
        half = (keep.shape[0] // 2,) + keep.shape[1:]
        keep, send = call(halve_kernel, "halve", [shape(half, f32), shape(half, bf16)], after=len(after))(
            keep, came, *after
        )
        came = exchange(send, axis, n, bit)
        bit *= 2
    return keep, came, send


def forward_kernel(source, *refs):
    refs[-1][...] = source[...]


def forwarded(block, after):
    (copy,) = call(forward_kernel, "forward", [shape(block.shape, block.dtype)], after=len(after))(block, *after)
    return copy


def inner_block(block, after):
    return lax.ppermute(forwarded(block, after), "blk", [(0, 0), (1, 2), (2, 1), (3, 3)])


def order_kernel(*refs):
    refs[-1][...] = jnp.zeros_like(refs[-1])


def behind(*arrays, cost=2 * 10**10):
    (mark,) = call(order_kernel, "order", [MARK], after=len(arrays), cost=cost)(*arrays)
    return mark


def combine_kernel(n, *refs):
    totals = [ref[0].astype(f32) for ref in refs[:n]]
    while len(totals) > 1:
        pairs = [a + b for a, b in zip(totals[::2], totals[1::2])]
        totals = pairs + totals[2 * len(pairs) :]
    refs[-1][0] = totals[0].astype(bf16)


def combine(pieces, after=()):
    (total,) = call(
        functools.partial(combine_kernel, len(pieces)),
        "combine",
        [shape((1,) + pieces[0].shape[1:], bf16)],
        after=len(after),
    )(*pieces, *after)
    return total


def deltas_kernel(n_rows, *refs):
    pieces, outs = [ref.at[0] for ref in refs[:n_rows]], refs[n_rows + 1 :]
    size = pieces[0].shape[0]
    for s, piece in enumerate(pieces):
        start = pl.multiple_of(lax.bitwise_xor(lax.axis_index("rows"), s) * size, size)
        first = 0
        for out in outs:
            last = first + out.shape[1]
            out[pl.ds(start, size), :] = piece[:, first:last].astype(f32)
            first = last


def shape(dims, kind):
    return jax.ShapeDtypeStruct(tuple(dims), kind)


def call(kernel, name, outs, scratch=(), after=0, cost=1000):
    def run(*operands):
        spaces = [pltpu.VMEM] * (len(operands) - after) + [pl.ANY] * after
        held = sum(math.prod(x.shape) * 4 for x in scratch)
        return pl.pallas_call(
            kernel,
            in_specs=[pl.BlockSpec(memory_space=space) for space in spaces],
            out_specs=[pl.BlockSpec(memory_space=pltpu.VMEM)] * len(outs),
            out_shape=outs,
            scratch_shapes=list(scratch),
            compiler_params=pltpu.CompilerParams(vmem_limit_bytes=held + SCOPED),
            cost_estimate=pl.CostEstimate(flops=cost, bytes_accessed=1000, transcendentals=0),
            name=name,
        )(*operands)

    return run


def per_device(
    n_rows,
    n_blk,
    pair_left,
    pair_right,
    pair_middle,
    cotangent,
    left_weight,
    right_weight,
    gate_weight,
    output_weight,
):
    n_i, k_left, width = pair_left.shape
    n_j, k_right, _ = pair_right.shape
    n_k = k_left * n_blk
    right_raw = [pair_right] + [exchange(pair_right, "rows", n_rows, s) for s in range(1, n_rows)]
    middle_shape = (n_i, n_j, width)
    begun = behind(cost=10**9)
    gate, middle_in, head_back, tri_up = call(
        middle_kernel,
        "middle",
        [shape(middle_shape, f32), shape(middle_shape, bf16), shape(middle_shape, bf16), shape(middle_shape, f32)],
        after=1,
    )(pair_middle, cotangent, gate_weight, output_weight, begun)
    act_shape = shape(pair_left.shape, f32)
    in_shape = shape(pair_left.shape, bf16)
    own_act, own_in = call(own_kernel, "own", [act_shape, in_shape], after=1)(pair_left, left_weight, begun)
    right_act, right_in, *right_flip = call(
        functools.partial(right_kernel, n_rows, n_blk, k_left),
        "right",
        [shape((n_j * n_k, width), f32), shape((n_rows, n_j, k_right, width), bf16)]
        + [shape((k_left, n_j, width), f32)] * n_blk,
        after=2,
    )(*right_raw, right_weight, own_act, middle_in)
    left_raw = [[pair_left]] + [[exchange(pair_left, "blk", n_blk, s)] for s in range(1, 3 if n_blk == 4 else n_blk)]
    passed = right_in
    if n_blk == 4:
        passed = forwarded(left_raw[2][0], (right_in, middle_in))
        left_raw.append([exchange(passed, "blk", 4, 1)])
    total = call(own_sum_kernel, "own_sum", [shape(middle_shape, f32)], after=1)(own_act, right_flip[0], passed)
    if n_blk == 4:
        left_raw[3].insert(0, inner_block(pair_left, tuple(total)))
    left_act, left_in = [own_act], [own_in]
    for s in range(1, n_blk - 1):
        act, inputs, *total = call(
            left_kernel,
            "left",
            [act_shape, in_shape, shape(middle_shape, f32)],
        )(*left_raw[s], left_weight, right_flip[s], *total)
        left_act.append(act)
        left_in.append(inputs)
    act, inputs, tri_in, tri_back = call(
        functools.partial(triangle_kernel, len(left_raw[-1])),
        "triangle",
        [act_shape, in_shape, shape(middle_shape, bf16), shape(middle_shape, f32)],
    )(*left_raw[-1], left_weight, right_flip[-1], tri_up, *total)
    left_act.append(act)
    left_in.append(inputs)
    half = n_blk // 2
    left_out = []
    for first in (half, 0):
        some = call(
            functools.partial(left_back_kernel, first, n_blk),
            "left_back",
            [shape(pair_left.shape, bf16)] * half,
            after=0,
        )(tri_back, right_act)
        left_out = [*some, *left_out]
    left_back = [left_out[0]] + [exchange(left_out[s], "blk", n_blk, s) for s in range(1, n_blk)]
    right_stack = shape((n_rows // 2,) + pair_right.shape, bf16)
    keep, send = call(
        functools.partial(right_back_kernel, n_rows, n_blk),
        "right_back",
        [right_stack, right_stack],
        scratch=[pltpu.VMEM((n_j, n_k, width), bf16)],
        after=1,
    )(tri_back, *left_act, left_out[0])
    kept, came, sent = halving_sum(keep, send, "rows", n_rows, (behind(*left_back[1:], cost=LEFT_COST),))
    update, pre_back, gate_part, output_part = call(
        heads_kernel,
        "heads",
        [
            shape(middle_shape, bf16),
            shape(middle_shape, bf16),
            shape(gate_weight.shape, f32),
            shape(output_weight.shape, f32),
        ],
        after=1,
    )(tri_in, output_weight, gate, middle_in, head_back, cotangent, left_out[0])
    parts = (n_rows // 2, width // n_rows, 6 * width)
    keep, send = call(
        functools.partial(weights_kernel, n_rows, n_blk),
        "weights",
        [shape(parts, f32), shape(parts, bf16)],
        scratch=[pltpu.VMEM((width, 6 * width), f32)],
    )(right_in, left_weight, right_weight, gate_part, output_part, *left_in, *left_out, keep, send)
    grad_middle, done_middle = call(
        grad_middle_kernel, "grad_middle", [shape(middle_shape, bf16), MARK], after=1
    )(pair_middle, pre_back, gate_weight, send)
    keep, part, _ = halving_sum(keep, send, "rows", n_rows, (done_middle,))
    part = combine([keep, part], (behind(sent),))
    grad_left, done_left = call(side_kernel, "left_side", [shape(pair_left.shape, bf16), MARK])(
        pair_left, left_weight, *left_back
    )
    part = combine([part] + [exchange(part, "blk", n_blk, s) for s in range(1, n_blk)], (done_left,))
    pieces = [part] + [exchange(part, "rows", n_rows, s) for s in range(1, n_rows)]
    grad_right, done_right = call(side_kernel, "right_side", [shape(pair_right.shape, bf16), MARK])(
        pair_right, right_weight, kept.reshape(pair_right.shape), came.reshape(pair_right.shape)
    )
    deltas = call(
        functools.partial(deltas_kernel, n_rows),
        "deltas",
        [shape(x.shape, f32) for x in (left_weight, right_weight, gate_weight, output_weight)],
        after=1,
    )(*pieces, done_right)
    return (
        update,
        grad_left,
        grad_right,
        grad_middle,
        *deltas,
    )


def solution(mesh):
    sides = P(("rep", "rows"), "blk", None)
    right = P(("rep", "blk"), "rows", None)
    return jax.shard_map(
        functools.partial(per_device, mesh.shape["rows"], mesh.shape["blk"]),
        mesh=mesh,
        in_specs=(sides, right, sides, sides, P(), P(), P(), P()),
        out_specs=(sides, sides, right, sides) + (P("rep", None),) * 4,
        check_vma=False,
    )
```
